32 devices in a mesh: tm: 2 (over x), sy: 4 (over z), sx: 4 (over y, core).
Axes of the slice: x: 2, y: 2, z: 4, core: 2. Of those that a mesh axis runs over, the one named last changes fastest.
Arguments:
- latent_init: float32 [64, 96, 320], P('sy', 'sx'), may hold values from -80 to 80
- step_noise: bfloat16 [8, 64, 96, 320], P('tm', 'sy', 'sx'), may hold values from -6 to 6
- coef_state: float32 [8], P('tm'), may hold values from -0.06 to -0.01
- coef_drift: float32 [8], P('tm'), may hold values from -0.1 to 0.1
- coef_noise: float32 [8], P('tm'), may hold values from 0.05 to 0.2
- step_index: int32 [8], P('tm'), may hold values from 0 to 999
- time_table: float32 [1000, 320], replicated, may hold values from -1.5 to 1.5
- norm_gain: float32 [320], replicated, may hold values from 0.25 to 1.75
- conv_weight: bfloat16 [3, 3, 320, 320], replicated, may hold values from -0.109375 to 0.109375
- reward_grad: float32 [64, 96, 320], P('sy', 'sx'), may hold values from -0.18 to 0.18
Outputs:
- trajectory: float32 [8, 64, 96, 320], P('tm', 'sy', 'sx')
- grad_weight: float32 [3, 3, 320, 320], P(None, None, None, 'tm')
The draws below stay inside these ranges and needn't reach their ends.
All inputs are finite; a program needn't handle non-finite values.
Results may differ from the reference program's by a relative error of at most 0.0009.
The reference program's roundings to bfloat16 on the way (of `activation` and `up_half`) count: a program that leaves them out, or rounds other values in their place, can miss the bound.
Values may be sent and summed in bfloat16 or wider, within the bound.
No kernel may reach another device: no remote copies, remote signals or barrier semaphores. Data moves between devices by JAX's collectives and lax.ppermute only.
A program may use at most 128 MiB of HBM per device.

```python
import math
import jax
import jax.numpy as jnp
from jax import lax

CH = 320
GROUPS = 32
TABLE = 1000
ITERS = 2
TSTEP = 8
LAT_H = 64
LAT_W = 96


def draw_latent_init(key, part):
    k_base, k_rows, k_cols, k_chan = jax.random.split(key, 4)
    full_shape = (LAT_H, LAT_W, CH)
    row_pos = jnp.arange(LAT_H, dtype=jnp.float32) / max(LAT_H - 1, 1)
    col_pos = jnp.arange(LAT_W, dtype=jnp.float32) / max(LAT_W - 1, 1)
    row_scale = jnp.exp(math.log(3.0) * (row_pos - 0.5)) * jnp.exp(jax.random.uniform(k_rows, (LAT_H,), jnp.float32, -0.35, 0.35))
    col_scale = jnp.exp(math.log(3.0) * (col_pos - 0.5)) * jnp.exp(jax.random.uniform(k_cols, (LAT_W,), jnp.float32, -0.35, 0.35))
    chan_scale = jnp.exp(jax.random.uniform(k_chan, (CH,), jnp.float32, math.log(0.3), math.log(3.0)))
    base_draw = jnp.clip(jax.random.normal(k_base, full_shape, jnp.float32), -4.0, 4.0)
    return base_draw * row_scale[:, None, None] * col_scale[None, :, None] * chan_scale[None, None, :]


def touch_ends(drawn, key, low, top_value):
    longest = drawn.shape.index(max(drawn.shape))
    spots = []
    for shift in (0, 1):
        where = [jax.random.randint(jax.random.fold_in(key, axis), (), 0, length) for axis, length in enumerate(drawn.shape)]
        where[longest] = (where[longest] + shift) % drawn.shape[longest]
        spots.append(tuple(where))
    return drawn.at[spots[0]].set(low).at[spots[1]].set(top_value)


def block_scale(own_key, dims, cuts, smallest, top_value):
    gain = 1.0
    for dim, parts in cuts:
        draws = jax.random.uniform(jax.random.fold_in(jax.random.fold_in(own_key, 6), dim), (parts,), jnp.float32, smallest / len(cuts), top_value / len(cuts))
        gain = gain * jnp.repeat(jnp.exp(draws), dims[dim] // parts).reshape((-1,) + (1,) * (len(dims) - 1 - dim))
    return gain


def normal_values(key, extent, width, limit, cuts=(), kind=jnp.bfloat16):
    values = width * jax.random.normal(key, extent, jnp.float32)
    if cuts:
        values = values * block_scale(key, extent, cuts, -0.22, 0.18)
    return jnp.clip(values, -limit, limit).astype(kind)


def setup_inputs(seed: int = 0) -> dict:
    seeds = jax.random.split(jax.random.key(seed), 11)
    latent_init = draw_latent_init(jax.random.fold_in(seeds[10], 71), 0)
    step_noise = normal_values(seeds[1], (TSTEP, LAT_H, LAT_W, CH), 1.0, 6.0, ((0, 2), (1, 4), (2, 4)))
    coef_state = jnp.clip(-0.06 + 0.04999999888241291 * jax.random.uniform(seeds[2], (TSTEP,), jnp.float32) ** block_scale(seeds[2], (TSTEP,), ((0, 2),), -0.2, 0.2), -0.06, -0.01)
    coef_drift = jnp.clip(jax.random.uniform(seeds[3], (TSTEP,), jnp.float32, -0.1, 0.1) * block_scale(seeds[3], (TSTEP,), ((0, 2),), -0.4, 0.0), -0.1, 0.1)
    coef_noise = jnp.clip(jnp.exp(math.log(0.2) - 1.3862944 * jax.random.uniform(seeds[4], (TSTEP,), jnp.float32) ** block_scale(seeds[4], (TSTEP,), ((0, 2),), -0.2, 0.2)), 0.05, 0.2)
    step_index = touch_ends(jax.random.randint(seeds[5], (TSTEP,), 0, TABLE), jax.random.fold_in(seeds[5], 1), 0, TABLE - 1).astype(jnp.int32)
    time_table = normal_values(seeds[6], (TABLE, CH), 0.3, 1.5, (), jnp.float32)
    norm_gain = jnp.clip(1.0 + 0.15 * jax.random.normal(seeds[7], (CH,), jnp.float32), 0.25, 1.75)
    conv_weight = normal_values(seeds[8], (3, 3, CH, CH), (9 * CH) ** -0.5, 0.109375)
    reward_grad = normal_values(seeds[9], (LAT_H, LAT_W, CH), 0.03, 0.18, ((0, 4), (1, 4)), jnp.float32)
    return dict(latent_init=latent_init, step_noise=step_noise, coef_state=coef_state, coef_drift=coef_drift, coef_noise=coef_noise, step_index=step_index, time_table=time_table, norm_gain=norm_gain, conv_weight=conv_weight, reward_grad=reward_grad)


EPSILON = 1e-05

def prepare_one(one_field, modulate):
    grouped = one_field.reshape(LAT_H * LAT_W, GROUPS, CH // GROUPS)
    cell_count = LAT_H * LAT_W * (CH // GROUPS)
    center = lax.optimization_barrier(jnp.sum(grouped, axis=(0, 2))) / cell_count
    shifted = grouped - center[None, :, None]
    spread = lax.optimization_barrier(jnp.sum(shifted * shifted, axis=(0, 2))) / cell_count
    inv_std = 1.0 / jnp.sqrt(spread + EPSILON)
    normal_field = (shifted * inv_std[None, :, None]).reshape(one_field.shape)
    pre_act = normal_field * modulate[None, None, :]
    activation = jax.nn.silu(pre_act).astype(jnp.bfloat16)
    act_pad = jnp.pad(activation, ((1, 1), (1, 1), (0, 0)))
    return (normal_field, inv_std, pre_act, act_pad)

def convolve_one(act_pad, conv_weight):
    result = jnp.zeros((LAT_H * LAT_W, CH), jnp.float32)
    for row_off in range(3):
        for col_off in range(3):
            window = act_pad[row_off:row_off + LAT_H, col_off:col_off + LAT_W, :].reshape(LAT_H * LAT_W, CH)
            result = result + jnp.dot(window, conv_weight[row_off, col_off], preferred_element_type=jnp.float32)
    return result.reshape(LAT_H, LAT_W, CH)

def drift_all(states, modulation, conv_weight):

    def map_one(field_pair):
        one_field, modulate = field_pair
        act_cache = prepare_one(one_field, modulate)
        return one_field + convolve_one(act_cache[3], conv_weight)
    return lax.map(map_one, (states, modulation))

def backprop_one(one_field, modulate, upstream, conv_weight, need_state):
    normal_field, inv_std, pre_act, act_pad = prepare_one(one_field, modulate)
    up_half = upstream.astype(jnp.bfloat16)
    up_flat = up_half.reshape(LAT_H * LAT_W, CH)
    pieces = []
    for row_off in range(3):
        row_terms = []
        for col_off in range(3):
            window = act_pad[row_off:row_off + LAT_H, col_off:col_off + LAT_W, :].reshape(LAT_H * LAT_W, CH)
            row_terms.append(jnp.dot(window.T, up_flat, preferred_element_type=jnp.float32))
        pieces.append(jnp.stack(row_terms))
    grad_piece = jnp.stack(pieces)
    if not need_state:
        return (jnp.zeros_like(upstream), grad_piece)
    up_pad = jnp.pad(up_half, ((1, 1), (1, 1), (0, 0)))
    d_act = jnp.zeros((LAT_H * LAT_W, CH), jnp.float32)
    for row_off in range(3):
        for col_off in range(3):
            window = up_pad[2 - row_off:2 - row_off + LAT_H, 2 - col_off:2 - col_off + LAT_W, :].reshape(LAT_H * LAT_W, CH)
            d_act = d_act + jnp.dot(window, conv_weight[row_off, col_off].T, preferred_element_type=jnp.float32)
    d_act = d_act.reshape(LAT_H, LAT_W, CH)
    sig_value = jax.nn.sigmoid(pre_act)
    d_norm = d_act * sig_value * (1.0 + pre_act * (1.0 - sig_value)) * modulate[None, None, :]
    cell_count = LAT_H * LAT_W * (CH // GROUPS)
    grouped_d = d_norm.reshape(LAT_H * LAT_W, GROUPS, CH // GROUPS)
    grouped_n = normal_field.reshape(LAT_H * LAT_W, GROUPS, CH // GROUPS)
    plain_mean = lax.optimization_barrier(jnp.sum(grouped_d, axis=(0, 2))) / cell_count
    cross_mean = lax.optimization_barrier(jnp.sum(grouped_d * grouped_n, axis=(0, 2))) / cell_count
    d_group = (grouped_d - plain_mean[None, :, None] - grouped_n * cross_mean[None, :, None]) * inv_std[None, :, None]
    return (upstream + d_group.reshape(upstream.shape), grad_piece)

def reference(latent_init, step_noise, coef_state, coef_drift, coef_noise, step_index, time_table, norm_gain, conv_weight, reward_grad):
    modulation = norm_gain[None, :] * (1.0 + time_table[step_index])
    state_c = coef_state[:, None, None, None]
    drift_c = coef_drift[:, None, None, None]
    noise_c = coef_noise[:, None, None, None]
    states = jnp.broadcast_to(latent_init[None], (TSTEP, LAT_H, LAT_W, CH))
    saved_states = []
    trajectory = states
    for sweep_index in range(ITERS):
        saved_states.append(states)
        drift_term = drift_all(states, modulation, conv_weight)
        increment = state_c * states + drift_c * drift_term + noise_c * step_noise.astype(jnp.float32)
        running = jnp.cumsum(increment, axis=0)
        trajectory = latent_init[None] + running
        before = jnp.concatenate([jnp.zeros_like(running[:1]), running[:-1]], axis=0)
        states = latent_init[None] + before
    adjoint = jnp.broadcast_to(reward_grad[None], trajectory.shape)
    grad_total = jnp.zeros((3, 3, CH, CH), jnp.float32)
    for sweep_index in range(ITERS - 1, -1, -1):
        upstream = drift_c * adjoint
        need_state = sweep_index > 0

        def scan_step(carry_sum, scan_items, need_state=need_state):
            one_field, modulate, one_up = scan_items
            d_state, grad_piece = backprop_one(one_field, modulate, one_up, conv_weight, need_state)
            return (carry_sum + grad_piece, d_state)
        grad_total, d_states = lax.scan(scan_step, grad_total, (saved_states[sweep_index], modulation, upstream))
        if need_state:
            through = state_c * adjoint + d_states
            suffix = jnp.cumsum(through[::-1], axis=0)[::-1]
            adjoint = jnp.concatenate([suffix[1:], jnp.zeros_like(suffix[:1])], axis=0)
    return (trajectory, grad_total)
```

```python
import functools

import jax
import jax.numpy as jnp
from jax import lax
from jax.experimental import pallas as pl
from jax.experimental.pallas import tpu as pltpu
from jax.sharding import PartitionSpec as P

GROUPS = 32
EPSILON = 1e-05
LANES = 128
F32 = jnp.float32
BF16 = jnp.bfloat16
VMEM_BYTES = 16 * 1024 * 1024
SMALL_BYTES = 4 * 1024 * 1024
WHOLE_BYTES = 61 * 10**6


def axis_bits(axes):
    bits = []
    for axis in axes:
        step = 1
        while step < lax.axis_size(axis):
            bits.append((axis, step))
            step *= 2
    return bits


def swap(value, axis, bit):
    pairs = [(i, i ^ bit) for i in range(lax.axis_size(axis))]
    return lax.ppermute(value, axis, pairs)


def half_of(tm_index, sy_index):
    last = lax.axis_size("tm") - 1
    return jnp.where(sy_index % 2 == 0, tm_index, last - tm_index)


def share(copies, axes):
    return lax.all_to_all(copies, axes, 0, 0)


def beside(value, axis, bit, work, needs):
    value, needs = lax.optimization_barrier((value, needs))
    other = swap(value, axis, bit)
    return lax.optimization_barrier((other, work(needs)))


def butterfly(value, axes, join, works):
    results = []
    for i, (axis, bit) in enumerate(axis_bits(axes)):
        if i < len(works):
            other, result = beside(value, axis, bit, *works[i](results))
            results.append(result)
        else:
            other = swap(value, axis, bit)
        value = join(value, other, 2**i)
    return value, results


def join_moments(count):
    def join(mine, other, size):
        gap = mine[0] - other[0]
        mean = 0.5 * (mine[0] + other[0])
        return jnp.stack([mean, mine[1] + other[1] + gap * gap * (0.5 * count * size)])

    return join


def join_sums(mine, other, size):
    return mine + other


def chain(axis):
    count = lax.axis_size(axis)
    forward = [(i, i + 1) for i in range(count - 1)]
    return forward, [(b, a) for a, b in forward]


def row_chain():
    slabs, tiles = lax.axis_size("tm"), lax.axis_size("sy")
    order = []
    for sy in range(tiles):
        for half in range(slabs):
            tm = half if sy % 2 == 0 else slabs - 1 - half
            order.append(tm * tiles + sy)
    forward = list(zip(order[:-1], order[1:]))
    return forward, [(b, a) for a, b in forward]


def group_matrix(rows, cols, group, channel_dim, slot):
    channel = lax.broadcasted_iota(jnp.int32, (rows, cols), channel_dim)
    place = lax.broadcasted_iota(jnp.int32, (rows, cols), 1 - channel_dim)
    scale = (1 << 16) // group + 1
    same = ((channel * scale) >> 16) + slot * GROUPS == place
    return (same & (channel < GROUPS * group)).astype(F32)


def exact_dot(left, right):
    return jnp.dot(left, right, precision=lax.Precision.HIGHEST, preferred_element_type=F32)


def gather_groups(values, group, slot):
    return exact_dot(values, group_matrix(values.shape[1], LANES, group, 0, slot))


def spread_groups(values, lanes, group):
    return exact_dot(values, group_matrix(LANES, lanes, group, 1, 0))


def lane_slot(values, slot):
    if slot:
        values = pltpu.roll(values, LANES - slot * GROUPS, 1)
    lane = lax.broadcasted_iota(jnp.int32, values.shape, 1)
    return jnp.where(lane < GROUPS, values, 0.0)


def merged_moments(parts, total_count, lanes, group):
    devices = parts.shape[0]
    total = jnp.sum(parts, axis=0)
    center = lane_slot(total, 0) * (1.0 / devices)
    gap = parts - center[None]
    between = lane_slot(jnp.sum(gap * gap, axis=0), 0) * (total_count / devices)
    spread = (between + lane_slot(total, 1)) * (1.0 / total_count)
    inv = lane_slot(1.0 / jnp.sqrt(spread + EPSILON), 0)
    return spread_groups(center, lanes, group), spread_groups(inv, lanes, group)


def final_moments(moments_ref, count, lanes, group):
    center = lane_slot(moments_ref[0], 0)
    inv = lane_slot(1.0 / jnp.sqrt(moments_ref[1] * (1.0 / count) + EPSILON), 0)
    return spread_groups(center, lanes, group), spread_groups(inv, lanes, group)


def start_copies(pairs, sem):
    copies = [pltpu.make_async_copy(a, b, sem.at[i]) for i, (a, b) in enumerate(pairs)]
    for copy in copies:
        copy.start()
    return copies


def wait_copies(copies):
    for copy in copies:
        copy.wait()


def widen(x, lanes):
    return jnp.concatenate([x, jnp.zeros((x.shape[0], lanes - x.shape[1]), x.dtype)], axis=1)


def framed_row(tile_ref, low_ref, high_ref, sides_ref, part, half, rows, row, lanes):
    tall = tile_ref.shape[0]
    place = half * rows + row - 1
    inner = tile_ref[jnp.clip(place, 0, tall - 1)]
    inner = jnp.where(place < 0, low_ref[part], jnp.where(place >= tall, high_ref[part], inner))
    left = sides_ref[0, part, pl.ds(place + 1, 1), :]
    right = sides_ref[1, part, pl.ds(place + 1, 1), :]
    return jnp.concatenate([left, widen(inner, lanes), right], axis=0)


def noise_of(own_ref, others_ref, place_ref, k, row, lanes):
    steps_here = own_ref.shape[0]
    slabs = others_ref.shape[0] + 1
    slab, step = divmod(k, steps_here)
    offset = lax.rem(place_ref[2] - slab + slabs, slabs)
    mine = own_ref[step, row].astype(F32)
    other = others_ref[jnp.maximum(offset - 1, 0), step, row].astype(F32)
    return widen(jnp.where(offset == 0, mine, other), lanes)


CORNERS = 8


def start_kernel(
    group, ready, index_ref, place_ref, state_ref, drift_ref, noise_coef_ref, lat_ref, reward_ref,
    time_ref, gain_ref, noise_hbm, part_ref, table_ref, low_ref, high_ref, first_ref, last_ref, sent_ref, sem,
):
    others, steps, rows = sent_ref.shape[:3]
    copies = start_copies(
        [
            (noise_hbm.at[:, pl.ds(place_ref[8 + i] * rows, rows)], sent_ref.at[i])
            for i in range(others)
        ],
        sem,
    )
    ready()
    tall, wide, channels = lat_ref.shape
    lanes = table_ref.shape[2]
    corners = []
    for part, ref in enumerate((lat_ref, reward_ref)):
        low_ref[part] = ref[tall - 1]
        high_ref[part] = ref[0]
        for row in range(tall):
            first_ref[part, row : row + 1] = ref[row, 0:1]
            last_ref[part, row : row + 1] = ref[row, wide - 1 : wide]
    for row in (0, tall - 1):
        for col in (0, wide - 1):
            for ref in (lat_ref, reward_ref):
                cell = widen(ref[row, col : col + 1], lanes)
                corners += [cell[:, at : at + LANES] for at in range(0, lanes, LANES)]
    entries = time_ref.shape[1]
    which = lax.broadcasted_iota(jnp.int32, (entries, LANES), 0)
    line = lax.broadcasted_iota(jnp.int32, (entries, LANES), 1)
    hit = jnp.zeros((entries, LANES), F32)
    for k in range(steps):
        hit = jnp.where((line == k) & (which == index_ref[k]), 1.0, hit)
    embedded = jnp.transpose(exact_dot(time_ref[...], hit))[:8]
    modulate = widen(gain_ref[...][None, :] * (1.0 + embedded), lanes)
    table_ref[0] = modulate[:steps]
    for k in range(steps):
        for i, ref in enumerate((state_ref, drift_ref, noise_coef_ref)):
            table_ref[i + 1, k : k + 1] = jnp.full((1, lanes), ref[k], F32)
    x = lat_ref[...].reshape(tall * wide, channels)
    sums = jnp.broadcast_to(jnp.sum(x, axis=0, keepdims=True), (8, channels))
    mean = gather_groups(sums, group, 0) * (1.0 / (tall * wide * group))
    gap = x - spread_groups(mean, channels, group)[0:1]
    square = jnp.broadcast_to(jnp.sum(gap * gap, axis=0, keepdims=True), (8, channels))
    part = jnp.concatenate([mean + gather_groups(square, group, 1)] + corners, axis=0)
    part_ref[...] = jnp.broadcast_to(part[None], part_ref.shape)
    wait_copies(copies)


def edge_kernel(ready, top_ref, bottom_ref, first_ref, last_ref, first_out, last_out):
    rows, steps, _ = first_ref.shape
    span = top_ref.shape[1]
    for out, ref, at in ((first_out, first_ref, 0), (last_out, last_ref, span - steps)):
        out[0] = top_ref[0, at : at + steps]
        out[1 : rows + 1] = ref[...]
        out[rows + 1] = bottom_ref[0, at : at + steps]


def table_kernel(ready, place_ref, own_ref, others_ref, out_ref):
    slabs = others_ref.shape[0] + 1
    kinds, steps, _ = own_ref.shape
    for offset in range(slabs):
        source = lax.rem(place_ref[2] - offset + slabs, slabs)
        for kind in range(kinds):
            rows = own_ref[kind] if offset == 0 else others_ref[offset - 1, kind]
            for k in range(steps):
                out_ref[kind, pl.ds(source * steps + k, 1), :] = rows[k : k + 1]


def packed_rows(taps, channels):
    whole = channels // LANES * LANES
    places = []
    for tap in range(taps):
        rest = taps * whole + tap // 2 * LANES + tap % 2 * (LANES // 2)
        places.append((tap * whole, rest))
    return whole, places


def pack_weight_kernel(ready, w_ref, out_ref, back_ref):
    taps, channels, _ = w_ref.shape
    lanes = out_ref.shape[1]
    whole, places = packed_rows(taps, channels)
    out_ref[...] = jnp.zeros(out_ref.shape, BF16)
    back_ref[...] = jnp.zeros(back_ref.shape, BF16)
    ready()
    for tap, (at, rest) in enumerate(places):
        for ref, value in ((out_ref, w_ref[tap]), (back_ref, jnp.transpose(w_ref[taps - 1 - tap]))):
            ref[at : at + whole, 0:channels] = value[:whole]
            ref[rest : rest + channels - whole, 0:channels] = value[whole:]


def half_turn(x):
    return pltpu.roll(x.astype(F32), LANES // 2, 1).astype(BF16)


def pair_rests(rests):
    pairs = []
    for i in range(0, len(rests), 2):
        pairs.append(rests[i] if i + 1 == len(rests) else rests[i] + half_turn(rests[i + 1]))
    return pairs


def convolve_rows(even_ref, odd_ref, w_ref, start, count, steps):
    span, lanes = odd_ref.shape[1:]
    parts = []
    for row_off in range(3):
        rows = pl.ds(start + row_off, count)
        parts.append(even_ref[rows, 0:span, :].reshape(count * span, lanes))
        parts.append(odd_ref[rows].reshape(count * span, lanes))
        parts.append(even_ref[rows, 2 * steps : 2 * steps + span, :].reshape(count * span, lanes))
    whole = lanes - LANES
    packed = [x[:, :whole] for x in parts] + pair_rests([x[:, whole:] for x in parts])
    return jnp.dot(jnp.concatenate(packed, axis=1), w_ref[...], preferred_element_type=F32)


def put_tiles(ref, value):
    for tile in range(ref.shape[0]):
        ref[tile] = value[:, tile * LANES : (tile + 1) * LANES]


def get_tiles(ref):
    return jnp.concatenate([ref[tile] for tile in range(ref.shape[0])], axis=1)


def get_step(ref, start, cols, steps):
    where = pl.ds(start, cols, stride=steps)
    return jnp.concatenate([ref[tile, where, :] for tile in range(ref.shape[0])], axis=1)


def put_step(ref, start, cols, steps, value):
    where = pl.ds(start, cols, stride=steps)
    for tile in range(ref.shape[0]):
        ref[tile, where, :] = value[:, tile * LANES : (tile + 1) * LANES]


def chunk_rows(rows, span):
    count = max(1, min(rows, 384 // span))
    while rows % count:
        count -= 1
    return count


def advance_row(row, at, half, rows, steps, lat_ref, noise, place_ref, coef_ref, y_ref, row_ref):
    lanes = row_ref.shape[0] * LANES
    cols = row_ref.shape[1] // steps
    own = widen(lat_ref[half * rows + row], lanes)
    run = jnp.zeros_like(own)
    for k in range(steps):
        put_step(row_ref, k, cols, steps, own + run)
        conv = get_step(y_ref, at + k, cols, steps)
        run = run + (
            coef_ref[1, k : k + 1] * own
            + coef_ref[2, k : k + 1] * (own + conv)
            + coef_ref[3, k : k + 1] * noise_of(*noise, place_ref, k, row, lanes)
        )
    return get_tiles(row_ref)


def edge_sweep_kernel(
    group, total_cells, ready, flag_ref, place_ref, low_ref, high_ref, left_ref, right_ref,
    parts_ref, coef_ref, lat_ref, others_ref, w_ref, noise_hbm,
    even_ref, odd_ref, sides_ref, first_row, last_row,
    noise_ref, y_ref, row_ref, sem,
):
    rows, span, lanes = odd_ref.shape
    rows = rows - 2
    steps = coef_ref.shape[1]
    cols = span // steps
    half = place_ref[0]
    tall = lat_ref.shape[0]
    own_noise = noise_hbm.at[:, pl.ds(half * rows, rows)]
    loads = start_copies([(own_noise, noise_ref)], sem)
    center, inv = merged_moments(parts_ref[:, :CORNERS], float(total_cells * group), lanes, group)
    center, inv = center[0:1], inv[0:1]
    pieces = lanes // LANES
    for side, ref in enumerate((left_ref, right_ref)):
        for part in range(2):
            sides_ref[side, part, 1 : tall + 1, :] = widen(ref[part], lanes)
            for end in range(2):
                at = CORNERS + ((3 - 2 * end - side) * 2 + part) * pieces
                device = place_ref[4 + 2 * end + side]
                cell = [parts_ref[device, at + i : at + i + 1, :] for i in range(pieces)]
                cell = jnp.concatenate(cell, axis=1) * flag_ref[4 + 2 * end + side]
                to = end * (tall + 1)
                sides_ref[side, part, to : to + 1, :] = cell
    ready()
    mod = coef_ref[0]

    def activate(row, _):
        field = framed_row(lat_ref, low_ref, high_ref, sides_ref, 0, half, rows, row, lanes)
        normal = (field - center) * inv
        pre = normal[:, None, :] * mod[None]
        act = pre / (1.0 + jnp.exp(-pre))
        keep = jnp.where(row == 0, flag_ref[0], jnp.where(row == rows + 1, flag_ref[1], 1.0))
        act = act * keep
        inner = act[1 : cols + 1]
        act = jnp.concatenate(
            [act[0:1] * flag_ref[2], inner, act[cols + 1 : cols + 2] * flag_ref[3]], axis=0
        )
        even_ref[row] = act.reshape((cols + 2) * steps, lanes).astype(BF16)
        odd_ref[row] = inner.reshape(span, lanes).astype(BF16)
        return 0

    lax.fori_loop(0, rows + 2, activate, 0)
    wait_copies(loads)
    for row, out in ((0, first_row), (rows - 1, last_row)):
        put_tiles(y_ref, convolve_rows(even_ref, odd_ref, w_ref, row, 1, steps))
        noise = (noise_ref, others_ref)
        out[0] = advance_row(row, 0, half, rows, steps, lat_ref, noise, place_ref, coef_ref, y_ref, row_ref)


def inner_sweep_kernel(
    group, ready, place_ref, first_row, last_row, even_ref, odd_ref, coef_ref, lat_ref, others_ref, w_ref,
    noise_hbm, states_ref, moment_ref, first_col, last_col, noise_ref, y_ref, row_ref, sem,
):
    rows, span, lanes = states_ref.shape
    steps = coef_ref.shape[1]
    cols = span // steps
    half = place_ref[0]
    own_noise = noise_hbm.at[:, pl.ds(half * rows, rows)]
    loads = start_copies([(own_noise, noise_ref)], sem)
    states_ref[0] = first_row[0]
    states_ref[rows - 1] = last_row[0]
    wait_copies(loads)
    count = chunk_rows(max(rows - 2, 1), span)

    def sweep(chunk, _):
        start = 1 + chunk * count
        put_tiles(y_ref, convolve_rows(even_ref, odd_ref, w_ref, start, count, steps))
        for inner in range(count):
            states_ref[start + inner] = advance_row(
                start + inner, inner * span, half, rows, steps, lat_ref, (noise_ref, others_ref),
                place_ref, coef_ref, y_ref, row_ref,
            )
        return 0

    lax.fori_loop(0, (rows - 2) // count, sweep, 0)
    zero = jnp.zeros((steps, lanes), F32)

    def add(row, total):
        return total + jnp.sum(states_ref[row].reshape(cols, steps, lanes), axis=0)

    mean = gather_groups(lax.fori_loop(0, rows, add, zero), group, 0) * (1.0 / (rows * cols * group))
    mean_here = spread_groups(mean, lanes, group)

    def squares(row, total):
        gap = states_ref[row].reshape(cols, steps, lanes) - mean_here[None]
        return total + jnp.sum(gap * gap, axis=0)

    moment_ref[0] = mean
    moment_ref[1] = gather_groups(lax.fori_loop(0, rows, squares, zero), group, 0)
    first_col[...] = states_ref[:, 0:steps]
    last_col[...] = states_ref[:, span - steps :]


def act_gradient_kernel(
    first, ready, place_ref, reward_ref, low_ref, high_ref, sides_ref, coef_ref, w_ref,
    out_ref, even_ref, odd_ref,
):
    rows, span, lanes = out_ref.shape
    steps = coef_ref.shape[1]
    cols = span // steps
    drift = coef_ref[2]

    def scale(row, _):
        field = framed_row(
            reward_ref, low_ref, high_ref, sides_ref, 1, place_ref[0], place_ref[3], row + first, lanes
        )
        up = field[:, None, :] * drift[None]
        even_ref[row] = up.reshape((cols + 2) * steps, lanes).astype(BF16)
        odd_ref[row] = up[1 : cols + 1].reshape(span, lanes).astype(BF16)
        return 0

    lax.fori_loop(0, rows + 2, scale, 0)
    count = chunk_rows(rows, span)

    def sweep(chunk, _):
        start = chunk * count
        out = convolve_rows(even_ref, odd_ref, w_ref, start, count, steps)
        out_ref[pl.ds(start, count)] = out.reshape(count, span, lanes)
        return 0

    lax.fori_loop(0, rows // count, sweep, 0)


def norm_gradient_kernel(
    group, total_cells, ready, flag_ref, place_ref, moments_ref, top_ref, bottom_ref, left_ref, right_ref,
    coef_ref, reward_ref, states_ref, *refs
):
    *d_act_refs, even_ref, odd_ref, d_norm_ref, sum_ref, norm_ref = refs
    rows, span, lanes = states_ref.shape
    steps = coef_ref.shape[1]
    cols = span // steps
    center, inv = final_moments(moments_ref, float(total_cells * group), lanes, group)
    norm_ref[0] = center
    norm_ref[1] = inv
    mod = coef_ref[0]

    def activate(at, inner, keep):
        field = jnp.concatenate(
            [left_ref[at][None], inner.reshape(cols, steps, lanes), right_ref[at][None]], axis=0
        )
        normal = (field - center[None]) * inv[None]
        pre = normal * mod[None]
        sig = 1.0 / (1.0 + jnp.exp(-pre))
        act = pre * sig
        if keep is not None:
            act = act * keep
        middle = act[1 : cols + 1]
        odd_ref[at] = middle.reshape(span, lanes).astype(BF16)
        act = jnp.concatenate(
            [act[0:1] * flag_ref[2], middle, act[cols + 1 : cols + 2] * flag_ref[3]], axis=0
        )
        even_ref[at] = act.reshape((cols + 2) * steps, lanes).astype(BF16)
        return [x[1 : cols + 1] for x in (normal, pre, sig)]

    activate(0, top_ref[0], flag_ref[0])
    activate(rows + 1, bottom_ref[0], flag_ref[1])

    def one(d_act_ref, first, index, sums):
        plain, cross, square = sums
        row = index + first
        normal, pre, sig = activate(row + 1, states_ref[row], None)
        slope = sig * (1.0 + pre * (1.0 - sig))
        d_norm = d_act_ref[index].reshape(cols, steps, lanes) * slope * mod[None]
        d_norm_ref[row] = d_norm.reshape(span, lanes)
        return (
            plain + jnp.sum(d_norm, axis=0),
            cross + jnp.sum(d_norm * normal, axis=0),
            square + jnp.sum(d_norm * d_norm, axis=0),
        )

    zero = jnp.zeros((steps, lanes), F32)
    sums = (zero, zero, zero)
    first = 0
    for d_act_ref in d_act_refs:
        count = d_act_ref.shape[0]
        sums = lax.fori_loop(0, count, functools.partial(one, d_act_ref, first), sums)
        first += count
    plain, cross, square = sums
    channels = reward_ref.shape[2]
    reward = reward_ref[pl.ds(place_ref[0] * rows, rows)].reshape(rows * cols, channels)
    reward = jnp.broadcast_to(jnp.sum(reward * reward, axis=0, keepdims=True), (steps, channels))
    sum_ref[...] = (
        gather_groups(plain, group, 0)
        + gather_groups(cross, group, 1)
        + gather_groups(square, group, 2)
        + gather_groups(reward, group, 3)
    )


def second_sweep_kernel(
    first, ready, place_ref, coef_ref, lat_ref, states_ref, others_ref, w_ref, even_ref, odd_ref, noise_hbm, *refs
):
    kept_hbm, sent_ref, noise_ref, y_ref, row_ref, out_ref, sem, out_sem = refs[-8:]
    all_rows, span, lanes = states_ref.shape
    slabs, steps_here, rows, cols, channels = out_ref.shape
    steps = slabs * steps_here
    half = place_ref[0]
    own_noise = noise_hbm.at[:, pl.ds(half * all_rows, all_rows)]
    wait_copies(start_copies([(own_noise, noise_ref)], sem))
    count = chunk_rows(rows, span)

    def sweep(chunk, _):
        start = chunk * count
        put_tiles(y_ref, convolve_rows(even_ref, odd_ref, w_ref, first + start, count, steps))
        for inner in range(count):
            row = first + start + inner
            own = widen(lat_ref[half * all_rows + row], lanes)
            put_tiles(row_ref, states_ref[row])
            run = jnp.zeros_like(own)
            for k in range(steps):
                conv = get_step(y_ref, inner * span + k, cols, steps)
                state = get_step(row_ref, k, cols, steps)
                run = run + (
                    coef_ref[1, k : k + 1] * state
                    + coef_ref[2, k : k + 1] * (state + conv)
                    + coef_ref[3, k : k + 1] * noise_of(noise_ref, others_ref, place_ref, k, row, lanes)
                )
                out_ref[k // steps_here, k % steps_here, start + inner] = run[:, :channels]
        return 0

    lax.fori_loop(0, rows // count, sweep, 0)
    for offset in range(1, slabs):
        sent_ref[offset - 1] = out_ref[lax.rem(place_ref[2] + offset, slabs)] * 0.125
    mine = place_ref[2]

    def complete(row, _):
        own = lat_ref[half * all_rows + first + row]
        for k in range(steps_here):
            out_ref[mine, k, row] = own + out_ref[mine, k, row]
        return 0

    lax.fori_loop(0, rows, complete, 0)
    pairs = [(out_ref.at[mine], kept_hbm.at[:, pl.ds(half * all_rows + first, rows)])]
    wait_copies(start_copies(pairs, out_sem))


def weight_terms(half, up_t, even_ref, odd_ref, steps, put):
    rows = odd_ref.shape[0] - 2
    span, lanes = odd_ref.shape[1:]
    whole = lanes - LANES

    def window(tap, first, last):
        row_off, col_off = divmod(tap, 3)
        if col_off == 1:
            part = odd_ref[row_off : row_off + rows, :, first:last]
        else:
            at = col_off * steps
            part = even_ref[row_off : row_off + rows, at : at + span, first:last]
        return part.reshape(rows * span, last - first)

    def emit(tile, part):
        term = jnp.dot(up_t, part, preferred_element_type=F32)
        for piece in range(part.shape[1] // LANES):
            put(tile + piece, term[:, piece * LANES : (piece + 1) * LANES])

    for i, tap in enumerate(range(6, 9) if half else range(0, 6)):
        emit(i * whole // LANES, window(tap, 0, whole))
    if half:
        rests = pair_rests([window(tap, whole, lanes) for tap in range(9)])
        emit(3 * whole // LANES, jnp.concatenate(rests, axis=1))
        put(3 * whole // LANES + 5, jnp.zeros((up_t.shape[0], LANES), F32))


def late_weight_kernel(half, ready, place_ref, reward_ref, coef_ref, even_ref, odd_ref, out_ref):
    rows, span, lanes = odd_ref.shape
    rows = rows - 2
    steps = coef_ref.shape[1]
    cols = span // steps
    channels = out_ref.shape[1]
    reward = reward_ref[pl.ds(place_ref[0] * rows, rows)].reshape(rows * cols, channels)
    up = widen(reward, lanes)[:, None, :] * coef_ref[2][None]
    up = up.reshape(rows * span, lanes).astype(BF16)

    def put(tile, value):
        out_ref[tile] = value

    weight_terms(half, jnp.transpose(up)[:channels], even_ref, odd_ref, steps, put)


def safe_scale(total, norm, mod, state_coef, drift_coef, cells, group):
    def whole(slot):
        return jnp.sqrt(jnp.sum(lane_slot(total, slot), axis=1, keepdims=True))

    gradient, reward = whole(2), whole(3)
    top_inv = jnp.max(norm, axis=1, keepdims=True)
    top_mod = jnp.max(jnp.abs(mod), axis=1, keepdims=True)
    state, drift = jnp.abs(state_coef[:, 0:1]), jnp.abs(drift_coef[:, 0:1])
    through = jnp.sum((state + drift) * reward + top_inv * gradient, axis=0, keepdims=True)
    field = top_mod * drift * (float(cells * group) ** 0.5)
    bound = jnp.sum(field * (reward + through), axis=0, keepdims=True) * 1.1
    power = jnp.clip(jnp.floor(jnp.log2(32768.0 / jnp.maximum(bound, 1e-30))), -60.0, 60.0)
    scale = jnp.ones_like(power)
    for bit in (32, 16, 8, 4, 2, 1):
        size = jnp.abs(power)
        has = jnp.floor(size / bit) - 2.0 * jnp.floor(size / (2 * bit)) > 0.5
        step = jnp.where(power > 0, 2.0**bit, 2.0**-bit)
        scale = jnp.where(has, scale * step, scale)
    return scale


def half_gradient(half, up_t, late_ref, scale, even_ref, odd_ref, steps, out_ref):
    slabs, _, share_rows, _ = out_ref.shape

    def put(tile, value):
        value = (value + late_ref[tile]) * scale
        for slab in range(slabs):
            out_ref[slab, tile] = value[slab * share_rows : (slab + 1) * share_rows]

    weight_terms(half, up_t, even_ref, odd_ref, steps, put)


def kept_weight_kernel(
    ready, place_ref, up_ref, coef_ref, scale_ref, even_ref, odd_ref, late_a_ref, late_b_ref, out_ref
):
    for half, late_ref in enumerate((late_a_ref, late_b_ref)):

        @pl.when(place_ref[1] == half)
        def _():
            scale, steps = scale_ref[0:1], coef_ref.shape[1]
            half_gradient(half, up_ref[...], late_ref, scale, even_ref, odd_ref, steps, out_ref)


def sent_weight_kernel(
    group, cells, ready, place_ref, states_ref, norm_ref, sums_ref, coef_ref,
    d_norm_ref, reward_ref, even_ref, odd_ref, late_a_ref, late_b_ref,
    out_ref, scale_ref, up_t_ref, d_ref, adj_ref, up_ref,
):
    rows, span, lanes = states_ref.shape
    steps = coef_ref.shape[1]
    cols = span // steps
    center, inv = norm_ref[0], norm_ref[1]
    total = sums_ref[...]
    count = 1.0 / (cells * group)
    plain = spread_groups(lane_slot(total, 0) * count, lanes, group)
    cross = spread_groups(lane_slot(total, 1) * count, lanes, group)
    scale = safe_scale(total, inv, coef_ref[0], coef_ref[1], coef_ref[2], cells, group)
    scale_ref[0:8] = jnp.broadcast_to(scale, (8, LANES))
    scale_ref[8:16] = jnp.broadcast_to(1.0 / scale, (8, LANES))

    def one(row, _):
        normal = (states_ref[row].reshape(cols, steps, lanes) - center[None]) * inv[None]
        d_norm = d_norm_ref[row].reshape(cols, steps, lanes)
        d_group = (d_norm - plain[None] - normal * cross[None]) * inv[None]
        put_tiles(d_ref, d_group.reshape(span, lanes))
        reward = widen(reward_ref[place_ref[0] * rows + row], lanes)
        run = jnp.zeros_like(reward)
        for k in range(steps - 1, -1, -1):
            drift = coef_ref[2, k : k + 1]
            put_step(adj_ref, k, cols, steps, drift * run)
            d_state = drift * reward + get_step(d_ref, k, cols, steps)
            run = run + (coef_ref[1, k : k + 1] * reward + d_state)
        up_ref[pl.ds(pl.multiple_of(row * span, 16), span), :] = get_tiles(adj_ref).astype(BF16)
        return 0

    lax.fori_loop(0, rows, one, 0)
    up_t_ref[...] = jnp.transpose(up_ref[...])[: up_t_ref.shape[0]]
    for half, late_ref in enumerate((late_a_ref, late_b_ref)):

        @pl.when(place_ref[1] != half)
        def _():
            half_gradient(half, up_t_ref[...], late_ref, scale, even_ref, odd_ref, steps, out_ref)


def unpack_kernel(ready, x_ref, scale_ref, out_ref):
    ready()
    whole = out_ref.shape[2] // LANES
    half = LANES // 2
    scale = scale_ref[8:9]
    for tap in range(9):
        for piece in range(whole):
            at = piece * LANES
            out_ref[tap, :, at : at + LANES] = x_ref[tap * whole + piece] * scale
        rest = x_ref[9 * whole + tap // 2] * scale
        if tap % 2:
            rest = pltpu.roll(rest, half, 1)
        out_ref[tap, :, whole * LANES :] = rest[:, :half]


def call(
    kernel, outs, scratch, flops, smem=(), vmem=(), load=(), hbm=(), grant=VMEM_BYTES, aliases=None, size=None
):
    args = [*smem, *vmem, *load, *hbm]
    counts = [len(smem) + len(vmem), len(load), len(hbm) + len(outs) + len(scratch)]
    specs = [pl.BlockSpec(memory_space=pltpu.SMEM)] * len(smem)
    specs += [pl.BlockSpec(memory_space=pltpu.VMEM)] * len(vmem)
    specs += [pl.BlockSpec(memory_space=pltpu.HBM)] * (len(load) + len(hbm))
    shapes = [jax.ShapeDtypeStruct(out[0], out[1]) for out in outs]
    out_specs = [pl.BlockSpec(memory_space=out[2] if len(out) > 2 else pltpu.VMEM) for out in outs]
    if size is None:
        size = sum(a.size * a.dtype.itemsize for a in [*args, *shapes])
    buffers = [s if not isinstance(s, tuple) else pltpu.VMEM(*s) for s in scratch]
    buffers += [pltpu.VMEM(x.shape, x.dtype) for x in load]
    buffers += [pltpu.SemaphoreType.DMA((len(load),))] if load else []

    def body(*refs):
        first, wanted, rest = counts[0], counts[1], counts[2]
        sources = refs[first : first + wanted]
        middle = refs[first + wanted : first + wanted + rest]
        held = refs[first + wanted + rest : first + wanted + rest + wanted]
        copies = start_copies(list(zip(sources, held)), refs[-1]) if wanted else []
        kernel(functools.partial(wait_copies, copies), *refs[:first], *held, *middle)

    return pl.pallas_call(
        body,
        out_shape=shapes,
        in_specs=specs,
        out_specs=out_specs,
        scratch_shapes=buffers,
        input_output_aliases=aliases or {},
        compiler_params=pltpu.CompilerParams(vmem_limit_bytes=grant),
        cost_estimate=pl.CostEstimate(flops=flops, bytes_accessed=size, transcendentals=0),
    )(*args)


F16 = jnp.float16


def bit_of(axis, bit):
    return (lax.axis_index(axis) // bit) % 2


def half_of_dim(value, which, dim):
    count = value.shape[dim] // 2
    return lax.dynamic_slice_in_dim(value, which * count, count, dim)


def half_sum(value, mine, send, dim):
    arrived = send(half_of_dim(value, 1 - mine, dim).astype(F16))
    return half_of_dim(value, mine, dim) + arrived.astype(value.dtype)


def both_halves(value, mine, send, dim):
    other = send(value)
    low = jnp.where(mine == 0, value, other)
    high = jnp.where(mine == 0, other, value)
    return jnp.concatenate([low, high], axis=dim)


def joint_sum(value, sides, dims, sends):
    def quarter(flips):
        part = value
        for side, dim, flip in zip(sides, dims, flips):
            part = half_of_dim(part, 1 - side if flip else side, dim)
        return part

    total = quarter((0, 0))
    arrived = [send(quarter(flips).astype(F16)) for flips, send in sends]
    for part in arrived:
        total = total + part.astype(value.dtype)
    return total


def joint_gather(value, sides, dims, sends):
    parts = {(0, 0): value}
    for flips, send in sends:
        parts[flips] = send(value)

    def order(first, second, side, dim):
        low = jnp.where(side == 0, first, second)
        high = jnp.where(side == 0, second, first)
        return jnp.concatenate([low, high], axis=dim)

    rows = [order(parts[(0, flip)], parts[(1, flip)], sides[0], dims[0]) for flip in (0, 1)]
    return order(rows[0], rows[1], sides[1], dims[1])


FLIPS = ((1, 0), (0, 1), (1, 1))


def reduce_weights(kept, arrived, ready):
    slabs, tiles, share_rows, lanes = kept.shape
    shape = (slabs, 2, tiles // 2, 2, 2, share_rows // 4, lanes)
    pieces = (kept.reshape(shape), arrived.reshape(shape))
    tall, wide = lax.axis_size("sy"), lax.axis_size("sx")
    even = bit_of("sx", 1) == 0

    def turned(sy, sx, turn):
        return (sy, sx ^ 2) if sx % 2 == turn else (sy ^ 1, sx)

    def send_tile(turn, flip_turn, flip_far):
        pairs = []
        for i in range(tall * wide):
            sy, sx = divmod(i, wide)
            to = turned(sy, sx, turn) if flip_turn else (sy, sx)
            to = (to[0] ^ 2, to[1]) if flip_far else to
            pairs.append((i, to[0] * wide + to[1]))
        return lambda value: lax.ppermute(value, ("sy", "sx"), pairs)

    def send_slab(bit, flip_slab, flip_far):
        pairs = []
        for i in range(slabs * tall):
            tm, sy = divmod(i, tall)
            pairs.append((i, (tm ^ (bit * flip_slab)) * tall + (sy ^ (2 * flip_far))))
        return lambda value: lax.ppermute(value, ("tm", "sy"), pairs)

    mine = [bit_of("sx", 2), bit_of("sy", 1)]
    first, second = (jnp.where(even, mine[turn], mine[1 - turn]) for turn in (0, 1))
    far = bit_of("sy", 2)

    def half(which):
        return sum(half_of_dim(x, which, 1) for x in pieces)

    other = send_tile(0, 1, 0)(half(1 - first).astype(F16))
    other, ready = lax.optimization_barrier((other, ready))
    value = half(first) + other.astype(F32)
    value = half_sum(value, second, send_tile(1, 1, 0), 3)
    bits = axis_bits(("tm",))[::-1]
    for axis, bit in bits[:-1]:
        value = half_sum(value, bit_of(axis, bit), lambda x, bit=bit: swap(x, "tm", bit), 0)
    if bits:
        sends = [(flips, send_slab(bits[-1][1], *flips)) for flips in FLIPS]
        value = joint_sum(value, (bit_of(*bits[-1]), far), (0, 4), sends)
    else:
        value = half_sum(value, far, lambda x: swap(x, "sy", 2), 4)
    value = value.astype(F16)
    sends = [(flips, send_tile(1, flips[1], flips[0])) for flips in FLIPS]
    value = joint_gather(value, (far, second), (4, 3), sends)
    value = both_halves(value, first, send_tile(0, 1, 0), 1)
    value = both_halves(value[None], bit_of("sx", 1), lambda x: swap(x, "sx", 1), 0)
    return value.astype(F32).reshape(2 * tiles, share_rows, lanes), ready


def shards(
    latent_init, step_noise, coef_state, coef_drift, coef_noise, step_index, time_table, norm_gain,
    conv_weight, reward_grad,
):
    tile_rows, cols, channels = latent_init.shape
    group = channels // GROUPS
    lanes = -(-channels // LANES) * LANES
    extra = lanes - channels
    slabs = lax.axis_size("tm")
    steps_here = step_noise.shape[0]
    steps = steps_here * slabs
    rows = tile_rows // slabs
    span = steps * cols
    tm, sy, sx = (lax.axis_index(axis) for axis in ("tm", "sy", "sx"))
    half = half_of(tm, sy)
    conv_flops = 2 * 9 * rows * span * channels * channels
    cells = tile_rows * lax.axis_size("sy") * cols * lax.axis_size("sx")
    targets = [half_of((tm + offset) % slabs, sy) for offset in range(1, slabs)]
    tall, wide = lax.axis_size("sy"), lax.axis_size("sx")
    diagonal = [(sy + dy, sx + dx) for dy in (-1, 1) for dx in (-1, 1)]
    corners = [jnp.clip(y, 0, tall - 1) * wide + jnp.clip(x, 0, wide - 1) for y, x in diagonal]
    place = [half, sx % 2, tm, jnp.int32(rows)] + corners + targets
    place = jnp.stack(place).astype(jnp.int32)
    flags = [(sy > 0) | (half > 0), (sy < tall - 1) | (half < slabs - 1), sx > 0, sx < wide - 1]
    flags += [(y >= 0) & (y < tall) & (x >= 0) & (x < wide) for y, x in diagonal]
    flags = jnp.stack(flags).astype(F32)

    def shifted(offset):
        return [(i, (i + offset) % slabs) for i in range(slabs)]

    tiles_axes = ("sy", "sx")
    tile_devices = lax.axis_size(tiles_axes)
    sent_shape = (slabs - 1, steps_here, rows, cols, channels)
    end_shape, col_shape = ((2, cols, channels), F32), ((2, tile_rows, channels), F32)
    part_rows = CORNERS + 8 * (lanes // LANES)
    moments, table, low_rows, high_rows, first_cols, last_cols, leaving = call(
        functools.partial(start_kernel, group),
        [((tile_devices, part_rows, LANES), F32), ((4, steps_here, lanes), F32)]
        + [end_shape, end_shape, col_shape, col_shape, (sent_shape, BF16)],
        [pltpu.SemaphoreType.DMA((slabs - 1,))],
        10**6,
        smem=[step_index, place, coef_state, coef_drift, coef_noise],
        load=[latent_init, reward_grad, time_table.T, norm_gain],
        hbm=[step_noise],
        grant=WHOLE_BYTES,
    )

    def to_slabs(pieces):
        if slabs == 2:
            return lax.ppermute(pieces, "tm", shifted(1))
        return jnp.stack([lax.ppermute(pieces[i], "tm", shifted(i + 1)) for i in range(slabs - 1)])

    down, up = chain("sy")
    right_way, left_way = chain("sx")
    low = lax.ppermute(low_rows, "sy", down)
    high = lax.ppermute(high_rows, "sy", up)
    left = lax.ppermute(last_cols, "sx", right_way)
    right = lax.ppermute(first_cols, "sx", left_way)
    other_tables = to_slabs(jnp.broadcast_to(table[None], (slabs - 1,) + table.shape))
    other_tables, leaving = lax.optimization_barrier((other_tables, leaving))
    others = to_slabs(leaving)
    parts1 = share(moments, tiles_axes)
    parts1, conv_weight = lax.optimization_barrier((parts1, conv_weight))
    (coefs,) = call(
        table_kernel, [((4, steps, lanes), F32)], [], 10**5, smem=[place], vmem=[table, other_tables],
        grant=SMALL_BYTES,
    )
    packed = ((9 * (lanes - LANES) + 5 * LANES, lanes), BF16)
    weight_out, weight_back = call(
        pack_weight_kernel, [packed, packed], [], 10**7, load=[conv_weight.reshape(9, channels, channels)],
    )

    even_shape = (rows + 2, (cols + 2) * steps, lanes)
    odd_shape = (rows + 2, span, lanes)
    field_shape = (rows, span, lanes)
    y_shape = (lanes // LANES, chunk_rows(rows, span) * span, LANES)
    row_shape = (lanes // LANES, span, LANES)
    noise_shape = (steps_here, rows, cols, channels)
    even_out, odd_out, field_out = (even_shape, BF16), (odd_shape, BF16), (field_shape, F32)
    edge_row, edge_col = ((1, span, lanes), F32), ((rows, steps, lanes), F32)
    noise_scratch = [(noise_shape, BF16)]
    even1, odd1, sides, first_row, last_row = call(
        functools.partial(edge_sweep_kernel, group, cells),
        [even_out, odd_out, ((2, 2, tile_rows + 2, lanes), F32), edge_row, edge_row],
        noise_scratch + [(row_shape, F32), (row_shape, F32), pltpu.SemaphoreType.DMA((1,))],
        conv_flops // 4,
        smem=[flags, place],
        vmem=[low, high, left, right, parts1, coefs, latent_init, others, weight_out],
        hbm=[step_noise],
    )
    down_rows, up_rows = row_chain()
    top = lax.ppermute(last_row, ("tm", "sy"), down_rows)
    bottom = lax.ppermute(first_row, ("tm", "sy"), up_rows)
    states, moments, first_col, last_col = call(
        functools.partial(inner_sweep_kernel, group),
        [field_out, ((2, steps, LANES), F32), edge_col, edge_col],
        noise_scratch + [(y_shape, F32), (row_shape, F32), pltpu.SemaphoreType.DMA((1,))],
        conv_flops,
        smem=[place],
        vmem=[first_row, last_row, even1, odd1, coefs, latent_init, others, weight_out],
        hbm=[step_noise],
    )

    def side_cols(args):
        top, bottom, first, last = args
        side_out = ((rows + 2, steps, lanes), F32)
        first, last = call(
            edge_kernel, [side_out, side_out], [], 10**5, vmem=[top, bottom, first, last], grant=SMALL_BYTES
        )
        return lax.ppermute(last, "sx", right_way), lax.ppermute(first, "sx", left_way)

    def act_gradient(first, count):
        def run(reward):
            (out,) = call(
                functools.partial(act_gradient_kernel, first),
                [((count, span, lanes), F32)],
                [((count + 2,) + even_shape[1:], BF16), ((count + 2,) + odd_shape[1:], BF16)],
                conv_flops // 4,
                smem=[place],
                vmem=[reward, low, high, sides, coefs, weight_back],
            )
            return out

        return run

    order = ("sx", "sy", "tm")
    cut = max(1, rows // 4)
    pieces = [(at, min(cut, rows - at)) for at in range(0, rows, cut)]

    def cols_and_first(args):
        return side_cols(args[1:]), act_gradient(*pieces[0])(args[0])

    def d_act_work(piece):
        return lambda done: (act_gradient(*piece), reward_grad)

    moments2, (((left2, right2), d_first), *d_rest) = butterfly(
        moments,
        order,
        join_moments(float(rows * cols * group)),
        [lambda done: (cols_and_first, (reward_grad, top, bottom, first_col, last_col))]
        + [d_act_work(piece) for piece in pieces[1:]],
    )
    even2, odd2, d_norm, sums, norm = call(
        functools.partial(norm_gradient_kernel, group, cells),
        [even_out, odd_out, field_out, ((steps, LANES), F32), ((2, steps, lanes), F32)],
        [],
        40 * rows * span * lanes,
        smem=[flags, place],
        vmem=[moments2, top, bottom, left2, right2, coefs, reward_grad, states, d_first, *d_rest],
    )

    share_rows = channels // slabs
    tiles = 9 * (channels // LANES) + 6

    def late_weight(half):
        def run(reward):
            (out,) = call(
                functools.partial(late_weight_kernel, half),
                [((tiles // 2, channels, LANES), F32)],
                [],
                conv_flops // 2,
                smem=[place],
                vmem=[reward, coefs, even2, odd2],
            )
            return out

        return lambda done: (run, reward_grad)

    def second_sweep(first, count):
        out_shape = (slabs, steps_here, count, cols, channels)

        def run(args):
            base = list(args[1:])
            return call(
                functools.partial(second_sweep_kernel, first),
                [(step_noise.shape, F32, pltpu.HBM), ((slabs - 1,) + out_shape[1:], F32)],
                [(noise_shape, BF16), (y_shape, F32), (row_shape, F32), (out_shape, F32)]
                + [pltpu.SemaphoreType.DMA((1,)), pltpu.SemaphoreType.DMA((1,))],
                conv_flops // 2,
                smem=[place],
                vmem=[coefs, args[0], states, others, weight_out, even2, odd2],
                hbm=[step_noise] + base,
                aliases={9: 0} if base else None,
            )

        return run

    sums, (late_a, late_b, (base, sent_a), (trajectory, sent_b)) = butterfly(
        sums,
        ("tm", "sx", "sy"),
        join_sums,
        [
            late_weight(0),
            late_weight(1),
            lambda done: (second_sweep(0, rows // 2), (latent_init,)),
            lambda done: (second_sweep(rows // 2, rows - rows // 2), (latent_init, done[2][0])),
        ],
    )
    landing = [to_slabs(sent_a.astype(F16)), to_slabs(sent_b.astype(F16))]

    payload = ((slabs, tiles // 2, share_rows, LANES), F32)
    up_shape = ((channels, rows * span), BF16)
    sent, scales, up_t = call(
        functools.partial(sent_weight_kernel, group, cells),
        [payload, ((16, LANES), F32), up_shape],
        [(row_shape, F32), (row_shape, F32), ((rows * span, lanes), BF16)],
        conv_flops // 2,
        smem=[place],
        vmem=[states, norm, sums, coefs, d_norm, reward_grad, even1, odd1, late_a, late_b],
        size=10**6,
    )

    def kept_weight(args):
        (kept,) = call(
            kept_weight_kernel,
            [payload],
            [],
            conv_flops // 2,
            smem=[place],
            vmem=[args[0], coefs, scales, even1, odd1, late_a, late_b],
        )
        return kept

    sent, landing = lax.optimization_barrier((sent, landing))
    arrived, kept = beside(sent, "sx", 1, kept_weight, (up_t,))

    cut = rows // 2
    for offset in range(1, slabs):
        source = half_of((tm - offset) % slabs, sy) * rows
        for part, at, count in zip(landing, (0, cut), (cut, rows - cut)):
            own = lax.dynamic_slice_in_dim(latent_init, source + at, count, 0)
            part = own[None] + 8.0 * part[offset - 1].astype(F32)
            trajectory = lax.dynamic_update_slice_in_dim(trajectory, part, source + at, 1)

    summed, trajectory = reduce_weights(kept, arrived, trajectory)
    (grad,) = call(
        unpack_kernel, [((9, share_rows, channels), F32)], [], 10**6, vmem=[summed, scales],
        grant=SMALL_BYTES,
    )
    return trajectory, grad.transpose(0, 2, 1).reshape(3, 3, channels, share_rows)


def solution(mesh):
    placed = (
        P("sy", "sx", None),
        P("tm", "sy", "sx", None),
        P("tm"),
        P("tm"),
        P("tm"),
        P("tm"),
        P(),
        P(),
        P(),
        P("sy", "sx", None),
    )
    return jax.shard_map(
        shards,
        mesh=mesh,
        in_specs=placed,
        out_specs=(P("tm", "sy", "sx", None), P(None, None, None, "tm")),
        check_vma=False,
    )
```

```python
import functools

import jax
import jax.numpy as jnp
from jax import lax
from jax.experimental import pallas as pl
from jax.experimental.pallas import tpu as pltpu
from jax.sharding import PartitionSpec as P

GROUPS = 32
EPSILON = 1e-05
LANES = 128
F32 = jnp.float32
BF16 = jnp.bfloat16
VMEM_BYTES = 16 * 1024 * 1024
SMALL_BYTES = 4 * 1024 * 1024
WHOLE_BYTES = 61 * 10**6


def axis_bits(axes):
    bits = []
    for axis in axes:
        step = 1
        while step < lax.axis_size(axis):
            bits.append((axis, step))
            step *= 2
    return bits


def swap(value, axis, bit):
    pairs = [(i, i ^ bit) for i in range(lax.axis_size(axis))]
    return lax.ppermute(value, axis, pairs)


def half_of(tm_index, sy_index):
    last = lax.axis_size("tm") - 1
    return jnp.where(sy_index % 2 == 0, tm_index, last - tm_index)


def share(copies, axes):
    return lax.all_to_all(copies, axes, 0, 0)


def beside(value, axis, bit, work, needs):
    value, needs = lax.optimization_barrier((value, needs))
    other = swap(value, axis, bit)
    return lax.optimization_barrier((other, work(needs)))


def butterfly(value, axes, join, works):
    results = []
    for i, (axis, bit) in enumerate(axis_bits(axes)):
        if i < len(works):
            other, result = beside(value, axis, bit, *works[i](results))
            results.append(result)
        else:
            other = swap(value, axis, bit)
        value = join(value, other, 2**i)
    return value, results


def join_moments(count):
    def join(mine, other, size):
        gap = mine[0] - other[0]
        mean = 0.5 * (mine[0] + other[0])
        return jnp.stack([mean, mine[1] + other[1] + gap * gap * (0.5 * count * size)])

    return join


def join_sums(mine, other, size):
    return mine + other


def chain(axis):
    count = lax.axis_size(axis)
    forward = [(i, i + 1) for i in range(count - 1)]
    return forward, [(b, a) for a, b in forward]


def row_chain():
    slabs, tiles = lax.axis_size("tm"), lax.axis_size("sy")
    order = []
    for sy in range(tiles):
        for half in range(slabs):
            tm = half if sy % 2 == 0 else slabs - 1 - half
            order.append(tm * tiles + sy)
    forward = list(zip(order[:-1], order[1:]))
    return forward, [(b, a) for a, b in forward]


def group_matrix(rows, cols, group, channel_dim, slot):
    channel = lax.broadcasted_iota(jnp.int32, (rows, cols), channel_dim)
    place = lax.broadcasted_iota(jnp.int32, (rows, cols), 1 - channel_dim)
    scale = (1 << 16) // group + 1
    same = ((channel * scale) >> 16) + slot * GROUPS == place
    return (same & (channel < GROUPS * group)).astype(F32)


def exact_dot(left, right):
    return jnp.dot(left, right, precision=lax.Precision.HIGHEST, preferred_element_type=F32)


def gather_groups(values, group, slot):
    return exact_dot(values, group_matrix(values.shape[1], LANES, group, 0, slot))


def spread_groups(values, lanes, group):
    return exact_dot(values, group_matrix(LANES, lanes, group, 1, 0))


def lane_slot(values, slot):
    if slot:
        values = pltpu.roll(values, LANES - slot * GROUPS, 1)
    lane = lax.broadcasted_iota(jnp.int32, values.shape, 1)
    return jnp.where(lane < GROUPS, values, 0.0)


def merged_moments(parts, total_count, lanes, group):
    devices = parts.shape[0]
    total = jnp.sum(parts, axis=0)
    center = lane_slot(total, 0) * (1.0 / devices)
    gap = parts - center[None]
    between = lane_slot(jnp.sum(gap * gap, axis=0), 0) * (total_count / devices)
    spread = (between + lane_slot(total, 1)) * (1.0 / total_count)
    inv = lane_slot(1.0 / jnp.sqrt(spread + EPSILON), 0)
    return spread_groups(center, lanes, group), spread_groups(inv, lanes, group)


def final_moments(moments_ref, count, lanes, group):
    center = lane_slot(moments_ref[0], 0)
    inv = lane_slot(1.0 / jnp.sqrt(moments_ref[1] * (1.0 / count) + EPSILON), 0)
    return spread_groups(center, lanes, group), spread_groups(inv, lanes, group)


def start_copies(pairs, sem):
    copies = [pltpu.make_async_copy(a, b, sem.at[i]) for i, (a, b) in enumerate(pairs)]
    for copy in copies:
        copy.start()
    return copies


def wait_copies(copies):
    for copy in copies:
        copy.wait()


def widen(x, lanes):
    return jnp.concatenate([x, jnp.zeros((x.shape[0], lanes - x.shape[1]), x.dtype)], axis=1)


def framed_row(tile_ref, low_ref, high_ref, sides_ref, part, half, rows, row, lanes):
    tall = tile_ref.shape[0]
    place = half * rows + row - 1
    inner = tile_ref[jnp.clip(place, 0, tall - 1)]
    inner = jnp.where(place < 0, low_ref[part], jnp.where(place >= tall, high_ref[part], inner))
    left = sides_ref[0, part, pl.ds(place + 1, 1), :]
    right = sides_ref[1, part, pl.ds(place + 1, 1), :]
    return jnp.concatenate([left, widen(inner, lanes), right], axis=0)


def noise_of(own_ref, others_ref, place_ref, k, row, lanes):
    steps_here = own_ref.shape[0]
    slabs = others_ref.shape[0] + 1
    slab, step = divmod(k, steps_here)
    offset = lax.rem(place_ref[2] - slab + slabs, slabs)
    mine = own_ref[step, row].astype(F32)
    other = others_ref[jnp.maximum(offset - 1, 0), step, row].astype(F32)
    return widen(jnp.where(offset == 0, mine, other), lanes)


CORNERS = 8


def start_kernel(
    group, ready, index_ref, place_ref, state_ref, drift_ref, noise_coef_ref, lat_ref, reward_ref,
    time_ref, gain_ref, noise_hbm, part_ref, table_ref, low_ref, high_ref, first_ref, last_ref, sent_ref, sem,
):
    others, steps, rows = sent_ref.shape[:3]
    copies = start_copies(
        [
            (noise_hbm.at[:, pl.ds(place_ref[8 + i] * rows, rows)], sent_ref.at[i])
            for i in range(others)
        ],
        sem,
    )
    ready()
    tall, wide, channels = lat_ref.shape
    lanes = table_ref.shape[2]
    corners = []
    for part, ref in enumerate((lat_ref, reward_ref)):
        low_ref[part] = ref[tall - 1]
        high_ref[part] = ref[0]
        for row in range(tall):
            first_ref[part, row : row + 1] = ref[row, 0:1]
            last_ref[part, row : row + 1] = ref[row, wide - 1 : wide]
    for row in (0, tall - 1):
        for col in (0, wide - 1):
            for ref in (lat_ref, reward_ref):
                cell = widen(ref[row, col : col + 1], lanes)
                corners += [cell[:, at : at + LANES] for at in range(0, lanes, LANES)]
    entries = time_ref.shape[1]
    which = lax.broadcasted_iota(jnp.int32, (entries, LANES), 0)
    line = lax.broadcasted_iota(jnp.int32, (entries, LANES), 1)
    hit = jnp.zeros((entries, LANES), F32)
    for k in range(steps):
        hit = jnp.where((line == k) & (which == index_ref[k]), 1.0, hit)
    embedded = jnp.transpose(exact_dot(time_ref[...], hit))[:8]
    modulate = widen(gain_ref[...][None, :] * (1.0 + embedded), lanes)
    table_ref[0] = modulate[:steps]
    for k in range(steps):
        for i, ref in enumerate((state_ref, drift_ref, noise_coef_ref)):
            table_ref[i + 1, k : k + 1] = jnp.full((1, lanes), ref[k], F32)
    x = lat_ref[...].reshape(tall * wide, channels)
    sums = jnp.broadcast_to(jnp.sum(x, axis=0, keepdims=True), (8, channels))
    mean = gather_groups(sums, group, 0) * (1.0 / (tall * wide * group))
    gap = x - spread_groups(mean, channels, group)[0:1]
    square = jnp.broadcast_to(jnp.sum(gap * gap, axis=0, keepdims=True), (8, channels))
    part = jnp.concatenate([mean + gather_groups(square, group, 1)] + corners, axis=0)
    part_ref[...] = jnp.broadcast_to(part[None], part_ref.shape)
    wait_copies(copies)


def edge_kernel(ready, top_ref, bottom_ref, first_ref, last_ref, first_out, last_out):
    rows, steps, _ = first_ref.shape
    span = top_ref.shape[1]
    for out, ref, at in ((first_out, first_ref, 0), (last_out, last_ref, span - steps)):
        out[0] = top_ref[0, at : at + steps]
        out[1 : rows + 1] = ref[...]
        out[rows + 1] = bottom_ref[0, at : at + steps]


def table_kernel(ready, place_ref, own_ref, others_ref, out_ref):
    slabs = others_ref.shape[0] + 1
    kinds, steps, _ = own_ref.shape
    for offset in range(slabs):
        source = lax.rem(place_ref[2] - offset + slabs, slabs)
        for kind in range(kinds):
            rows = own_ref[kind] if offset == 0 else others_ref[offset - 1, kind]
            for k in range(steps):
                out_ref[kind, pl.ds(source * steps + k, 1), :] = rows[k : k + 1]


def packed_rows(taps, channels):
    whole = channels // LANES * LANES
    places = []
    for tap in range(taps):
        rest = taps * whole + tap // 2 * LANES + tap % 2 * (LANES // 2)
        places.append((tap * whole, rest))
    return whole, places


def pack_weight_kernel(ready, w_ref, out_ref, back_ref):
    taps, channels, _ = w_ref.shape
    lanes = out_ref.shape[1]
    whole, places = packed_rows(taps, channels)
    out_ref[...] = jnp.zeros(out_ref.shape, BF16)
    back_ref[...] = jnp.zeros(back_ref.shape, BF16)
    ready()
    for tap, (at, rest) in enumerate(places):
        for ref, value in ((out_ref, w_ref[tap]), (back_ref, jnp.transpose(w_ref[taps - 1 - tap]))):
            ref[at : at + whole, 0:channels] = value[:whole]
            ref[rest : rest + channels - whole, 0:channels] = value[whole:]


def half_turn(x):
    return pltpu.roll(x.astype(F32), LANES // 2, 1).astype(BF16)


def pair_rests(rests):
    pairs = []
    for i in range(0, len(rests), 2):
        pairs.append(rests[i] if i + 1 == len(rests) else rests[i] + half_turn(rests[i + 1]))
    return pairs


def convolve_rows(even_ref, odd_ref, w_ref, start, count, steps):
    span, lanes = odd_ref.shape[1:]
    parts = []
    for row_off in range(3):
        rows = pl.ds(start + row_off, count)
        parts.append(even_ref[rows, 0:span, :].reshape(count * span, lanes))
        parts.append(odd_ref[rows].reshape(count * span, lanes))
        parts.append(even_ref[rows, 2 * steps : 2 * steps + span, :].reshape(count * span, lanes))
    whole = lanes - LANES
    packed = [x[:, :whole] for x in parts] + pair_rests([x[:, whole:] for x in parts])
    return jnp.dot(jnp.concatenate(packed, axis=1), w_ref[...], preferred_element_type=F32)


def put_tiles(ref, value):
    for tile in range(ref.shape[0]):
        ref[tile] = value[:, tile * LANES : (tile + 1) * LANES]


def get_tiles(ref):
    return jnp.concatenate([ref[tile] for tile in range(ref.shape[0])], axis=1)


def get_step(ref, start, cols, steps):
    where = pl.ds(start, cols, stride=steps)
    return jnp.concatenate([ref[tile, where, :] for tile in range(ref.shape[0])], axis=1)


def put_step(ref, start, cols, steps, value):
    where = pl.ds(start, cols, stride=steps)
    for tile in range(ref.shape[0]):
        ref[tile, where, :] = value[:, tile * LANES : (tile + 1) * LANES]


def chunk_rows(rows, span):
    count = max(1, min(rows, 384 // span))
    while rows % count:
        count -= 1
    return count


def advance_row(row, at, half, rows, steps, lat_ref, noise, place_ref, coef_ref, y_ref, row_ref):
    lanes = row_ref.shape[0] * LANES
    cols = row_ref.shape[1] // steps
    own = widen(lat_ref[half * rows + row], lanes)
    run = jnp.zeros_like(own)
    for k in range(steps):
        put_step(row_ref, k, cols, steps, own + run)
        conv = get_step(y_ref, at + k, cols, steps)
        run = run + (
            coef_ref[1, k : k + 1] * own
            + coef_ref[2, k : k + 1] * (own + conv)
            + coef_ref[3, k : k + 1] * noise_of(*noise, place_ref, k, row, lanes)
        )
    return get_tiles(row_ref)


def edge_sweep_kernel(
    group, total_cells, ready, flag_ref, place_ref, low_ref, high_ref, left_ref, right_ref,
    parts_ref, coef_ref, lat_ref, others_ref, w_ref, noise_hbm,
    even_ref, odd_ref, sides_ref, first_row, last_row,
    noise_ref, y_ref, row_ref, sem,
):
    rows, span, lanes = odd_ref.shape
    rows = rows - 2
    steps = coef_ref.shape[1]
    cols = span // steps
    half = place_ref[0]
    tall = lat_ref.shape[0]
    own_noise = noise_hbm.at[:, pl.ds(half * rows, rows)]
    loads = start_copies([(own_noise, noise_ref)], sem)
    center, inv = merged_moments(parts_ref[:, :CORNERS], float(total_cells * group), lanes, group)
    center, inv = center[0:1], inv[0:1]
    pieces = lanes // LANES
    for side, ref in enumerate((left_ref, right_ref)):
        for part in range(2):
            sides_ref[side, part, 1 : tall + 1, :] = widen(ref[part], lanes)
            for end in range(2):
                at = CORNERS + ((3 - 2 * end - side) * 2 + part) * pieces
                device = place_ref[4 + 2 * end + side]
                cell = [parts_ref[device, at + i : at + i + 1, :] for i in range(pieces)]
                cell = jnp.concatenate(cell, axis=1) * flag_ref[4 + 2 * end + side]
                to = end * (tall + 1)
                sides_ref[side, part, to : to + 1, :] = cell
    ready()
    mod = coef_ref[0]

    def activate(row, _):
        field = framed_row(lat_ref, low_ref, high_ref, sides_ref, 0, half, rows, row, lanes)
        normal = (field - center) * inv
        pre = normal[:, None, :] * mod[None]
        act = pre / (1.0 + jnp.exp(-pre))
        keep = jnp.where(row == 0, flag_ref[0], jnp.where(row == rows + 1, flag_ref[1], 1.0))
        act = act * keep
        inner = act[1 : cols + 1]
        act = jnp.concatenate(
            [act[0:1] * flag_ref[2], inner, act[cols + 1 : cols + 2] * flag_ref[3]], axis=0
        )
        even_ref[row] = act.reshape((cols + 2) * steps, lanes).astype(BF16)
        odd_ref[row] = inner.reshape(span, lanes).astype(BF16)
        return 0

    lax.fori_loop(0, rows + 2, activate, 0)
    wait_copies(loads)
    for row, out in ((0, first_row), (rows - 1, last_row)):
        put_tiles(y_ref, convolve_rows(even_ref, odd_ref, w_ref, row, 1, steps))
        noise = (noise_ref, others_ref)
        out[0] = advance_row(row, 0, half, rows, steps, lat_ref, noise, place_ref, coef_ref, y_ref, row_ref)


def inner_sweep_kernel(
    group, ready, place_ref, first_row, last_row, even_ref, odd_ref, coef_ref, lat_ref, others_ref, w_ref,
    noise_hbm, states_ref, moment_ref, first_col, last_col, noise_ref, y_ref, row_ref, sem,
):
    rows, span, lanes = states_ref.shape
    steps = coef_ref.shape[1]
    cols = span // steps
    half = place_ref[0]
    own_noise = noise_hbm.at[:, pl.ds(half * rows, rows)]
    loads = start_copies([(own_noise, noise_ref)], sem)
    states_ref[0] = first_row[0]
    states_ref[rows - 1] = last_row[0]
    wait_copies(loads)
    count = chunk_rows(max(rows - 2, 1), span)

    def sweep(chunk, _):
        start = 1 + chunk * count
        put_tiles(y_ref, convolve_rows(even_ref, odd_ref, w_ref, start, count, steps))
        for inner in range(count):
            states_ref[start + inner] = advance_row(
                start + inner, inner * span, half, rows, steps, lat_ref, (noise_ref, others_ref),
                place_ref, coef_ref, y_ref, row_ref,
            )
        return 0

    lax.fori_loop(0, (rows - 2) // count, sweep, 0)
    zero = jnp.zeros((steps, lanes), F32)

    def add(row, total):
        return total + jnp.sum(states_ref[row].reshape(cols, steps, lanes), axis=0)

    mean = gather_groups(lax.fori_loop(0, rows, add, zero), group, 0) * (1.0 / (rows * cols * group))
    mean_here = spread_groups(mean, lanes, group)

    def squares(row, total):
        gap = states_ref[row].reshape(cols, steps, lanes) - mean_here[None]
        return total + jnp.sum(gap * gap, axis=0)

    moment_ref[0] = mean
    moment_ref[1] = gather_groups(lax.fori_loop(0, rows, squares, zero), group, 0)
    first_col[...] = states_ref[:, 0:steps]
    last_col[...] = states_ref[:, span - steps :]


def act_gradient_kernel(
    first, ready, place_ref, reward_ref, low_ref, high_ref, sides_ref, coef_ref, w_ref,
    out_ref, even_ref, odd_ref,
):
    rows, span, lanes = out_ref.shape
    steps = coef_ref.shape[1]
    cols = span // steps
    drift = coef_ref[2]

    def scale(row, _):
        field = framed_row(
            reward_ref, low_ref, high_ref, sides_ref, 1, place_ref[0], place_ref[3], row + first, lanes
        )
        up = field[:, None, :] * drift[None]
        even_ref[row] = up.reshape((cols + 2) * steps, lanes).astype(BF16)
        odd_ref[row] = up[1 : cols + 1].reshape(span, lanes).astype(BF16)
        return 0

    lax.fori_loop(0, rows + 2, scale, 0)
    count = chunk_rows(rows, span)

    def sweep(chunk, _):
        start = chunk * count
        out = convolve_rows(even_ref, odd_ref, w_ref, start, count, steps)
        out_ref[pl.ds(start, count)] = out.reshape(count, span, lanes)
        return 0

    lax.fori_loop(0, rows // count, sweep, 0)


def norm_gradient_kernel(
    group, total_cells, ready, flag_ref, place_ref, moments_ref, top_ref, bottom_ref, left_ref, right_ref,
    coef_ref, reward_ref, states_ref, *refs
):
    *d_act_refs, even_ref, odd_ref, d_norm_ref, sum_ref, norm_ref = refs
    rows, span, lanes = states_ref.shape
    steps = coef_ref.shape[1]
    cols = span // steps
    center, inv = final_moments(moments_ref, float(total_cells * group), lanes, group)
    norm_ref[0] = center
    norm_ref[1] = inv
    mod = coef_ref[0]

    def activate(at, inner, keep):
        field = jnp.concatenate(
            [left_ref[at][None], inner.reshape(cols, steps, lanes), right_ref[at][None]], axis=0
        )
        normal = (field - center[None]) * inv[None]
        pre = normal * mod[None]
        sig = 1.0 / (1.0 + jnp.exp(-pre))
        act = pre * sig
        if keep is not None:
            act = act * keep
        middle = act[1 : cols + 1]
        odd_ref[at] = middle.reshape(span, lanes).astype(BF16)
        act = jnp.concatenate(
            [act[0:1] * flag_ref[2], middle, act[cols + 1 : cols + 2] * flag_ref[3]], axis=0
        )
        even_ref[at] = act.reshape((cols + 2) * steps, lanes).astype(BF16)
        return [x[1 : cols + 1] for x in (normal, pre, sig)]

    activate(0, top_ref[0], flag_ref[0])
    activate(rows + 1, bottom_ref[0], flag_ref[1])

    def one(d_act_ref, first, index, sums):
        plain, cross, square = sums
        row = index + first
        normal, pre, sig = activate(row + 1, states_ref[row], None)
        slope = sig * (1.0 + pre * (1.0 - sig))
        d_norm = d_act_ref[index].reshape(cols, steps, lanes) * slope * mod[None]
        d_norm_ref[row] = d_norm.reshape(span, lanes)
        return (
            plain + jnp.sum(d_norm, axis=0),
            cross + jnp.sum(d_norm * normal, axis=0),
            square + jnp.sum(d_norm * d_norm, axis=0),
        )

    zero = jnp.zeros((steps, lanes), F32)
    sums = (zero, zero, zero)
    first = 0
    for d_act_ref in d_act_refs:
        count = d_act_ref.shape[0]
        sums = lax.fori_loop(0, count, functools.partial(one, d_act_ref, first), sums)
        first += count
    plain, cross, square = sums
    channels = reward_ref.shape[2]
    reward = reward_ref[pl.ds(place_ref[0] * rows, rows)].reshape(rows * cols, channels)
    reward = jnp.broadcast_to(jnp.sum(reward * reward, axis=0, keepdims=True), (steps, channels))
    sum_ref[...] = (
        gather_groups(plain, group, 0)
        + gather_groups(cross, group, 1)
        + gather_groups(square, group, 2)
        + gather_groups(reward, group, 3)
    )


def second_sweep_kernel(
    first, ready, place_ref, coef_ref, lat_ref, states_ref, others_ref, w_ref, even_ref, odd_ref, noise_hbm, *refs
):
    kept_hbm, sent_ref, noise_ref, y_ref, row_ref, out_ref, sem, out_sem = refs[-8:]
    all_rows, span, lanes = states_ref.shape
    slabs, steps_here, rows, cols, channels = out_ref.shape
    steps = slabs * steps_here
    half = place_ref[0]
    own_noise = noise_hbm.at[:, pl.ds(half * all_rows, all_rows)]
    wait_copies(start_copies([(own_noise, noise_ref)], sem))
    count = chunk_rows(rows, span)

    def sweep(chunk, _):
        start = chunk * count
        put_tiles(y_ref, convolve_rows(even_ref, odd_ref, w_ref, first + start, count, steps))
        for inner in range(count):
            row = first + start + inner
            own = widen(lat_ref[half * all_rows + row], lanes)
            put_tiles(row_ref, states_ref[row])
            run = jnp.zeros_like(own)
            for k in range(steps):
                conv = get_step(y_ref, inner * span + k, cols, steps)
                state = get_step(row_ref, k, cols, steps)
                run = run + (
                    coef_ref[1, k : k + 1] * state
                    + coef_ref[2, k : k + 1] * (state + conv)
                    + coef_ref[3, k : k + 1] * noise_of(noise_ref, others_ref, place_ref, k, row, lanes)
                )
                out_ref[k // steps_here, k % steps_here, start + inner] = run[:, :channels]
        return 0

    lax.fori_loop(0, rows // count, sweep, 0)
    for offset in range(1, slabs):
        sent_ref[offset - 1] = out_ref[lax.rem(place_ref[2] + offset, slabs)] * 0.125
    mine = place_ref[2]

    def complete(row, _):
        own = lat_ref[half * all_rows + first + row]
        for k in range(steps_here):
            out_ref[mine, k, row] = own + out_ref[mine, k, row]
        return 0

    lax.fori_loop(0, rows, complete, 0)
    pairs = [(out_ref.at[mine], kept_hbm.at[:, pl.ds(half * all_rows + first, rows)])]
    wait_copies(start_copies(pairs, out_sem))


def land_kernel(first, ready, place_ref, lat_ref, part_ref, base_hbm, out_hbm, hold_ref, sem):
    others, steps, count = part_ref.shape[:3]
    copies = []
    for i in range(others):
        at = place_ref[8 + others + i] * place_ref[3] + first

        def add(row, _):
            own = lat_ref[at + row]
            for k in range(steps):
                hold_ref[i, k, row] = own + 8.0 * part_ref[i, k, row]
            return 0

        lax.fori_loop(0, count, add, 0)
        copies.append(pltpu.make_async_copy(hold_ref.at[i], out_hbm.at[:, pl.ds(at, count)], sem.at[i]))
        copies[-1].start()
    wait_copies(copies)


def weight_terms(half, up_t, even_ref, odd_ref, steps, put):
    rows = odd_ref.shape[0] - 2
    span, lanes = odd_ref.shape[1:]
    whole = lanes - LANES

    def window(tap, first, last):
        row_off, col_off = divmod(tap, 3)
        if col_off == 1:
            part = odd_ref[row_off : row_off + rows, :, first:last]
        else:
            at = col_off * steps
            part = even_ref[row_off : row_off + rows, at : at + span, first:last]
        return part.reshape(rows * span, last - first)

    def emit(tile, part):
        term = jnp.dot(up_t, part, preferred_element_type=F32)
        for piece in range(part.shape[1] // LANES):
            put(tile + piece, term[:, piece * LANES : (piece + 1) * LANES])

    for i, tap in enumerate(range(6, 9) if half else range(0, 6)):
        emit(i * whole // LANES, window(tap, 0, whole))
    if half:
        rests = pair_rests([window(tap, whole, lanes) for tap in range(9)])
        emit(3 * whole // LANES, jnp.concatenate(rests, axis=1))
        put(3 * whole // LANES + 5, jnp.zeros((up_t.shape[0], LANES), F32))


def late_weight_kernel(half, ready, place_ref, reward_ref, coef_ref, even_ref, odd_ref, out_ref):
    rows, span, lanes = odd_ref.shape
    rows = rows - 2
    steps = coef_ref.shape[1]
    cols = span // steps
    channels = out_ref.shape[1]
    reward = reward_ref[pl.ds(place_ref[0] * rows, rows)].reshape(rows * cols, channels)
    up = widen(reward, lanes)[:, None, :] * coef_ref[2][None]
    up = up.reshape(rows * span, lanes).astype(BF16)

    def put(tile, value):
        out_ref[tile] = value

    weight_terms(half, jnp.transpose(up)[:channels], even_ref, odd_ref, steps, put)


def safe_scale(total, norm, mod, state_coef, drift_coef, cells, group):
    def whole(slot):
        return jnp.sqrt(jnp.sum(lane_slot(total, slot), axis=1, keepdims=True))

    gradient, reward = whole(2), whole(3)
    top_inv = jnp.max(norm, axis=1, keepdims=True)
    top_mod = jnp.max(jnp.abs(mod), axis=1, keepdims=True)
    state, drift = jnp.abs(state_coef[:, 0:1]), jnp.abs(drift_coef[:, 0:1])
    through = jnp.sum((state + drift) * reward + top_inv * gradient, axis=0, keepdims=True)
    field = top_mod * drift * (float(cells * group) ** 0.5)
    bound = jnp.sum(field * (reward + through), axis=0, keepdims=True) * 1.1
    power = jnp.clip(jnp.floor(jnp.log2(32768.0 / jnp.maximum(bound, 1e-30))), -60.0, 60.0)
    scale = jnp.ones_like(power)
    for bit in (32, 16, 8, 4, 2, 1):
        size = jnp.abs(power)
        has = jnp.floor(size / bit) - 2.0 * jnp.floor(size / (2 * bit)) > 0.5
        step = jnp.where(power > 0, 2.0**bit, 2.0**-bit)
        scale = jnp.where(has, scale * step, scale)
    return scale


def half_gradient(half, up_t, late_ref, scale, even_ref, odd_ref, steps, out_ref):
    slabs, _, share_rows, _ = out_ref.shape

    def put(tile, value):
        value = (value + late_ref[tile]) * scale
        for slab in range(slabs):
            out_ref[slab, tile] = value[slab * share_rows : (slab + 1) * share_rows]

    weight_terms(half, up_t, even_ref, odd_ref, steps, put)


def kept_weight_kernel(
    ready, place_ref, up_ref, coef_ref, scale_ref, even_ref, odd_ref, late_a_ref, late_b_ref, out_ref
):
    for half, late_ref in enumerate((late_a_ref, late_b_ref)):

        @pl.when(place_ref[1] == half)
        def _():
            scale, steps = scale_ref[0:1], coef_ref.shape[1]
            half_gradient(half, up_ref[...], late_ref, scale, even_ref, odd_ref, steps, out_ref)


def sent_weight_kernel(
    group, cells, ready, place_ref, states_ref, norm_ref, sums_ref, coef_ref,
    d_norm_ref, reward_ref, even_ref, odd_ref, late_a_ref, late_b_ref,
    out_ref, scale_ref, up_t_ref, d_ref, adj_ref, up_ref,
):
    rows, span, lanes = states_ref.shape
    steps = coef_ref.shape[1]
    cols = span // steps
    center, inv = norm_ref[0], norm_ref[1]
    total = sums_ref[...]
    count = 1.0 / (cells * group)
    plain = spread_groups(lane_slot(total, 0) * count, lanes, group)
    cross = spread_groups(lane_slot(total, 1) * count, lanes, group)
    scale = safe_scale(total, inv, coef_ref[0], coef_ref[1], coef_ref[2], cells, group)
    scale_ref[0:8] = jnp.broadcast_to(scale, (8, LANES))
    scale_ref[8:16] = jnp.broadcast_to(1.0 / scale, (8, LANES))

    def one(row, _):
        normal = (states_ref[row].reshape(cols, steps, lanes) - center[None]) * inv[None]
        d_norm = d_norm_ref[row].reshape(cols, steps, lanes)
        d_group = (d_norm - plain[None] - normal * cross[None]) * inv[None]
        put_tiles(d_ref, d_group.reshape(span, lanes))
        reward = widen(reward_ref[place_ref[0] * rows + row], lanes)
        run = jnp.zeros_like(reward)
        for k in range(steps - 1, -1, -1):
            drift = coef_ref[2, k : k + 1]
            put_step(adj_ref, k, cols, steps, drift * run)
            d_state = drift * reward + get_step(d_ref, k, cols, steps)
            run = run + (coef_ref[1, k : k + 1] * reward + d_state)
        up_ref[pl.ds(pl.multiple_of(row * span, 16), span), :] = get_tiles(adj_ref).astype(BF16)
        return 0

    lax.fori_loop(0, rows, one, 0)
    up_t_ref[...] = jnp.transpose(up_ref[...])[: up_t_ref.shape[0]]
    for half, late_ref in enumerate((late_a_ref, late_b_ref)):

        @pl.when(place_ref[1] != half)
        def _():
            half_gradient(half, up_t_ref[...], late_ref, scale, even_ref, odd_ref, steps, out_ref)


def unpack_kernel(ready, x_ref, scale_ref, out_ref):
    ready()
    whole = out_ref.shape[2] // LANES
    half = LANES // 2
    scale = scale_ref[8:9]
    for tap in range(9):
        for piece in range(whole):
            at = piece * LANES
            out_ref[tap, :, at : at + LANES] = x_ref[tap * whole + piece] * scale
        rest = x_ref[9 * whole + tap // 2] * scale
        if tap % 2:
            rest = pltpu.roll(rest, half, 1)
        out_ref[tap, :, whole * LANES :] = rest[:, :half]


def call(
    kernel, outs, scratch, flops, smem=(), vmem=(), load=(), hbm=(), grant=VMEM_BYTES, aliases=None, size=None
):
    args = [*smem, *vmem, *load, *hbm]
    counts = [len(smem) + len(vmem), len(load), len(hbm) + len(outs) + len(scratch)]
    specs = [pl.BlockSpec(memory_space=pltpu.SMEM)] * len(smem)
    specs += [pl.BlockSpec(memory_space=pltpu.VMEM)] * len(vmem)
    specs += [pl.BlockSpec(memory_space=pltpu.HBM)] * (len(load) + len(hbm))
    shapes = [jax.ShapeDtypeStruct(out[0], out[1]) for out in outs]
    out_specs = [pl.BlockSpec(memory_space=out[2] if len(out) > 2 else pltpu.VMEM) for out in outs]
    if size is None:
        size = sum(a.size * a.dtype.itemsize for a in [*args, *shapes])
    buffers = [s if not isinstance(s, tuple) else pltpu.VMEM(*s) for s in scratch]
    buffers += [pltpu.VMEM(x.shape, x.dtype) for x in load]
    buffers += [pltpu.SemaphoreType.DMA((len(load),))] if load else []

    def body(*refs):
        first, wanted, rest = counts[0], counts[1], counts[2]
        sources = refs[first : first + wanted]
        middle = refs[first + wanted : first + wanted + rest]
        held = refs[first + wanted + rest : first + wanted + rest + wanted]
        copies = start_copies(list(zip(sources, held)), refs[-1]) if wanted else []
        kernel(functools.partial(wait_copies, copies), *refs[:first], *held, *middle)

    return pl.pallas_call(
        body,
        out_shape=shapes,
        in_specs=specs,
        out_specs=out_specs,
        scratch_shapes=buffers,
        input_output_aliases=aliases or {},
        compiler_params=pltpu.CompilerParams(vmem_limit_bytes=grant),
        cost_estimate=pl.CostEstimate(flops=flops, bytes_accessed=size, transcendentals=0),
    )(*args)


F16 = jnp.float16


def bit_of(axis, bit):
    return (lax.axis_index(axis) // bit) % 2


def side(which, count=1):
    unsigned = jnp.uint32
    return (which * count).astype(unsigned), ((1 - which) * count).astype(unsigned), which == 0


def part_of(value, start, count, dim):
    starts = [start if i == dim else jnp.uint32(0) for i in range(value.ndim)]
    sizes = [count if i == dim else size for i, size in enumerate(value.shape)]
    return lax.dynamic_slice(value, starts, sizes)


def half_of_dim(value, start, dim):
    return part_of(value, start, value.shape[dim] // 2, dim)


def half_sum(value, mine, send, dim):
    arrived = send(half_of_dim(value, mine[1], dim).astype(F16))
    return half_of_dim(value, mine[0], dim) + arrived.astype(value.dtype)


def both_halves(value, mine, send, dim):
    other = send(value)
    low = jnp.where(mine[2], value, other)
    high = jnp.where(mine[2], other, value)
    return jnp.concatenate([low, high], axis=dim)


def joint_sum(value, sides, dims, sends):
    def quarter(flips):
        part = value
        for mine, dim, flip in zip(sides, dims, flips):
            part = half_of_dim(part, mine[1 if flip else 0], dim)
        return part

    total = quarter((0, 0))
    arrived = [send(quarter(flips).astype(F16)) for flips, send in sends]
    for part in arrived:
        total = total + part.astype(value.dtype)
    return total


def joint_gather(value, sides, dims, sends):
    parts = {(0, 0): value}
    for flips, send in sends:
        parts[flips] = send(value)

    def order(first, second, mine, dim):
        low = jnp.where(mine[2], first, second)
        high = jnp.where(mine[2], second, first)
        return jnp.concatenate([low, high], axis=dim)

    rows = [order(parts[(0, flip)], parts[(1, flip)], sides[0], dims[0]) for flip in (0, 1)]
    return order(rows[0], rows[1], sides[1], dims[1])


FLIPS = ((1, 0), (0, 1), (1, 1))


def reduce_weights(kept, arrived, latent, sweeps, travel, land, sides):
    slabs, tiles, share_rows, lanes = kept.shape
    shape = (slabs, 2, tiles // 2, 2, 2, share_rows // 4, lanes)
    pieces = (kept.reshape(shape), arrived.reshape(shape))
    tall, wide = lax.axis_size("sy"), lax.axis_size("sx")

    def turned(sy, sx, turn):
        return (sy, sx ^ 2) if sx % 2 == turn else (sy ^ 1, sx)

    def send_tile(turn, flip_turn, flip_far):
        pairs = []
        for i in range(tall * wide):
            sy, sx = divmod(i, wide)
            to = turned(sy, sx, turn) if flip_turn else (sy, sx)
            to = (to[0] ^ 2, to[1]) if flip_far else to
            pairs.append((i, to[0] * wide + to[1]))
        return lambda value: lax.ppermute(value, ("sy", "sx"), pairs)

    def send_slab(bit, flip_slab, flip_far):
        pairs = []
        for i in range(slabs * tall):
            tm, sy = divmod(i, tall)
            pairs.append((i, (tm ^ (bit * flip_slab)) * tall + (sy ^ (2 * flip_far))))
        return lambda value: lax.ppermute(value, ("tm", "sy"), pairs)

    first, second, far, core, *slab_sides = sides

    def half(which):
        return sum(half_of_dim(x, which, 1) for x in pieces)

    outgoing, latent = lax.optimization_barrier((half(first[1]).astype(F16), latent))
    other = send_tile(0, 1, 0)(outgoing)
    other, (base, leaving) = lax.optimization_barrier((other, sweeps[0]((latent,))))
    value = half(first[0]) + other.astype(F32)
    landing = travel(leaving)
    outgoing = half_of_dim(value, second[1], 3).astype(F16)
    outgoing, latent, base = lax.optimization_barrier((outgoing, latent, base))
    other = send_tile(1, 1, 0)(outgoing)
    other, (base, leaving), landing = lax.optimization_barrier((other, sweeps[1]((latent, base)), landing))
    value = half_of_dim(value, second[0], 3) + other.astype(F32)
    bits = axis_bits(("tm",))[::-1]
    for (_, bit), mine in zip(bits[:-1], slab_sides):
        value = half_sum(value, mine, lambda x, bit=bit: swap(x, "tm", bit), 0)
    if bits:
        sends = [(flips, send_slab(bits[-1][1], *flips)) for flips in FLIPS]
        value = joint_sum(value, (slab_sides[-1], far), (0, 4), sends)
    else:
        value = half_sum(value, far, lambda x: swap(x, "sy", 2), 4)
    value = value.astype(F16)
    trajectory = land(landing, base, 0)
    landing = travel(leaving)
    sends = [(flips, send_tile(1, flips[1], flips[0])) for flips in FLIPS]
    value = joint_gather(value, (far, second), (4, 3), sends)
    value, landing, trajectory = lax.optimization_barrier((value, landing, trajectory))
    trajectory = land(landing, trajectory, 1)
    value = both_halves(value, first, send_tile(0, 1, 0), 1)
    value, trajectory = lax.optimization_barrier((value, trajectory))
    value = both_halves(value[None], core, lambda x: swap(x, "sx", 1), 0)
    return value.astype(F32).reshape(2 * tiles, share_rows, lanes), trajectory


def shards(
    latent_init, step_noise, coef_state, coef_drift, coef_noise, step_index, time_table, norm_gain,
    conv_weight, reward_grad,
):
    tile_rows, cols, channels = latent_init.shape
    group = channels // GROUPS
    lanes = -(-channels // LANES) * LANES
    extra = lanes - channels
    slabs = lax.axis_size("tm")
    steps_here = step_noise.shape[0]
    steps = steps_here * slabs
    rows = tile_rows // slabs
    span = steps * cols
    tm, sy, sx = (lax.axis_index(axis) for axis in ("tm", "sy", "sx"))
    half = half_of(tm, sy)
    conv_flops = 2 * 9 * rows * span * channels * channels
    cells = tile_rows * lax.axis_size("sy") * cols * lax.axis_size("sx")
    targets = [half_of((tm + offset) % slabs, sy) for offset in range(1, slabs)]
    tall, wide = lax.axis_size("sy"), lax.axis_size("sx")
    diagonal = [(sy + dy, sx + dx) for dy in (-1, 1) for dx in (-1, 1)]
    corners = [jnp.clip(y, 0, tall - 1) * wide + jnp.clip(x, 0, wide - 1) for y, x in diagonal]
    origins = [half_of((tm - offset + slabs) % slabs, sy) for offset in range(1, slabs)]
    place = [half, sx % 2, tm, jnp.int32(rows)] + corners + targets + origins
    place = jnp.stack(place).astype(jnp.int32)
    flags = [(sy > 0) | (half > 0), (sy < tall - 1) | (half < slabs - 1), sx > 0, sx < wide - 1]
    flags += [(y >= 0) & (y < tall) & (x >= 0) & (x < wide) for y, x in diagonal]
    flags = jnp.stack(flags).astype(F32)
    turns = [bit_of("sx", 2), bit_of("sy", 1)]
    core = bit_of("sx", 1)
    halves = [
        side(jnp.where(core == 0, turns[0], turns[1])),
        side(jnp.where(core == 0, turns[1], turns[0])),
        side(bit_of("sy", 2)),
        side(core),
    ]
    held = slabs
    for _, bit in axis_bits(("tm",))[::-1]:
        held //= 2
        halves.append(side(bit_of("tm", bit), held))
    cut = rows // 2
    place, flags, halves, latent_init = lax.optimization_barrier((place, flags, halves, latent_init))

    def shifted(offset):
        return [(i, (i + offset) % slabs) for i in range(slabs)]

    tiles_axes = ("sy", "sx")
    tile_devices = lax.axis_size(tiles_axes)
    sent_shape = (slabs - 1, steps_here, rows, cols, channels)
    end_shape, col_shape = ((2, cols, channels), F32), ((2, tile_rows, channels), F32)
    part_rows = CORNERS + 8 * (lanes // LANES)
    moments, table, low_rows, high_rows, first_cols, last_cols, leaving = call(
        functools.partial(start_kernel, group),
        [((tile_devices, part_rows, LANES), F32), ((4, steps_here, lanes), F32)]
        + [end_shape, end_shape, col_shape, col_shape, (sent_shape, BF16)],
        [pltpu.SemaphoreType.DMA((slabs - 1,))],
        10**6,
        smem=[step_index, place, coef_state, coef_drift, coef_noise],
        load=[latent_init, reward_grad, time_table.T, norm_gain],
        hbm=[step_noise],
        grant=WHOLE_BYTES,
    )

    def to_slabs(pieces):
        if slabs == 2:
            return lax.ppermute(pieces, "tm", shifted(1))
        return jnp.stack([lax.ppermute(pieces[i], "tm", shifted(i + 1)) for i in range(slabs - 1)])

    down, up = chain("sy")
    right_way, left_way = chain("sx")
    parts1, low_rows, high_rows, first_cols, last_cols, conv_weight = lax.optimization_barrier(
        (share(moments, tiles_axes), low_rows, high_rows, first_cols, last_cols, conv_weight)
    )
    low = lax.ppermute(low_rows, "sy", down)
    high = lax.ppermute(high_rows, "sy", up)
    left = lax.ppermute(last_cols, "sx", right_way)
    right = lax.ppermute(first_cols, "sx", left_way)
    other_tables = to_slabs(jnp.broadcast_to(table[None], (slabs - 1,) + table.shape))
    other_tables, leaving = lax.optimization_barrier((other_tables, leaving))
    others = to_slabs(leaving)
    (coefs,) = call(
        table_kernel, [((4, steps, lanes), F32)], [], 10**5, smem=[place], vmem=[table, other_tables],
        grant=SMALL_BYTES,
    )
    packed = ((9 * (lanes - LANES) + 5 * LANES, lanes), BF16)
    weight_out, weight_back = call(
        pack_weight_kernel, [packed, packed], [], 10**7, load=[conv_weight.reshape(9, channels, channels)],
    )

    even_shape = (rows + 2, (cols + 2) * steps, lanes)
    odd_shape = (rows + 2, span, lanes)
    field_shape = (rows, span, lanes)
    y_shape = (lanes // LANES, chunk_rows(rows, span) * span, LANES)
    row_shape = (lanes // LANES, span, LANES)
    noise_shape = (steps_here, rows, cols, channels)
    even_out, odd_out, field_out = (even_shape, BF16), (odd_shape, BF16), (field_shape, F32)
    edge_row, edge_col = ((1, span, lanes), F32), ((rows, steps, lanes), F32)
    noise_scratch = [(noise_shape, BF16)]
    even1, odd1, sides, first_row, last_row = call(
        functools.partial(edge_sweep_kernel, group, cells),
        [even_out, odd_out, ((2, 2, tile_rows + 2, lanes), F32), edge_row, edge_row],
        noise_scratch + [(row_shape, F32), (row_shape, F32), pltpu.SemaphoreType.DMA((1,))],
        conv_flops // 4,
        smem=[flags, place],
        vmem=[low, high, left, right, parts1, coefs, latent_init, others, weight_out],
        hbm=[step_noise],
    )
    down_rows, up_rows = row_chain()
    top = lax.ppermute(last_row, ("tm", "sy"), down_rows)
    bottom = lax.ppermute(first_row, ("tm", "sy"), up_rows)
    states, moments, first_col, last_col = call(
        functools.partial(inner_sweep_kernel, group),
        [field_out, ((2, steps, LANES), F32), edge_col, edge_col],
        noise_scratch + [(y_shape, F32), (row_shape, F32), pltpu.SemaphoreType.DMA((1,))],
        conv_flops,
        smem=[place],
        vmem=[first_row, last_row, even1, odd1, coefs, latent_init, others, weight_out],
        hbm=[step_noise],
    )

    def side_cols(args):
        top, bottom, first, last = args
        side_out = ((rows + 2, steps, lanes), F32)
        first, last = call(
            edge_kernel, [side_out, side_out], [], 10**5, vmem=[top, bottom, first, last], grant=SMALL_BYTES
        )
        return lax.ppermute(last, "sx", right_way), lax.ppermute(first, "sx", left_way)

    def act_gradient(first, count):
        def run(reward):
            (out,) = call(
                functools.partial(act_gradient_kernel, first),
                [((count, span, lanes), F32)],
                [((count + 2,) + even_shape[1:], BF16), ((count + 2,) + odd_shape[1:], BF16)],
                conv_flops // 4,
                smem=[place],
                vmem=[reward, low, high, sides, coefs, weight_back],
            )
            return out

        return run

    order = ("sx", "sy", "tm")
    quarter = max(1, rows // 4)
    pieces = [(at, min(quarter, rows - at)) for at in range(0, rows, quarter)]

    def cols_and_first(args):
        return side_cols(args[1:]), act_gradient(*pieces[0])(args[0])

    def d_act_work(piece):
        return lambda done: (act_gradient(*piece), reward_grad)

    moments2, (((left2, right2), d_first), *d_rest) = butterfly(
        moments,
        order,
        join_moments(float(rows * cols * group)),
        [lambda done: (cols_and_first, (reward_grad, top, bottom, first_col, last_col))]
        + [d_act_work(piece) for piece in pieces[1:]],
    )
    even2, odd2, d_norm, sums, norm = call(
        functools.partial(norm_gradient_kernel, group, cells),
        [even_out, odd_out, field_out, ((steps, LANES), F32), ((2, steps, lanes), F32)],
        [],
        40 * rows * span * lanes,
        smem=[flags, place],
        vmem=[moments2, top, bottom, left2, right2, coefs, reward_grad, states, d_first, *d_rest],
    )

    share_rows = channels // slabs
    tiles = 9 * (channels // LANES) + 6

    def late_weight(half):
        def run(reward):
            (out,) = call(
                functools.partial(late_weight_kernel, half),
                [((tiles // 2, channels, LANES), F32)],
                [],
                conv_flops // 2,
                smem=[place],
                vmem=[reward, coefs, even2, odd2],
            )
            return out

        return lambda done: (run, reward_grad)

    def second_sweep(first, count):
        out_shape = (slabs, steps_here, count, cols, channels)

        def run(args):
            base = list(args[1:])
            return call(
                functools.partial(second_sweep_kernel, first),
                [(step_noise.shape, F32, pltpu.HBM), ((slabs - 1,) + out_shape[1:], F32)],
                [(noise_shape, BF16), (y_shape, F32), (row_shape, F32), (out_shape, F32)]
                + [pltpu.SemaphoreType.DMA((1,)), pltpu.SemaphoreType.DMA((1,))],
                conv_flops // 2,
                smem=[place],
                vmem=[coefs, args[0], states, others, weight_out, even2, odd2],
                hbm=[step_noise] + base,
                aliases={9: 0} if base else None,
            )

        return run

    sums, (late_a, late_b) = butterfly(
        sums,
        order,
        join_sums,
        [late_weight(0), late_weight(1)],
    )

    payload = ((slabs, tiles // 2, share_rows, LANES), F32)
    up_shape = ((channels, rows * span), BF16)
    sent, scales, up_t = call(
        functools.partial(sent_weight_kernel, group, cells),
        [payload, ((16, LANES), F32), up_shape],
        [(row_shape, F32), (row_shape, F32), ((rows * span, lanes), BF16)],
        conv_flops // 2,
        smem=[place],
        vmem=[states, norm, sums, coefs, d_norm, reward_grad, even1, odd1, late_a, late_b],
        size=10**6,
    )

    def kept_weight(args):
        (kept,) = call(
            kept_weight_kernel,
            [payload],
            [],
            conv_flops // 2,
            smem=[place],
            vmem=[args[0], coefs, scales, even1, odd1, late_a, late_b],
        )
        return kept

    arrived, kept = beside(sent, "sx", 1, kept_weight, (up_t,))

    def land(part, trajectory, which):
        (trajectory,) = call(
            functools.partial(land_kernel, (0, cut)[which]),
            [(step_noise.shape, F32, pltpu.HBM)],
            [(part.shape, F32), pltpu.SemaphoreType.DMA((slabs - 1,))],
            10**6,
            smem=[place],
            vmem=[latent_init, part.astype(F32)],
            hbm=[trajectory],
            aliases={3: 0},
        )
        return trajectory

    summed, trajectory = reduce_weights(
        kept,
        arrived,
        latent_init,
        (second_sweep(0, cut), second_sweep(cut, rows - cut)),
        lambda leaving: to_slabs(leaving.astype(F16)),
        land,
        halves,
    )
    (grad,) = call(
        unpack_kernel, [((9, share_rows, channels), F32)], [], 10**6, vmem=[summed, scales],
        grant=SMALL_BYTES,
    )
    return trajectory, grad.transpose(0, 2, 1).reshape(3, 3, channels, share_rows)


def solution(mesh):
    placed = (
        P("sy", "sx", None),
        P("tm", "sy", "sx", None),
        P("tm"),
        P("tm"),
        P("tm"),
        P("tm"),
        P(),
        P(),
        P(),
        P("sy", "sx", None),
    )
    return jax.shard_map(
        shards,
        mesh=mesh,
        in_specs=placed,
        out_specs=(P("tm", "sy", "sx", None), P(None, None, None, "tm")),
        check_vma=False,
    )
```

```python
import functools

import jax
import jax.numpy as jnp
from jax import lax
from jax.experimental import pallas as pl
from jax.experimental.pallas import tpu as pltpu
from jax.sharding import PartitionSpec as P

GROUPS = 32
EPSILON = 1e-05
LANES = 128
F32 = jnp.float32
BF16 = jnp.bfloat16
VMEM_BYTES = 16 * 1024 * 1024
SMALL_BYTES = 4 * 1024 * 1024
WHOLE_BYTES = 61 * 10**6


def axis_bits(axes):
    bits = []
    for axis in axes:
        step = 1
        while step < lax.axis_size(axis):
            bits.append((axis, step))
            step *= 2
    return bits


def swap(value, axis, bit):
    pairs = [(i, i ^ bit) for i in range(lax.axis_size(axis))]
    return lax.ppermute(value, axis, pairs)


def half_of(tm_index, sy_index):
    last = lax.axis_size("tm") - 1
    return jnp.where(sy_index % 2 == 0, tm_index, last - tm_index)


def share(copies, axes):
    return lax.all_to_all(copies, axes, 0, 0)


def beside(value, axis, bit, work, needs):
    value, needs = lax.optimization_barrier((value, needs))
    other = swap(value, axis, bit)
    return lax.optimization_barrier((other, work(needs)))


def butterfly(value, axes, join, works):
    results = []
    for i, (axis, bit) in enumerate(axis_bits(axes)):
        if i < len(works):
            other, result = beside(value, axis, bit, *works[i](results))
            results.append(result)
        else:
            other = swap(value, axis, bit)
        value = join(value, other, 2**i)
    return value, results


def join_moments(count):
    def join(mine, other, size):
        gap = mine[0] - other[0]
        mean = 0.5 * (mine[0] + other[0])
        return jnp.stack([mean, mine[1] + other[1] + gap * gap * (0.5 * count * size)])

    return join


def join_sums(mine, other, size):
    return mine + other


def chain(axis):
    count = lax.axis_size(axis)
    forward = [(i, i + 1) for i in range(count - 1)]
    return forward, [(b, a) for a, b in forward]


def row_chain():
    slabs, tiles = lax.axis_size("tm"), lax.axis_size("sy")
    order = []
    for sy in range(tiles):
        for half in range(slabs):
            tm = half if sy % 2 == 0 else slabs - 1 - half
            order.append(tm * tiles + sy)
    forward = list(zip(order[:-1], order[1:]))
    return forward, [(b, a) for a, b in forward]


def group_matrix(rows, cols, group, channel_dim, slot):
    channel = lax.broadcasted_iota(jnp.int32, (rows, cols), channel_dim)
    place = lax.broadcasted_iota(jnp.int32, (rows, cols), 1 - channel_dim)
    scale = (1 << 16) // group + 1
    same = ((channel * scale) >> 16) + slot * GROUPS == place
    return (same & (channel < GROUPS * group)).astype(F32)


def exact_dot(left, right):
    return jnp.dot(left, right, precision=lax.Precision.HIGHEST, preferred_element_type=F32)


def gather_groups(values, group, slot):
    return exact_dot(values, group_matrix(values.shape[1], LANES, group, 0, slot))


def spread_groups(values, lanes, group):
    return exact_dot(values, group_matrix(LANES, lanes, group, 1, 0))


def lane_slot(values, slot):
    if slot:
        values = pltpu.roll(values, LANES - slot * GROUPS, 1)
    lane = lax.broadcasted_iota(jnp.int32, values.shape, 1)
    return jnp.where(lane < GROUPS, values, 0.0)


def merged_moments(parts, total_count, lanes, group):
    devices = parts.shape[0]
    total = jnp.sum(parts, axis=0)
    center = lane_slot(total, 0) * (1.0 / devices)
    gap = parts - center[None]
    between = lane_slot(jnp.sum(gap * gap, axis=0), 0) * (total_count / devices)
    spread = (between + lane_slot(total, 1)) * (1.0 / total_count)
    inv = lane_slot(1.0 / jnp.sqrt(spread + EPSILON), 0)
    return spread_groups(center, lanes, group), spread_groups(inv, lanes, group)


def final_moments(moments_ref, count, lanes, group):
    center = lane_slot(moments_ref[0], 0)
    inv = lane_slot(1.0 / jnp.sqrt(moments_ref[1] * (1.0 / count) + EPSILON), 0)
    return spread_groups(center, lanes, group), spread_groups(inv, lanes, group)


def start_copies(pairs, sem):
    copies = [pltpu.make_async_copy(a, b, sem.at[i]) for i, (a, b) in enumerate(pairs)]
    for copy in copies:
        copy.start()
    return copies


def wait_copies(copies):
    for copy in copies:
        copy.wait()


def widen(x, lanes):
    return jnp.concatenate([x, jnp.zeros((x.shape[0], lanes - x.shape[1]), x.dtype)], axis=1)


def framed_row(tile_ref, low_ref, high_ref, sides_ref, part, half, rows, row, lanes):
    tall = tile_ref.shape[0]
    place = half * rows + row - 1
    inner = tile_ref[jnp.clip(place, 0, tall - 1)]
    inner = jnp.where(place < 0, low_ref[part], jnp.where(place >= tall, high_ref[part], inner))
    left = sides_ref[0, part, pl.ds(place + 1, 1), :]
    right = sides_ref[1, part, pl.ds(place + 1, 1), :]
    return jnp.concatenate([left, widen(inner, lanes), right], axis=0)


def noise_of(own_ref, others_ref, place_ref, k, row, lanes):
    steps_here = own_ref.shape[0]
    slabs = others_ref.shape[0] + 1
    slab, step = divmod(k, steps_here)
    offset = lax.rem(place_ref[2] - slab + slabs, slabs)
    mine = own_ref[step, row].astype(F32)
    other = others_ref[jnp.maximum(offset - 1, 0), step, row].astype(F32)
    return widen(jnp.where(offset == 0, mine, other), lanes)


CORNERS = 8


def start_kernel(
    group, ready, index_ref, place_ref, state_ref, drift_ref, noise_coef_ref, lat_ref, reward_ref,
    time_ref, gain_ref, noise_hbm, part_ref, table_ref, low_ref, high_ref, first_ref, last_ref, sent_ref, sem,
):
    others, steps, rows = sent_ref.shape[:3]
    copies = start_copies(
        [
            (noise_hbm.at[:, pl.ds(place_ref[8 + i] * rows, rows)], sent_ref.at[i])
            for i in range(others)
        ],
        sem,
    )
    ready()
    tall, wide, channels = lat_ref.shape
    lanes = table_ref.shape[2]
    corners = []
    for part, ref in enumerate((lat_ref, reward_ref)):
        low_ref[part] = ref[tall - 1]
        high_ref[part] = ref[0]
        for row in range(tall):
            first_ref[part, row : row + 1] = ref[row, 0:1]
            last_ref[part, row : row + 1] = ref[row, wide - 1 : wide]
    for row in (0, tall - 1):
        for col in (0, wide - 1):
            for ref in (lat_ref, reward_ref):
                cell = widen(ref[row, col : col + 1], lanes)
                corners += [cell[:, at : at + LANES] for at in range(0, lanes, LANES)]
    entries = time_ref.shape[1]
    which = lax.broadcasted_iota(jnp.int32, (entries, LANES), 0)
    line = lax.broadcasted_iota(jnp.int32, (entries, LANES), 1)
    hit = jnp.zeros((entries, LANES), F32)
    for k in range(steps):
        hit = jnp.where((line == k) & (which == index_ref[k]), 1.0, hit)
    embedded = jnp.transpose(exact_dot(time_ref[...], hit))[:8]
    modulate = widen(gain_ref[...][None, :] * (1.0 + embedded), lanes)
    table_ref[0] = modulate[:steps]
    for k in range(steps):
        for i, ref in enumerate((state_ref, drift_ref, noise_coef_ref)):
            table_ref[i + 1, k : k + 1] = jnp.full((1, lanes), ref[k], F32)
    x = lat_ref[...].reshape(tall * wide, channels)
    sums = jnp.broadcast_to(jnp.sum(x, axis=0, keepdims=True), (8, channels))
    mean = gather_groups(sums, group, 0) * (1.0 / (tall * wide * group))
    gap = x - spread_groups(mean, channels, group)[0:1]
    square = jnp.broadcast_to(jnp.sum(gap * gap, axis=0, keepdims=True), (8, channels))
    part = jnp.concatenate([mean + gather_groups(square, group, 1)] + corners, axis=0)
    part_ref[...] = jnp.broadcast_to(part[None], part_ref.shape)
    wait_copies(copies)


def edge_kernel(ready, top_ref, bottom_ref, first_ref, last_ref, first_out, last_out):
    rows, steps, _ = first_ref.shape
    span = top_ref.shape[1]
    for out, ref, at in ((first_out, first_ref, 0), (last_out, last_ref, span - steps)):
        out[0] = top_ref[0, at : at + steps]
        out[1 : rows + 1] = ref[...]
        out[rows + 1] = bottom_ref[0, at : at + steps]


def join_tables(place_ref, own_ref, others_ref, out_ref):
    slabs = others_ref.shape[0] + 1
    kinds, steps, _ = own_ref.shape
    for offset in range(slabs):
        source = lax.rem(place_ref[2] - offset + slabs, slabs)
        for kind in range(kinds):
            rows = own_ref[kind] if offset == 0 else others_ref[offset - 1, kind]
            for k in range(steps):
                out_ref[kind, pl.ds(source * steps + k, 1), :] = rows[k : k + 1]


def packed_rows(taps, channels):
    whole = channels // LANES * LANES
    places = []
    for tap in range(taps):
        rest = taps * whole + tap // 2 * LANES + tap % 2 * (LANES // 2)
        places.append((tap * whole, rest))
    return whole, places


def pack_weights(w_ref, out_ref, back_ref):
    taps, channels, _ = w_ref.shape
    lanes = out_ref.shape[1]
    whole, places = packed_rows(taps, channels)
    out_ref[...] = jnp.zeros(out_ref.shape, BF16)
    back_ref[...] = jnp.zeros(back_ref.shape, BF16)
    for tap, (at, rest) in enumerate(places):
        for ref, value in ((out_ref, w_ref[tap]), (back_ref, jnp.transpose(w_ref[taps - 1 - tap]))):
            ref[at : at + whole, 0:channels] = value[:whole]
            ref[rest : rest + channels - whole, 0:channels] = value[whole:]


def half_turn(x):
    return pltpu.roll(x.astype(F32), LANES // 2, 1).astype(BF16)


def pair_rests(rests):
    pairs = []
    for i in range(0, len(rests), 2):
        pairs.append(rests[i] if i + 1 == len(rests) else rests[i] + half_turn(rests[i + 1]))
    return pairs


def convolve_rows(even_ref, odd_ref, w_ref, start, count, steps):
    span, lanes = odd_ref.shape[1:]
    parts = []
    for row_off in range(3):
        rows = pl.ds(start + row_off, count)
        parts.append(even_ref[rows, 0:span, :].reshape(count * span, lanes))
        parts.append(odd_ref[rows].reshape(count * span, lanes))
        parts.append(even_ref[rows, 2 * steps : 2 * steps + span, :].reshape(count * span, lanes))
    whole = lanes - LANES
    packed = [x[:, :whole] for x in parts] + pair_rests([x[:, whole:] for x in parts])
    return jnp.dot(jnp.concatenate(packed, axis=1), w_ref[...], preferred_element_type=F32)


def put_tiles(ref, value):
    for tile in range(ref.shape[0]):
        ref[tile] = value[:, tile * LANES : (tile + 1) * LANES]


def get_tiles(ref):
    return jnp.concatenate([ref[tile] for tile in range(ref.shape[0])], axis=1)


def get_step(ref, start, cols, steps):
    where = pl.ds(start, cols, stride=steps)
    return jnp.concatenate([ref[tile, where, :] for tile in range(ref.shape[0])], axis=1)


def put_step(ref, start, cols, steps, value):
    where = pl.ds(start, cols, stride=steps)
    for tile in range(ref.shape[0]):
        ref[tile, where, :] = value[:, tile * LANES : (tile + 1) * LANES]


def chunk_rows(rows, span):
    count = max(1, min(rows, 384 // span))
    while rows % count:
        count -= 1
    return count


def advance_row(row, at, half, rows, steps, lat_ref, noise, place_ref, coef_ref, y_ref, row_ref):
    lanes = row_ref.shape[0] * LANES
    cols = row_ref.shape[1] // steps
    own = widen(lat_ref[half * rows + row], lanes)
    run = jnp.zeros_like(own)
    for k in range(steps):
        put_step(row_ref, k, cols, steps, own + run)
        conv = get_step(y_ref, at + k, cols, steps)
        run = run + (
            coef_ref[1, k : k + 1] * own
            + coef_ref[2, k : k + 1] * (own + conv)
            + coef_ref[3, k : k + 1] * noise_of(*noise, place_ref, k, row, lanes)
        )
    return get_tiles(row_ref)


def edge_sweep_kernel(
    group, total_cells, ready, flag_ref, place_ref, low_ref, high_ref, left_ref, right_ref,
    parts_ref, table_ref, tables_ref, lat_ref, others_ref, noise_hbm, w_hbm,
    even_ref, odd_ref, sides_ref, first_row, last_row, coef_ref, w_ref, back_ref,
    noise_ref, y_ref, row_ref, raw_ref, sem,
):
    rows, span, lanes = odd_ref.shape
    rows = rows - 2
    steps = coef_ref.shape[1]
    cols = span // steps
    half = place_ref[0]
    tall = lat_ref.shape[0]
    own_noise = noise_hbm.at[:, pl.ds(half * rows, rows)]
    loads = start_copies([(own_noise, noise_ref), (w_hbm, raw_ref)], sem)
    join_tables(place_ref, table_ref, tables_ref, coef_ref)
    center, inv = merged_moments(parts_ref[:, :CORNERS], float(total_cells * group), lanes, group)
    center, inv = center[0:1], inv[0:1]
    pieces = lanes // LANES
    for side, ref in enumerate((left_ref, right_ref)):
        for part in range(2):
            sides_ref[side, part, 1 : tall + 1, :] = widen(ref[part], lanes)
            for end in range(2):
                at = CORNERS + ((3 - 2 * end - side) * 2 + part) * pieces
                device = place_ref[4 + 2 * end + side]
                cell = [parts_ref[device, at + i : at + i + 1, :] for i in range(pieces)]
                cell = jnp.concatenate(cell, axis=1) * flag_ref[4 + 2 * end + side]
                to = end * (tall + 1)
                sides_ref[side, part, to : to + 1, :] = cell
    ready()
    mod = coef_ref[0]

    def activate(row, _):
        field = framed_row(lat_ref, low_ref, high_ref, sides_ref, 0, half, rows, row, lanes)
        normal = (field - center) * inv
        pre = normal[:, None, :] * mod[None]
        act = pre / (1.0 + jnp.exp(-pre))
        keep = jnp.where(row == 0, flag_ref[0], jnp.where(row == rows + 1, flag_ref[1], 1.0))
        act = act * keep
        inner = act[1 : cols + 1]
        act = jnp.concatenate(
            [act[0:1] * flag_ref[2], inner, act[cols + 1 : cols + 2] * flag_ref[3]], axis=0
        )
        even_ref[row] = act.reshape((cols + 2) * steps, lanes).astype(BF16)
        odd_ref[row] = inner.reshape(span, lanes).astype(BF16)
        return 0

    lax.fori_loop(0, rows + 2, activate, 0)
    wait_copies(loads)
    pack_weights(raw_ref, w_ref, back_ref)
    for row, out in ((0, first_row), (rows - 1, last_row)):
        put_tiles(y_ref, convolve_rows(even_ref, odd_ref, w_ref, row, 1, steps))
        noise = (noise_ref, others_ref)
        out[0] = advance_row(row, 0, half, rows, steps, lat_ref, noise, place_ref, coef_ref, y_ref, row_ref)


def inner_sweep_kernel(
    group, ready, place_ref, first_row, last_row, even_ref, odd_ref, coef_ref, lat_ref, others_ref, w_ref,
    noise_hbm, states_ref, moment_ref, first_col, last_col, noise_ref, y_ref, row_ref, sem,
):
    rows, span, lanes = states_ref.shape
    steps = coef_ref.shape[1]
    cols = span // steps
    half = place_ref[0]
    own_noise = noise_hbm.at[:, pl.ds(half * rows, rows)]
    loads = start_copies([(own_noise, noise_ref)], sem)
    states_ref[0] = first_row[0]
    states_ref[rows - 1] = last_row[0]
    wait_copies(loads)
    count = chunk_rows(max(rows - 2, 1), span)

    def sweep(chunk, _):
        start = 1 + chunk * count
        put_tiles(y_ref, convolve_rows(even_ref, odd_ref, w_ref, start, count, steps))
        for inner in range(count):
            states_ref[start + inner] = advance_row(
                start + inner, inner * span, half, rows, steps, lat_ref, (noise_ref, others_ref),
                place_ref, coef_ref, y_ref, row_ref,
            )
        return 0

    lax.fori_loop(0, (rows - 2) // count, sweep, 0)
    zero = jnp.zeros((steps, lanes), F32)

    def add(row, total):
        return total + jnp.sum(states_ref[row].reshape(cols, steps, lanes), axis=0)

    mean = gather_groups(lax.fori_loop(0, rows, add, zero), group, 0) * (1.0 / (rows * cols * group))
    mean_here = spread_groups(mean, lanes, group)

    def squares(row, total):
        gap = states_ref[row].reshape(cols, steps, lanes) - mean_here[None]
        return total + jnp.sum(gap * gap, axis=0)

    moment_ref[0] = mean
    moment_ref[1] = gather_groups(lax.fori_loop(0, rows, squares, zero), group, 0)
    first_col[...] = states_ref[:, 0:steps]
    last_col[...] = states_ref[:, span - steps :]


def act_gradient_kernel(
    first, ready, place_ref, reward_ref, low_ref, high_ref, sides_ref, coef_ref, w_ref,
    out_ref, even_ref, odd_ref,
):
    rows, span, lanes = out_ref.shape
    steps = coef_ref.shape[1]
    cols = span // steps
    drift = coef_ref[2]

    def scale(row, _):
        field = framed_row(
            reward_ref, low_ref, high_ref, sides_ref, 1, place_ref[0], place_ref[3], row + first, lanes
        )
        up = field[:, None, :] * drift[None]
        even_ref[row] = up.reshape((cols + 2) * steps, lanes).astype(BF16)
        odd_ref[row] = up[1 : cols + 1].reshape(span, lanes).astype(BF16)
        return 0

    lax.fori_loop(0, rows + 2, scale, 0)
    count = chunk_rows(rows, span)

    def sweep(chunk, _):
        start = chunk * count
        out = convolve_rows(even_ref, odd_ref, w_ref, start, count, steps)
        out_ref[pl.ds(start, count)] = out.reshape(count, span, lanes)
        return 0

    lax.fori_loop(0, rows // count, sweep, 0)


def norm_gradient_kernel(
    group, total_cells, ready, flag_ref, place_ref, moments_ref, top_ref, bottom_ref, left_ref, right_ref,
    coef_ref, reward_ref, states_ref, *refs
):
    *d_act_refs, even_ref, odd_ref, d_norm_ref, sum_ref, norm_ref = refs
    rows, span, lanes = states_ref.shape
    steps = coef_ref.shape[1]
    cols = span // steps
    center, inv = final_moments(moments_ref, float(total_cells * group), lanes, group)
    norm_ref[0] = center
    norm_ref[1] = inv
    mod = coef_ref[0]

    def activate(at, inner, keep):
        field = jnp.concatenate(
            [left_ref[at][None], inner.reshape(cols, steps, lanes), right_ref[at][None]], axis=0
        )
        normal = (field - center[None]) * inv[None]
        pre = normal * mod[None]
        sig = 1.0 / (1.0 + jnp.exp(-pre))
        act = pre * sig
        if keep is not None:
            act = act * keep
        middle = act[1 : cols + 1]
        odd_ref[at] = middle.reshape(span, lanes).astype(BF16)
        act = jnp.concatenate(
            [act[0:1] * flag_ref[2], middle, act[cols + 1 : cols + 2] * flag_ref[3]], axis=0
        )
        even_ref[at] = act.reshape((cols + 2) * steps, lanes).astype(BF16)
        return [x[1 : cols + 1] for x in (normal, pre, sig)]

    activate(0, top_ref[0], flag_ref[0])
    activate(rows + 1, bottom_ref[0], flag_ref[1])

    def one(d_act_ref, first, index, sums):
        plain, cross, square = sums
        row = index + first
        normal, pre, sig = activate(row + 1, states_ref[row], None)
        slope = sig * (1.0 + pre * (1.0 - sig))
        d_norm = d_act_ref[index].reshape(cols, steps, lanes) * slope * mod[None]
        d_norm_ref[row] = d_norm.reshape(span, lanes)
        return (
            plain + jnp.sum(d_norm, axis=0),
            cross + jnp.sum(d_norm * normal, axis=0),
            square + jnp.sum(d_norm * d_norm, axis=0),
        )

    zero = jnp.zeros((steps, lanes), F32)
    sums = (zero, zero, zero)
    first = 0
    for d_act_ref in d_act_refs:
        count = d_act_ref.shape[0]
        sums = lax.fori_loop(0, count, functools.partial(one, d_act_ref, first), sums)
        first += count
    plain, cross, square = sums
    channels = reward_ref.shape[2]
    reward = reward_ref[pl.ds(place_ref[0] * rows, rows)].reshape(rows * cols, channels)
    reward = jnp.broadcast_to(jnp.sum(reward * reward, axis=0, keepdims=True), (steps, channels))
    sum_ref[...] = (
        gather_groups(plain, group, 0)
        + gather_groups(cross, group, 1)
        + gather_groups(square, group, 2)
        + gather_groups(reward, group, 3)
    )


def second_sweep_kernel(
    first, ready, place_ref, coef_ref, lat_ref, states_ref, others_ref, w_ref, even_ref, odd_ref, noise_hbm, *refs
):
    kept_hbm, sent_ref, noise_ref, y_ref, row_ref, out_ref, sem, out_sem = refs[-8:]
    all_rows, span, lanes = states_ref.shape
    slabs, steps_here, rows, cols, channels = out_ref.shape
    steps = slabs * steps_here
    half = place_ref[0]
    own_noise = noise_hbm.at[:, pl.ds(half * all_rows, all_rows)]
    wait_copies(start_copies([(own_noise, noise_ref)], sem))
    count = chunk_rows(rows, span)

    def sweep(chunk, _):
        start = chunk * count
        put_tiles(y_ref, convolve_rows(even_ref, odd_ref, w_ref, first + start, count, steps))
        for inner in range(count):
            row = first + start + inner
            own = widen(lat_ref[half * all_rows + row], lanes)
            put_tiles(row_ref, states_ref[row])
            run = jnp.zeros_like(own)
            for k in range(steps):
                conv = get_step(y_ref, inner * span + k, cols, steps)
                state = get_step(row_ref, k, cols, steps)
                run = run + (
                    coef_ref[1, k : k + 1] * state
                    + coef_ref[2, k : k + 1] * (state + conv)
                    + coef_ref[3, k : k + 1] * noise_of(noise_ref, others_ref, place_ref, k, row, lanes)
                )
                out_ref[k // steps_here, k % steps_here, start + inner] = run[:, :channels]
        return 0

    lax.fori_loop(0, rows // count, sweep, 0)
    for offset in range(1, slabs):
        sent_ref[offset - 1] = out_ref[lax.rem(place_ref[2] + offset, slabs)] * 0.125
    mine = place_ref[2]

    def complete(row, _):
        own = lat_ref[half * all_rows + first + row]
        for k in range(steps_here):
            out_ref[mine, k, row] = own + out_ref[mine, k, row]
        return 0

    lax.fori_loop(0, rows, complete, 0)
    pairs = [(out_ref.at[mine], kept_hbm.at[:, pl.ds(half * all_rows + first, rows)])]
    wait_copies(start_copies(pairs, out_sem))


def land_kernel(first, ready, place_ref, lat_ref, part_ref, base_hbm, out_hbm, hold_ref, sem):
    others, steps, count = part_ref.shape[:3]
    copies = []
    for i in range(others):
        at = place_ref[8 + others + i] * place_ref[3] + first

        def add(row, _):
            own = lat_ref[at + row]
            for k in range(steps):
                hold_ref[i, k, row] = own + 8.0 * part_ref[i, k, row]
            return 0

        lax.fori_loop(0, count, add, 0)
        copies.append(pltpu.make_async_copy(hold_ref.at[i], out_hbm.at[:, pl.ds(at, count)], sem.at[i]))
        copies[-1].start()
    wait_copies(copies)


def weight_terms(half, up_t, even_ref, odd_ref, steps, put):
    rows = odd_ref.shape[0] - 2
    span, lanes = odd_ref.shape[1:]
    whole = lanes - LANES

    def window(tap, first, last):
        row_off, col_off = divmod(tap, 3)
        if col_off == 1:
            part = odd_ref[row_off : row_off + rows, :, first:last]
        else:
            at = col_off * steps
            part = even_ref[row_off : row_off + rows, at : at + span, first:last]
        return part.reshape(rows * span, last - first)

    def emit(tile, part):
        term = jnp.dot(up_t, part, preferred_element_type=F32)
        for piece in range(part.shape[1] // LANES):
            put(tile + piece, term[:, piece * LANES : (piece + 1) * LANES])

    for i, tap in enumerate(range(6, 9) if half else range(0, 6)):
        emit(i * whole // LANES, window(tap, 0, whole))
    if half:
        rests = pair_rests([window(tap, whole, lanes) for tap in range(9)])
        emit(3 * whole // LANES, jnp.concatenate(rests, axis=1))
        put(3 * whole // LANES + 5, jnp.zeros((up_t.shape[0], LANES), F32))


def late_weight_kernel(half, ready, place_ref, reward_ref, coef_ref, even_ref, odd_ref, out_ref):
    rows, span, lanes = odd_ref.shape
    rows = rows - 2
    steps = coef_ref.shape[1]
    cols = span // steps
    channels = out_ref.shape[1]
    reward = reward_ref[pl.ds(place_ref[0] * rows, rows)].reshape(rows * cols, channels)
    up = widen(reward, lanes)[:, None, :] * coef_ref[2][None]
    up = up.reshape(rows * span, lanes).astype(BF16)

    def put(tile, value):
        out_ref[tile] = value

    weight_terms(half, jnp.transpose(up)[:channels], even_ref, odd_ref, steps, put)


def safe_scale(total, norm, mod, state_coef, drift_coef, cells, group):
    def whole(slot):
        return jnp.sqrt(jnp.sum(lane_slot(total, slot), axis=1, keepdims=True))

    gradient, reward = whole(2), whole(3)
    top_inv = jnp.max(norm, axis=1, keepdims=True)
    top_mod = jnp.max(jnp.abs(mod), axis=1, keepdims=True)
    state, drift = jnp.abs(state_coef[:, 0:1]), jnp.abs(drift_coef[:, 0:1])
    through = jnp.sum((state + drift) * reward + top_inv * gradient, axis=0, keepdims=True)
    field = top_mod * drift * (float(cells * group) ** 0.5)
    bound = jnp.sum(field * (reward + through), axis=0, keepdims=True) * 1.1
    power = jnp.clip(jnp.floor(jnp.log2(32768.0 / jnp.maximum(bound, 1e-30))), -60.0, 60.0)
    scale = jnp.ones_like(power)
    for bit in (32, 16, 8, 4, 2, 1):
        size = jnp.abs(power)
        has = jnp.floor(size / bit) - 2.0 * jnp.floor(size / (2 * bit)) > 0.5
        step = jnp.where(power > 0, 2.0**bit, 2.0**-bit)
        scale = jnp.where(has, scale * step, scale)
    return scale


def half_gradient(half, up_t, late_ref, scale, even_ref, odd_ref, steps, out_ref):
    slabs, _, share_rows, _ = out_ref.shape

    def put(tile, value):
        value = (value + late_ref[tile]) * scale
        for slab in range(slabs):
            out_ref[slab, tile] = value[slab * share_rows : (slab + 1) * share_rows]

    weight_terms(half, up_t, even_ref, odd_ref, steps, put)


def kept_weight_kernel(
    ready, place_ref, up_ref, coef_ref, scale_ref, even_ref, odd_ref, late_a_ref, late_b_ref, out_ref
):
    for half, late_ref in enumerate((late_a_ref, late_b_ref)):

        @pl.when(place_ref[1] == half)
        def _():
            scale, steps = scale_ref[0:1], coef_ref.shape[1]
            half_gradient(half, up_ref[...], late_ref, scale, even_ref, odd_ref, steps, out_ref)


def sent_weight_kernel(
    group, cells, ready, place_ref, states_ref, norm_ref, sums_ref, coef_ref,
    d_norm_ref, reward_ref, even_ref, odd_ref, late_a_ref, late_b_ref,
    out_ref, scale_ref, up_t_ref, d_ref, adj_ref, up_ref,
):
    rows, span, lanes = states_ref.shape
    steps = coef_ref.shape[1]
    cols = span // steps
    center, inv = norm_ref[0], norm_ref[1]
    total = sums_ref[...]
    count = 1.0 / (cells * group)
    plain = spread_groups(lane_slot(total, 0) * count, lanes, group)
    cross = spread_groups(lane_slot(total, 1) * count, lanes, group)
    scale = safe_scale(total, inv, coef_ref[0], coef_ref[1], coef_ref[2], cells, group)
    scale_ref[0:8] = jnp.broadcast_to(scale, (8, LANES))
    scale_ref[8:16] = jnp.broadcast_to(1.0 / scale, (8, LANES))

    def one(row, _):
        normal = (states_ref[row].reshape(cols, steps, lanes) - center[None]) * inv[None]
        d_norm = d_norm_ref[row].reshape(cols, steps, lanes)
        d_group = (d_norm - plain[None] - normal * cross[None]) * inv[None]
        put_tiles(d_ref, d_group.reshape(span, lanes))
        reward = widen(reward_ref[place_ref[0] * rows + row], lanes)
        run = jnp.zeros_like(reward)
        for k in range(steps - 1, -1, -1):
            drift = coef_ref[2, k : k + 1]
            put_step(adj_ref, k, cols, steps, drift * run)
            d_state = drift * reward + get_step(d_ref, k, cols, steps)
            run = run + (coef_ref[1, k : k + 1] * reward + d_state)
        up_ref[pl.ds(pl.multiple_of(row * span, 16), span), :] = get_tiles(adj_ref).astype(BF16)
        return 0

    lax.fori_loop(0, rows, one, 0)
    up_t_ref[...] = jnp.transpose(up_ref[...])[: up_t_ref.shape[0]]
    for half, late_ref in enumerate((late_a_ref, late_b_ref)):

        @pl.when(place_ref[1] != half)
        def _():
            half_gradient(half, up_t_ref[...], late_ref, scale, even_ref, odd_ref, steps, out_ref)


def unpack_kernel(ready, x_ref, scale_ref, out_ref):
    ready()
    whole = out_ref.shape[2] // LANES
    half = LANES // 2
    scale = scale_ref[8:9]
    for tap in range(9):
        for piece in range(whole):
            at = piece * LANES
            out_ref[tap, :, at : at + LANES] = x_ref[tap * whole + piece] * scale
        rest = x_ref[9 * whole + tap // 2] * scale
        if tap % 2:
            rest = pltpu.roll(rest, half, 1)
        out_ref[tap, :, whole * LANES :] = rest[:, :half]


def call(
    kernel, outs, scratch, flops, smem=(), vmem=(), load=(), hbm=(), grant=VMEM_BYTES, aliases=None, size=None
):
    args = [*smem, *vmem, *load, *hbm]
    counts = [len(smem) + len(vmem), len(load), len(hbm) + len(outs) + len(scratch)]
    specs = [pl.BlockSpec(memory_space=pltpu.SMEM)] * len(smem)
    specs += [pl.BlockSpec(memory_space=pltpu.VMEM)] * len(vmem)
    specs += [pl.BlockSpec(memory_space=pltpu.HBM)] * (len(load) + len(hbm))
    shapes = [jax.ShapeDtypeStruct(out[0], out[1]) for out in outs]
    out_specs = [pl.BlockSpec(memory_space=out[2] if len(out) > 2 else pltpu.VMEM) for out in outs]
    if size is None:
        size = sum(a.size * a.dtype.itemsize for a in [*args, *shapes])
    buffers = [s if not isinstance(s, tuple) else pltpu.VMEM(*s) for s in scratch]
    buffers += [pltpu.VMEM(x.shape, x.dtype) for x in load]
    buffers += [pltpu.SemaphoreType.DMA((len(load),))] if load else []

    def body(*refs):
        first, wanted, rest = counts[0], counts[1], counts[2]
        sources = refs[first : first + wanted]
        middle = refs[first + wanted : first + wanted + rest]
        held = refs[first + wanted + rest : first + wanted + rest + wanted]
        copies = start_copies(list(zip(sources, held)), refs[-1]) if wanted else []
        kernel(functools.partial(wait_copies, copies), *refs[:first], *held, *middle)

    return pl.pallas_call(
        body,
        out_shape=shapes,
        in_specs=specs,
        out_specs=out_specs,
        scratch_shapes=buffers,
        input_output_aliases=aliases or {},
        compiler_params=pltpu.CompilerParams(vmem_limit_bytes=grant),
        cost_estimate=pl.CostEstimate(flops=flops, bytes_accessed=size, transcendentals=0),
    )(*args)


F16 = jnp.float16


def bit_of(axis, bit):
    return (lax.axis_index(axis) // bit) % 2


def side(which, count=1):
    unsigned = jnp.uint32
    return (which * count).astype(unsigned), ((1 - which) * count).astype(unsigned), which == 0


def part_of(value, start, count, dim):
    starts = [start if i == dim else jnp.uint32(0) for i in range(value.ndim)]
    sizes = [count if i == dim else size for i, size in enumerate(value.shape)]
    return lax.dynamic_slice(value, starts, sizes)


def half_of_dim(value, start, dim):
    return part_of(value, start, value.shape[dim] // 2, dim)


def half_sum(value, mine, send, dim):
    arrived = send(half_of_dim(value, mine[1], dim).astype(F16))
    return half_of_dim(value, mine[0], dim) + arrived.astype(value.dtype)


def both_halves(value, mine, send, dim):
    other = send(value)
    low = jnp.where(mine[2], value, other)
    high = jnp.where(mine[2], other, value)
    return jnp.concatenate([low, high], axis=dim)


def joint_sum(value, sides, dims, sends):
    def quarter(flips):
        part = value
        for mine, dim, flip in zip(sides, dims, flips):
            part = half_of_dim(part, mine[1 if flip else 0], dim)
        return part

    total = quarter((0, 0))
    arrived = [send(quarter(flips).astype(F16)) for flips, send in sends]
    for part in arrived:
        total = total + part.astype(value.dtype)
    return total


def joint_gather(value, sides, dims, sends):
    parts = {(0, 0): value}
    for flips, send in sends:
        parts[flips] = send(value)

    def order(first, second, mine, dim):
        low = jnp.where(mine[2], first, second)
        high = jnp.where(mine[2], second, first)
        return jnp.concatenate([low, high], axis=dim)

    rows = [order(parts[(0, flip)], parts[(1, flip)], sides[0], dims[0]) for flip in (0, 1)]
    return order(rows[0], rows[1], sides[1], dims[1])


FLIPS = ((1, 0), (0, 1), (1, 1))


def reduce_weights(kept, arrived, needs, sweep, travel, land, landing, sides):
    slabs, tiles, share_rows, lanes = kept.shape
    shape = (slabs, 2, tiles // 2, 2, 2, share_rows // 4, lanes)
    pieces = (kept.reshape(shape), arrived.reshape(shape))
    tall, wide = lax.axis_size("sy"), lax.axis_size("sx")

    def turned(sy, sx, turn):
        return (sy, sx ^ 2) if sx % 2 == turn else (sy ^ 1, sx)

    def send_tile(turn, flip_turn, flip_far):
        pairs = []
        for i in range(tall * wide):
            sy, sx = divmod(i, wide)
            to = turned(sy, sx, turn) if flip_turn else (sy, sx)
            to = (to[0] ^ 2, to[1]) if flip_far else to
            pairs.append((i, to[0] * wide + to[1]))
        return lambda value: lax.ppermute(value, ("sy", "sx"), pairs)

    def send_slab(bit, flip_slab, flip_far):
        pairs = []
        for i in range(slabs * tall):
            tm, sy = divmod(i, tall)
            pairs.append((i, (tm ^ (bit * flip_slab)) * tall + (sy ^ (2 * flip_far))))
        return lambda value: lax.ppermute(value, ("tm", "sy"), pairs)

    first, second, far, core, *slab_sides = sides

    def half(which):
        return sum(half_of_dim(x, which, 1) for x in pieces)

    outgoing, needs = lax.optimization_barrier((half(first[1]).astype(F16), needs))
    other = send_tile(0, 1, 0)(outgoing)
    other, (trajectory, leaving) = lax.optimization_barrier((other, sweep(needs)))
    value = half(first[0]) + other.astype(F32)
    trajectory = land(landing, trajectory, 0)
    landing = travel(leaving)
    value = half_sum(value, second, send_tile(1, 1, 0), 3)
    value, landing, trajectory = lax.optimization_barrier((value, landing, trajectory))
    bits = axis_bits(("tm",))[::-1]
    for (_, bit), mine in zip(bits[:-1], slab_sides):
        value = half_sum(value, mine, lambda x, bit=bit: swap(x, "tm", bit), 0)
    if bits:
        sends = [(flips, send_slab(bits[-1][1], *flips)) for flips in FLIPS]
        value = joint_sum(value, (slab_sides[-1], far), (0, 4), sends)
    else:
        value = half_sum(value, far, lambda x: swap(x, "sy", 2), 4)
    value = value.astype(F16)
    sends = [(flips, send_tile(1, flips[1], flips[0])) for flips in FLIPS]
    value = joint_gather(value, (far, second), (4, 3), sends)
    value = both_halves(value, first, send_tile(0, 1, 0), 1)
    value, trajectory = lax.optimization_barrier((value, land(landing, trajectory, 1)))
    value = both_halves(value[None], core, lambda x: swap(x, "sx", 1), 0)
    return value.astype(F32).reshape(2 * tiles, share_rows, lanes), trajectory


def shards(
    latent_init, step_noise, coef_state, coef_drift, coef_noise, step_index, time_table, norm_gain,
    conv_weight, reward_grad,
):
    tile_rows, cols, channels = latent_init.shape
    group = channels // GROUPS
    lanes = -(-channels // LANES) * LANES
    extra = lanes - channels
    slabs = lax.axis_size("tm")
    steps_here = step_noise.shape[0]
    steps = steps_here * slabs
    rows = tile_rows // slabs
    span = steps * cols
    tm, sy, sx = (lax.axis_index(axis) for axis in ("tm", "sy", "sx"))
    half = half_of(tm, sy)
    conv_flops = 2 * 9 * rows * span * channels * channels
    cells = tile_rows * lax.axis_size("sy") * cols * lax.axis_size("sx")
    targets = [half_of((tm + offset) % slabs, sy) for offset in range(1, slabs)]
    tall, wide = lax.axis_size("sy"), lax.axis_size("sx")
    diagonal = [(sy + dy, sx + dx) for dy in (-1, 1) for dx in (-1, 1)]
    corners = [jnp.clip(y, 0, tall - 1) * wide + jnp.clip(x, 0, wide - 1) for y, x in diagonal]
    origins = [half_of((tm - offset + slabs) % slabs, sy) for offset in range(1, slabs)]
    place = [half, sx % 2, tm, jnp.int32(rows)] + corners + targets + origins
    place = jnp.stack(place).astype(jnp.int32)
    flags = [(sy > 0) | (half > 0), (sy < tall - 1) | (half < slabs - 1), sx > 0, sx < wide - 1]
    flags += [(y >= 0) & (y < tall) & (x >= 0) & (x < wide) for y, x in diagonal]
    flags = jnp.stack(flags).astype(F32)
    turns = [bit_of("sx", 2), bit_of("sy", 1)]
    core = bit_of("sx", 1)
    halves = [
        side(jnp.where(core == 0, turns[0], turns[1])),
        side(jnp.where(core == 0, turns[1], turns[0])),
        side(bit_of("sy", 2)),
        side(core),
    ]
    held = slabs
    for _, bit in axis_bits(("tm",))[::-1]:
        held //= 2
        halves.append(side(bit_of("tm", bit), held))
    cut = rows // 2
    place, flags, halves, latent_init = lax.optimization_barrier((place, flags, halves, latent_init))

    def shifted(offset):
        return [(i, (i + offset) % slabs) for i in range(slabs)]

    tiles_axes = ("sy", "sx")
    tile_devices = lax.axis_size(tiles_axes)
    sent_shape = (slabs - 1, steps_here, rows, cols, channels)
    end_shape, col_shape = ((2, cols, channels), F32), ((2, tile_rows, channels), F32)
    part_rows = CORNERS + 8 * (lanes // LANES)
    moments, table, low_rows, high_rows, first_cols, last_cols, leaving = call(
        functools.partial(start_kernel, group),
        [((tile_devices, part_rows, LANES), F32), ((4, steps_here, lanes), F32)]
        + [end_shape, end_shape, col_shape, col_shape, (sent_shape, BF16)],
        [pltpu.SemaphoreType.DMA((slabs - 1,))],
        10**6,
        smem=[step_index, place, coef_state, coef_drift, coef_noise],
        load=[latent_init, reward_grad, time_table.T, norm_gain],
        hbm=[step_noise],
        grant=WHOLE_BYTES,
    )

    def to_slabs(pieces):
        if slabs == 2:
            return lax.ppermute(pieces, "tm", shifted(1))
        return jnp.stack([lax.ppermute(pieces[i], "tm", shifted(i + 1)) for i in range(slabs - 1)])

    down, up = chain("sy")
    right_way, left_way = chain("sx")
    low = lax.ppermute(low_rows, "sy", down)
    high = lax.ppermute(high_rows, "sy", up)
    left = lax.ppermute(last_cols, "sx", right_way)
    right = lax.ppermute(first_cols, "sx", left_way)
    other_tables = to_slabs(jnp.broadcast_to(table[None], (slabs - 1,) + table.shape))
    other_tables, leaving = lax.optimization_barrier((other_tables, leaving))
    others = to_slabs(leaving)
    parts1 = share(moments, tiles_axes)
    packed = ((9 * (lanes - LANES) + 5 * LANES, lanes), BF16)

    even_shape = (rows + 2, (cols + 2) * steps, lanes)
    odd_shape = (rows + 2, span, lanes)
    field_shape = (rows, span, lanes)
    y_shape = (lanes // LANES, chunk_rows(rows, span) * span, LANES)
    row_shape = (lanes // LANES, span, LANES)
    noise_shape = (steps_here, rows, cols, channels)
    even_out, odd_out, field_out = (even_shape, BF16), (odd_shape, BF16), (field_shape, F32)
    edge_row, edge_col = ((1, span, lanes), F32), ((rows, steps, lanes), F32)
    noise_scratch = [(noise_shape, BF16)]
    even1, odd1, sides, first_row, last_row, coefs, weight_out, weight_back = call(
        functools.partial(edge_sweep_kernel, group, cells),
        [even_out, odd_out, ((2, 2, tile_rows + 2, lanes), F32), edge_row, edge_row]
        + [((4, steps, lanes), F32), packed, packed],
        noise_scratch + [(row_shape, F32), (row_shape, F32), ((9, channels, channels), BF16)]
        + [pltpu.SemaphoreType.DMA((2,))],
        conv_flops // 4,
        smem=[flags, place],
        vmem=[low, high, left, right, parts1, table, other_tables, latent_init, others],
        hbm=[step_noise, conv_weight.reshape(9, channels, channels)],
    )
    down_rows, up_rows = row_chain()
    top = lax.ppermute(last_row, ("tm", "sy"), down_rows)
    bottom = lax.ppermute(first_row, ("tm", "sy"), up_rows)
    states, moments, first_col, last_col = call(
        functools.partial(inner_sweep_kernel, group),
        [field_out, ((2, steps, LANES), F32), edge_col, edge_col],
        noise_scratch + [(y_shape, F32), (row_shape, F32), pltpu.SemaphoreType.DMA((1,))],
        conv_flops,
        smem=[place],
        vmem=[first_row, last_row, even1, odd1, coefs, latent_init, others, weight_out],
        hbm=[step_noise],
    )

    def side_cols(args):
        top, bottom, first, last = args
        side_out = ((rows + 2, steps, lanes), F32)
        first, last = call(
            edge_kernel, [side_out, side_out], [], 10**5, vmem=[top, bottom, first, last], grant=SMALL_BYTES
        )
        return lax.ppermute(last, "sx", right_way), lax.ppermute(first, "sx", left_way)

    def act_gradient(first, count):
        def run(reward):
            (out,) = call(
                functools.partial(act_gradient_kernel, first),
                [((count, span, lanes), F32)],
                [((count + 2,) + even_shape[1:], BF16), ((count + 2,) + odd_shape[1:], BF16)],
                conv_flops // 4,
                smem=[place],
                vmem=[reward, low, high, sides, coefs, weight_back],
            )
            return out

        return run

    order = ("sx", "sy", "tm")
    quarter = max(1, rows // 4)
    pieces = [(at, min(quarter, rows - at)) for at in range(0, rows, quarter)]

    def cols_and_first(args):
        return side_cols(args[1:]), act_gradient(*pieces[0])(args[0])

    def d_act_work(piece):
        return lambda done: (act_gradient(*piece), reward_grad)

    moments2, (((left2, right2), d_first), *d_rest) = butterfly(
        moments,
        order,
        join_moments(float(rows * cols * group)),
        [lambda done: (cols_and_first, (reward_grad, top, bottom, first_col, last_col))]
        + [d_act_work(piece) for piece in pieces[1:]],
    )
    even2, odd2, d_norm, sums, norm = call(
        functools.partial(norm_gradient_kernel, group, cells),
        [even_out, odd_out, field_out, ((steps, LANES), F32), ((2, steps, lanes), F32)],
        [],
        40 * rows * span * lanes,
        smem=[flags, place],
        vmem=[moments2, top, bottom, left2, right2, coefs, reward_grad, states, d_first, *d_rest],
    )

    share_rows = channels // slabs
    tiles = 9 * (channels // LANES) + 6

    def late_weight(half):
        def run(reward):
            (out,) = call(
                functools.partial(late_weight_kernel, half),
                [((tiles // 2, channels, LANES), F32)],
                [],
                conv_flops // 2,
                smem=[place],
                vmem=[reward, coefs, even2, odd2],
            )
            return out

        return lambda done: (run, reward_grad)

    def second_sweep(first, count):
        out_shape = (slabs, steps_here, count, cols, channels)

        def run(args):
            base = list(args[1:])
            return call(
                functools.partial(second_sweep_kernel, first),
                [(step_noise.shape, F32, pltpu.HBM), ((slabs - 1,) + out_shape[1:], F32)],
                [(noise_shape, BF16), (y_shape, F32), (row_shape, F32), (out_shape, F32)]
                + [pltpu.SemaphoreType.DMA((1,)), pltpu.SemaphoreType.DMA((1,))],
                conv_flops // 2,
                smem=[place],
                vmem=[coefs, args[0], states, others, weight_out, even2, odd2],
                hbm=[step_noise] + base,
                aliases={9: 0} if base else None,
            )

        return run

    sums, (late_a, late_b, (base, leaving)) = butterfly(
        sums,
        ("tm", "sx", "sy"),
        join_sums,
        [
            late_weight(0),
            late_weight(1),
            lambda done: (second_sweep(0, cut), (latent_init,)),
        ],
    )
    landing = to_slabs(leaving.astype(F16))

    payload = ((slabs, tiles // 2, share_rows, LANES), F32)
    up_shape = ((channels, rows * span), BF16)
    sent, scales, up_t = call(
        functools.partial(sent_weight_kernel, group, cells),
        [payload, ((16, LANES), F32), up_shape],
        [(row_shape, F32), (row_shape, F32), ((rows * span, lanes), BF16)],
        conv_flops // 2,
        smem=[place],
        vmem=[states, norm, sums, coefs, d_norm, reward_grad, even1, odd1, late_a, late_b],
        size=10**6,
    )

    def kept_weight(args):
        (kept,) = call(
            kept_weight_kernel,
            [payload],
            [],
            conv_flops // 2,
            smem=[place],
            vmem=[args[0], coefs, scales, even1, odd1, late_a, late_b],
        )
        return kept

    sent, landing = lax.optimization_barrier((sent, landing))
    arrived, kept = beside(sent, "sx", 1, kept_weight, (up_t,))

    def land(part, trajectory, which):
        (trajectory,) = call(
            functools.partial(land_kernel, (0, cut)[which]),
            [(step_noise.shape, F32, pltpu.HBM)],
            [(part.shape, F32), pltpu.SemaphoreType.DMA((slabs - 1,))],
            10**6,
            smem=[place],
            vmem=[latent_init, part.astype(F32)],
            hbm=[trajectory],
            aliases={3: 0},
        )
        return trajectory

    summed, trajectory = reduce_weights(
        kept,
        arrived,
        (latent_init, base),
        second_sweep(cut, rows - cut),
        lambda leaving: to_slabs(leaving.astype(F16)),
        land,
        landing,
        halves,
    )
    (grad,) = call(
        unpack_kernel, [((9, share_rows, channels), F32)], [], 10**6, vmem=[summed, scales],
        grant=SMALL_BYTES,
    )
    return trajectory, grad.transpose(0, 2, 1).reshape(3, 3, channels, share_rows)


def solution(mesh):
    placed = (
        P("sy", "sx", None),
        P("tm", "sy", "sx", None),
        P("tm"),
        P("tm"),
        P("tm"),
        P("tm"),
        P(),
        P(),
        P(),
        P("sy", "sx", None),
    )
    return jax.shard_map(
        shards,
        mesh=mesh,
        in_specs=placed,
        out_specs=(P("tm", "sy", "sx", None), P(None, None, None, "tm")),
        check_vma=False,
    )
```

```python
import functools

import jax
import jax.numpy as jnp
from jax import lax
from jax.experimental import pallas as pl
from jax.experimental.pallas import tpu as pltpu
from jax.sharding import PartitionSpec as P

GROUPS = 32
EPSILON = 1e-05
LANES = 128
F32 = jnp.float32
BF16 = jnp.bfloat16
VMEM_BYTES = 16 * 1024 * 1024
SMALL_BYTES = 4 * 1024 * 1024
WHOLE_BYTES = 61 * 10**6


def axis_bits(axes):
    bits = []
    for axis in axes:
        step = 1
        while step < lax.axis_size(axis):
            bits.append((axis, step))
            step *= 2
    return bits


def swap(value, axis, bit):
    pairs = [(i, i ^ bit) for i in range(lax.axis_size(axis))]
    return lax.ppermute(value, axis, pairs)


def half_of(tm_index, sy_index):
    last = lax.axis_size("tm") - 1
    return jnp.where(sy_index % 2 == 0, tm_index, last - tm_index)


def share(copies, axes):
    return lax.all_to_all(copies, axes, 0, 0)


def beside(value, axis, bit, work, needs):
    value, needs = lax.optimization_barrier((value, needs))
    other = swap(value, axis, bit)
    return lax.optimization_barrier((other, work(needs)))


def butterfly(value, axes, join, works):
    results = []
    for i, (axis, bit) in enumerate(axis_bits(axes)):
        if i < len(works):
            other, result = beside(value, axis, bit, *works[i](results))
            results.append(result)
        else:
            other = swap(value, axis, bit)
        value = join(value, other, 2**i)
    return value, results


def join_moments(count):
    def join(mine, other, size):
        gap = mine[0] - other[0]
        mean = 0.5 * (mine[0] + other[0])
        return jnp.stack([mean, mine[1] + other[1] + gap * gap * (0.5 * count * size)])

    return join


def join_sums(mine, other, size):
    return mine + other


def chain(axis):
    count = lax.axis_size(axis)
    forward = [(i, i + 1) for i in range(count - 1)]
    return forward, [(b, a) for a, b in forward]


def row_chain():
    slabs, tiles = lax.axis_size("tm"), lax.axis_size("sy")
    order = []
    for sy in range(tiles):
        for half in range(slabs):
            tm = half if sy % 2 == 0 else slabs - 1 - half
            order.append(tm * tiles + sy)
    forward = list(zip(order[:-1], order[1:]))
    return forward, [(b, a) for a, b in forward]


def group_matrix(rows, cols, group, channel_dim, slot):
    channel = lax.broadcasted_iota(jnp.int32, (rows, cols), channel_dim)
    place = lax.broadcasted_iota(jnp.int32, (rows, cols), 1 - channel_dim)
    scale = (1 << 16) // group + 1
    same = ((channel * scale) >> 16) + slot * GROUPS == place
    return (same & (channel < GROUPS * group)).astype(F32)


def exact_dot(left, right):
    return jnp.dot(left, right, precision=lax.Precision.HIGHEST, preferred_element_type=F32)


def gather_groups(values, group, slot):
    return exact_dot(values, group_matrix(values.shape[1], LANES, group, 0, slot))


def spread_groups(values, lanes, group):
    return exact_dot(values, group_matrix(LANES, lanes, group, 1, 0))


def lane_slot(values, slot):
    if slot:
        values = pltpu.roll(values, LANES - slot * GROUPS, 1)
    lane = lax.broadcasted_iota(jnp.int32, values.shape, 1)
    return jnp.where(lane < GROUPS, values, 0.0)


def merged_moments(parts, total_count, lanes, group):
    devices = parts.shape[0]
    total = jnp.sum(parts, axis=0)
    center = lane_slot(total, 0) * (1.0 / devices)
    gap = parts - center[None]
    between = lane_slot(jnp.sum(gap * gap, axis=0), 0) * (total_count / devices)
    spread = (between + lane_slot(total, 1)) * (1.0 / total_count)
    inv = lane_slot(1.0 / jnp.sqrt(spread + EPSILON), 0)
    return spread_groups(center, lanes, group), spread_groups(inv, lanes, group)


def final_moments(moments_ref, count, lanes, group):
    center = lane_slot(moments_ref[0], 0)
    inv = lane_slot(1.0 / jnp.sqrt(moments_ref[1] * (1.0 / count) + EPSILON), 0)
    return spread_groups(center, lanes, group), spread_groups(inv, lanes, group)


def start_copies(pairs, sem):
    copies = [pltpu.make_async_copy(a, b, sem.at[i]) for i, (a, b) in enumerate(pairs)]
    for copy in copies:
        copy.start()
    return copies


def wait_copies(copies):
    for copy in copies:
        copy.wait()


def widen(x, lanes):
    return jnp.concatenate([x, jnp.zeros((x.shape[0], lanes - x.shape[1]), x.dtype)], axis=1)


def framed_row(tile_ref, low_ref, high_ref, sides_ref, part, half, rows, row, lanes):
    tall = tile_ref.shape[0]
    place = half * rows + row - 1
    inner = tile_ref[jnp.clip(place, 0, tall - 1)]
    inner = jnp.where(place < 0, low_ref[part], jnp.where(place >= tall, high_ref[part], inner))
    left = sides_ref[0, part, pl.ds(place + 1, 1), :]
    right = sides_ref[1, part, pl.ds(place + 1, 1), :]
    return jnp.concatenate([left, widen(inner, lanes), right], axis=0)


def noise_of(own_ref, others_ref, place_ref, k, row, lanes):
    steps_here = own_ref.shape[0]
    slabs = others_ref.shape[0] + 1
    slab, step = divmod(k, steps_here)
    offset = lax.rem(place_ref[2] - slab + slabs, slabs)
    mine = own_ref[step, row].astype(F32)
    other = others_ref[jnp.maximum(offset - 1, 0), step, row].astype(F32)
    return widen(jnp.where(offset == 0, mine, other), lanes)


CORNERS = 8


def start_kernel(
    group, ready, index_ref, place_ref, state_ref, drift_ref, noise_coef_ref, lat_ref, reward_ref,
    time_ref, gain_ref, noise_hbm, part_ref, table_ref, low_ref, high_ref, first_ref, last_ref, sent_ref, sem,
):
    others, steps, rows = sent_ref.shape[:3]
    copies = start_copies(
        [
            (noise_hbm.at[:, pl.ds(place_ref[8 + i] * rows, rows)], sent_ref.at[i])
            for i in range(others)
        ],
        sem,
    )
    ready()
    tall, wide, channels = lat_ref.shape
    lanes = table_ref.shape[2]
    corners = []
    for part, ref in enumerate((lat_ref, reward_ref)):
        low_ref[part] = ref[tall - 1]
        high_ref[part] = ref[0]
        for row in range(tall):
            first_ref[part, row : row + 1] = ref[row, 0:1]
            last_ref[part, row : row + 1] = ref[row, wide - 1 : wide]
    for row in (0, tall - 1):
        for col in (0, wide - 1):
            for ref in (lat_ref, reward_ref):
                cell = widen(ref[row, col : col + 1], lanes)
                corners += [cell[:, at : at + LANES] for at in range(0, lanes, LANES)]
    entries = time_ref.shape[1]
    which = lax.broadcasted_iota(jnp.int32, (entries, LANES), 0)
    line = lax.broadcasted_iota(jnp.int32, (entries, LANES), 1)
    hit = jnp.zeros((entries, LANES), F32)
    for k in range(steps):
        hit = jnp.where((line == k) & (which == index_ref[k]), 1.0, hit)
    embedded = jnp.transpose(exact_dot(time_ref[...], hit))[:8]
    modulate = widen(gain_ref[...][None, :] * (1.0 + embedded), lanes)
    table_ref[0] = modulate[:steps]
    for k in range(steps):
        for i, ref in enumerate((state_ref, drift_ref, noise_coef_ref)):
            table_ref[i + 1, k : k + 1] = jnp.full((1, lanes), ref[k], F32)
    x = lat_ref[...].reshape(tall * wide, channels)
    sums = jnp.broadcast_to(jnp.sum(x, axis=0, keepdims=True), (8, channels))
    mean = gather_groups(sums, group, 0) * (1.0 / (tall * wide * group))
    gap = x - spread_groups(mean, channels, group)[0:1]
    square = jnp.broadcast_to(jnp.sum(gap * gap, axis=0, keepdims=True), (8, channels))
    part = jnp.concatenate([mean + gather_groups(square, group, 1)] + corners, axis=0)
    part_ref[...] = jnp.broadcast_to(part[None], part_ref.shape)
    wait_copies(copies)


def edge_kernel(ready, top_ref, bottom_ref, first_ref, last_ref, first_out, last_out):
    rows, steps, _ = first_ref.shape
    span = top_ref.shape[1]
    for out, ref, at in ((first_out, first_ref, 0), (last_out, last_ref, span - steps)):
        out[0] = top_ref[0, at : at + steps]
        out[1 : rows + 1] = ref[...]
        out[rows + 1] = bottom_ref[0, at : at + steps]


def table_kernel(ready, place_ref, own_ref, others_ref, out_ref):
    slabs = others_ref.shape[0] + 1
    kinds, steps, _ = own_ref.shape
    for offset in range(slabs):
        source = lax.rem(place_ref[2] - offset + slabs, slabs)
        for kind in range(kinds):
            rows = own_ref[kind] if offset == 0 else others_ref[offset - 1, kind]
            for k in range(steps):
                out_ref[kind, pl.ds(source * steps + k, 1), :] = rows[k : k + 1]


def packed_rows(taps, channels):
    whole = channels // LANES * LANES
    places = []
    for tap in range(taps):
        rest = taps * whole + tap // 2 * LANES + tap % 2 * (LANES // 2)
        places.append((tap * whole, rest))
    return whole, places


def pack_weight_kernel(ready, w_ref, out_ref, back_ref):
    taps, channels, _ = w_ref.shape
    lanes = out_ref.shape[1]
    whole, places = packed_rows(taps, channels)
    out_ref[...] = jnp.zeros(out_ref.shape, BF16)
    back_ref[...] = jnp.zeros(back_ref.shape, BF16)
    ready()
    for tap, (at, rest) in enumerate(places):
        for ref, value in ((out_ref, w_ref[tap]), (back_ref, jnp.transpose(w_ref[taps - 1 - tap]))):
            ref[at : at + whole, 0:channels] = value[:whole]
            ref[rest : rest + channels - whole, 0:channels] = value[whole:]


def half_turn(x):
    return pltpu.roll(x.astype(F32), LANES // 2, 1).astype(BF16)


def pair_rests(rests):
    pairs = []
    for i in range(0, len(rests), 2):
        pairs.append(rests[i] if i + 1 == len(rests) else rests[i] + half_turn(rests[i + 1]))
    return pairs


def convolve_rows(even_ref, odd_ref, w_ref, start, count, steps):
    span, lanes = odd_ref.shape[1:]
    parts = []
    for row_off in range(3):
        rows = pl.ds(start + row_off, count)
        parts.append(even_ref[rows, 0:span, :].reshape(count * span, lanes))
        parts.append(odd_ref[rows].reshape(count * span, lanes))
        parts.append(even_ref[rows, 2 * steps : 2 * steps + span, :].reshape(count * span, lanes))
    whole = lanes - LANES
    packed = [x[:, :whole] for x in parts] + pair_rests([x[:, whole:] for x in parts])
    return jnp.dot(jnp.concatenate(packed, axis=1), w_ref[...], preferred_element_type=F32)


def put_tiles(ref, value):
    for tile in range(ref.shape[0]):
        ref[tile] = value[:, tile * LANES : (tile + 1) * LANES]


def get_tiles(ref):
    return jnp.concatenate([ref[tile] for tile in range(ref.shape[0])], axis=1)


def get_step(ref, start, cols, steps):
    where = pl.ds(start, cols, stride=steps)
    return jnp.concatenate([ref[tile, where, :] for tile in range(ref.shape[0])], axis=1)


def put_step(ref, start, cols, steps, value):
    where = pl.ds(start, cols, stride=steps)
    for tile in range(ref.shape[0]):
        ref[tile, where, :] = value[:, tile * LANES : (tile + 1) * LANES]


def chunk_rows(rows, span):
    count = max(1, min(rows, 384 // span))
    while rows % count:
        count -= 1
    return count


def advance_row(row, at, half, rows, steps, lat_ref, noise, place_ref, coef_ref, y_ref, row_ref):
    lanes = row_ref.shape[0] * LANES
    cols = row_ref.shape[1] // steps
    own = widen(lat_ref[half * rows + row], lanes)
    run = jnp.zeros_like(own)
    for k in range(steps):
        put_step(row_ref, k, cols, steps, own + run)
        conv = get_step(y_ref, at + k, cols, steps)
        run = run + (
            coef_ref[1, k : k + 1] * own
            + coef_ref[2, k : k + 1] * (own + conv)
            + coef_ref[3, k : k + 1] * noise_of(*noise, place_ref, k, row, lanes)
        )
    return get_tiles(row_ref)


def edge_sweep_kernel(
    group, total_cells, ready, flag_ref, place_ref, low_ref, high_ref, left_ref, right_ref,
    parts_ref, coef_ref, lat_ref, others_ref, w_ref, noise_hbm,
    even_ref, odd_ref, sides_ref, first_row, last_row,
    noise_ref, y_ref, row_ref, sem,
):
    rows, span, lanes = odd_ref.shape
    rows = rows - 2
    steps = coef_ref.shape[1]
    cols = span // steps
    half = place_ref[0]
    tall = lat_ref.shape[0]
    own_noise = noise_hbm.at[:, pl.ds(half * rows, rows)]
    loads = start_copies([(own_noise, noise_ref)], sem)
    center, inv = merged_moments(parts_ref[:, :CORNERS], float(total_cells * group), lanes, group)
    center, inv = center[0:1], inv[0:1]
    pieces = lanes // LANES
    for side, ref in enumerate((left_ref, right_ref)):
        for part in range(2):
            sides_ref[side, part, 1 : tall + 1, :] = widen(ref[part], lanes)
            for end in range(2):
                at = CORNERS + ((3 - 2 * end - side) * 2 + part) * pieces
                device = place_ref[4 + 2 * end + side]
                cell = [parts_ref[device, at + i : at + i + 1, :] for i in range(pieces)]
                cell = jnp.concatenate(cell, axis=1) * flag_ref[4 + 2 * end + side]
                to = end * (tall + 1)
                sides_ref[side, part, to : to + 1, :] = cell
    ready()
    mod = coef_ref[0]

    def activate(row, _):
        field = framed_row(lat_ref, low_ref, high_ref, sides_ref, 0, half, rows, row, lanes)
        normal = (field - center) * inv
        pre = normal[:, None, :] * mod[None]
        act = pre / (1.0 + jnp.exp(-pre))
        keep = jnp.where(row == 0, flag_ref[0], jnp.where(row == rows + 1, flag_ref[1], 1.0))
        act = act * keep
        inner = act[1 : cols + 1]
        act = jnp.concatenate(
            [act[0:1] * flag_ref[2], inner, act[cols + 1 : cols + 2] * flag_ref[3]], axis=0
        )
        even_ref[row] = act.reshape((cols + 2) * steps, lanes).astype(BF16)
        odd_ref[row] = inner.reshape(span, lanes).astype(BF16)
        return 0

    lax.fori_loop(0, rows + 2, activate, 0)
    wait_copies(loads)
    for row, out in ((0, first_row), (rows - 1, last_row)):
        put_tiles(y_ref, convolve_rows(even_ref, odd_ref, w_ref, row, 1, steps))
        noise = (noise_ref, others_ref)
        out[0] = advance_row(row, 0, half, rows, steps, lat_ref, noise, place_ref, coef_ref, y_ref, row_ref)


def inner_sweep_kernel(
    group, ready, place_ref, first_row, last_row, even_ref, odd_ref, coef_ref, lat_ref, others_ref, w_ref,
    noise_hbm, states_ref, moment_ref, first_col, last_col, noise_ref, y_ref, row_ref, sem,
):
    rows, span, lanes = states_ref.shape
    steps = coef_ref.shape[1]
    cols = span // steps
    half = place_ref[0]
    own_noise = noise_hbm.at[:, pl.ds(half * rows, rows)]
    loads = start_copies([(own_noise, noise_ref)], sem)
    states_ref[0] = first_row[0]
    states_ref[rows - 1] = last_row[0]
    wait_copies(loads)
    count = chunk_rows(max(rows - 2, 1), span)

    def sweep(chunk, _):
        start = 1 + chunk * count
        put_tiles(y_ref, convolve_rows(even_ref, odd_ref, w_ref, start, count, steps))
        for inner in range(count):
            states_ref[start + inner] = advance_row(
                start + inner, inner * span, half, rows, steps, lat_ref, (noise_ref, others_ref),
                place_ref, coef_ref, y_ref, row_ref,
            )
        return 0

    lax.fori_loop(0, (rows - 2) // count, sweep, 0)
    zero = jnp.zeros((steps, lanes), F32)

    def add(row, total):
        return total + jnp.sum(states_ref[row].reshape(cols, steps, lanes), axis=0)

    mean = gather_groups(lax.fori_loop(0, rows, add, zero), group, 0) * (1.0 / (rows * cols * group))
    mean_here = spread_groups(mean, lanes, group)

    def squares(row, total):
        gap = states_ref[row].reshape(cols, steps, lanes) - mean_here[None]
        return total + jnp.sum(gap * gap, axis=0)

    moment_ref[0] = mean
    moment_ref[1] = gather_groups(lax.fori_loop(0, rows, squares, zero), group, 0)
    first_col[...] = states_ref[:, 0:steps]
    last_col[...] = states_ref[:, span - steps :]


def act_gradient_kernel(
    first, ready, place_ref, reward_ref, low_ref, high_ref, sides_ref, coef_ref, w_ref,
    out_ref, even_ref, odd_ref,
):
    rows, span, lanes = out_ref.shape
    steps = coef_ref.shape[1]
    cols = span // steps
    drift = coef_ref[2]

    def scale(row, _):
        field = framed_row(
            reward_ref, low_ref, high_ref, sides_ref, 1, place_ref[0], place_ref[3], row + first, lanes
        )
        up = field[:, None, :] * drift[None]
        even_ref[row] = up.reshape((cols + 2) * steps, lanes).astype(BF16)
        odd_ref[row] = up[1 : cols + 1].reshape(span, lanes).astype(BF16)
        return 0

    lax.fori_loop(0, rows + 2, scale, 0)
    count = chunk_rows(rows, span)

    def sweep(chunk, _):
        start = chunk * count
        out = convolve_rows(even_ref, odd_ref, w_ref, start, count, steps)
        out_ref[pl.ds(start, count)] = out.reshape(count, span, lanes)
        return 0

    lax.fori_loop(0, rows // count, sweep, 0)


def norm_gradient_kernel(
    group, total_cells, ready, flag_ref, place_ref, moments_ref, top_ref, bottom_ref, left_ref, right_ref,
    coef_ref, reward_ref, states_ref, *refs
):
    *d_act_refs, even_ref, odd_ref, d_norm_ref, sum_ref, norm_ref = refs
    rows, span, lanes = states_ref.shape
    steps = coef_ref.shape[1]
    cols = span // steps
    center, inv = final_moments(moments_ref, float(total_cells * group), lanes, group)
    norm_ref[0] = center
    norm_ref[1] = inv
    mod = coef_ref[0]

    def activate(at, inner, keep):
        field = jnp.concatenate(
            [left_ref[at][None], inner.reshape(cols, steps, lanes), right_ref[at][None]], axis=0
        )
        normal = (field - center[None]) * inv[None]
        pre = normal * mod[None]
        sig = 1.0 / (1.0 + jnp.exp(-pre))
        act = pre * sig
        if keep is not None:
            act = act * keep
        middle = act[1 : cols + 1]
        odd_ref[at] = middle.reshape(span, lanes).astype(BF16)
        act = jnp.concatenate(
            [act[0:1] * flag_ref[2], middle, act[cols + 1 : cols + 2] * flag_ref[3]], axis=0
        )
        even_ref[at] = act.reshape((cols + 2) * steps, lanes).astype(BF16)
        return [x[1 : cols + 1] for x in (normal, pre, sig)]

    activate(0, top_ref[0], flag_ref[0])
    activate(rows + 1, bottom_ref[0], flag_ref[1])

    def one(d_act_ref, first, index, sums):
        plain, cross, square = sums
        row = index + first
        normal, pre, sig = activate(row + 1, states_ref[row], None)
        slope = sig * (1.0 + pre * (1.0 - sig))
        d_norm = d_act_ref[index].reshape(cols, steps, lanes) * slope * mod[None]
        d_norm_ref[row] = d_norm.reshape(span, lanes)
        return (
            plain + jnp.sum(d_norm, axis=0),
            cross + jnp.sum(d_norm * normal, axis=0),
            square + jnp.sum(d_norm * d_norm, axis=0),
        )

    zero = jnp.zeros((steps, lanes), F32)
    sums = (zero, zero, zero)
    first = 0
    for d_act_ref in d_act_refs:
        count = d_act_ref.shape[0]
        sums = lax.fori_loop(0, count, functools.partial(one, d_act_ref, first), sums)
        first += count
    plain, cross, square = sums
    channels = reward_ref.shape[2]
    reward = reward_ref[pl.ds(place_ref[0] * rows, rows)].reshape(rows * cols, channels)
    reward = jnp.broadcast_to(jnp.sum(reward * reward, axis=0, keepdims=True), (steps, channels))
    sum_ref[...] = (
        gather_groups(plain, group, 0)
        + gather_groups(cross, group, 1)
        + gather_groups(square, group, 2)
        + gather_groups(reward, group, 3)
    )


def second_sweep_kernel(
    first, ready, place_ref, coef_ref, lat_ref, states_ref, others_ref, w_ref, even_ref, odd_ref, noise_hbm, *refs
):
    kept_hbm, sent_ref, noise_ref, y_ref, row_ref, out_ref, sem, out_sem = refs[-8:]
    all_rows, span, lanes = states_ref.shape
    slabs, steps_here, rows, cols, channels = out_ref.shape
    steps = slabs * steps_here
    half = place_ref[0]
    own_noise = noise_hbm.at[:, pl.ds(half * all_rows, all_rows)]
    wait_copies(start_copies([(own_noise, noise_ref)], sem))
    count = chunk_rows(rows, span)

    def sweep(chunk, _):
        start = chunk * count
        put_tiles(y_ref, convolve_rows(even_ref, odd_ref, w_ref, first + start, count, steps))
        for inner in range(count):
            row = first + start + inner
            own = widen(lat_ref[half * all_rows + row], lanes)
            put_tiles(row_ref, states_ref[row])
            run = jnp.zeros_like(own)
            for k in range(steps):
                conv = get_step(y_ref, inner * span + k, cols, steps)
                state = get_step(row_ref, k, cols, steps)
                run = run + (
                    coef_ref[1, k : k + 1] * state
                    + coef_ref[2, k : k + 1] * (state + conv)
                    + coef_ref[3, k : k + 1] * noise_of(noise_ref, others_ref, place_ref, k, row, lanes)
                )
                out_ref[k // steps_here, k % steps_here, start + inner] = run[:, :channels]
        return 0

    lax.fori_loop(0, rows // count, sweep, 0)
    for offset in range(1, slabs):
        sent_ref[offset - 1] = out_ref[lax.rem(place_ref[2] + offset, slabs)] * 0.125
    mine = place_ref[2]

    def complete(row, _):
        own = lat_ref[half * all_rows + first + row]
        for k in range(steps_here):
            out_ref[mine, k, row] = own + out_ref[mine, k, row]
        return 0

    lax.fori_loop(0, rows, complete, 0)
    pairs = [(out_ref.at[mine], kept_hbm.at[:, pl.ds(half * all_rows + first, rows)])]
    wait_copies(start_copies(pairs, out_sem))


def land_kernel(first, ready, place_ref, lat_ref, part_ref, base_hbm, out_hbm, hold_ref, sem):
    others, steps, count = part_ref.shape[:3]
    copies = []
    for i in range(others):
        at = place_ref[8 + others + i] * place_ref[3] + first

        def add(row, _):
            own = lat_ref[at + row]
            for k in range(steps):
                hold_ref[i, k, row] = own + 8.0 * part_ref[i, k, row]
            return 0

        lax.fori_loop(0, count, add, 0)
        copies.append(pltpu.make_async_copy(hold_ref.at[i], out_hbm.at[:, pl.ds(at, count)], sem.at[i]))
        copies[-1].start()
    wait_copies(copies)


def weight_terms(half, up_t, even_ref, odd_ref, steps, put):
    rows = odd_ref.shape[0] - 2
    span, lanes = odd_ref.shape[1:]
    whole = lanes - LANES

    def window(tap, first, last):
        row_off, col_off = divmod(tap, 3)
        if col_off == 1:
            part = odd_ref[row_off : row_off + rows, :, first:last]
        else:
            at = col_off * steps
            part = even_ref[row_off : row_off + rows, at : at + span, first:last]
        return part.reshape(rows * span, last - first)

    def emit(tile, part):
        term = jnp.dot(up_t, part, preferred_element_type=F32)
        for piece in range(part.shape[1] // LANES):
            put(tile + piece, term[:, piece * LANES : (piece + 1) * LANES])

    for i, tap in enumerate(range(6, 9) if half else range(0, 6)):
        emit(i * whole // LANES, window(tap, 0, whole))
    if half:
        rests = pair_rests([window(tap, whole, lanes) for tap in range(9)])
        emit(3 * whole // LANES, jnp.concatenate(rests, axis=1))
        put(3 * whole // LANES + 5, jnp.zeros((up_t.shape[0], LANES), F32))


def late_weight_kernel(half, ready, place_ref, reward_ref, coef_ref, even_ref, odd_ref, out_ref):
    rows, span, lanes = odd_ref.shape
    rows = rows - 2
    steps = coef_ref.shape[1]
    cols = span // steps
    channels = out_ref.shape[1]
    reward = reward_ref[pl.ds(place_ref[0] * rows, rows)].reshape(rows * cols, channels)
    up = widen(reward, lanes)[:, None, :] * coef_ref[2][None]
    up = up.reshape(rows * span, lanes).astype(BF16)

    def put(tile, value):
        out_ref[tile] = value

    weight_terms(half, jnp.transpose(up)[:channels], even_ref, odd_ref, steps, put)


def safe_scale(total, norm, mod, state_coef, drift_coef, cells, group):
    def whole(slot):
        return jnp.sqrt(jnp.sum(lane_slot(total, slot), axis=1, keepdims=True))

    gradient, reward = whole(2), whole(3)
    top_inv = jnp.max(norm, axis=1, keepdims=True)
    top_mod = jnp.max(jnp.abs(mod), axis=1, keepdims=True)
    state, drift = jnp.abs(state_coef[:, 0:1]), jnp.abs(drift_coef[:, 0:1])
    through = jnp.sum((state + drift) * reward + top_inv * gradient, axis=0, keepdims=True)
    field = top_mod * drift * (float(cells * group) ** 0.5)
    bound = jnp.sum(field * (reward + through), axis=0, keepdims=True) * 1.1
    power = jnp.clip(jnp.floor(jnp.log2(32768.0 / jnp.maximum(bound, 1e-30))), -60.0, 60.0)
    scale = jnp.ones_like(power)
    for bit in (32, 16, 8, 4, 2, 1):
        size = jnp.abs(power)
        has = jnp.floor(size / bit) - 2.0 * jnp.floor(size / (2 * bit)) > 0.5
        step = jnp.where(power > 0, 2.0**bit, 2.0**-bit)
        scale = jnp.where(has, scale * step, scale)
    return scale


def half_gradient(half, up_t, late_ref, scale, even_ref, odd_ref, steps, out_ref):
    slabs, _, share_rows, _ = out_ref.shape

    def put(tile, value):
        value = (value + late_ref[tile]) * scale
        for slab in range(slabs):
            out_ref[slab, tile] = value[slab * share_rows : (slab + 1) * share_rows]

    weight_terms(half, up_t, even_ref, odd_ref, steps, put)


def kept_weight_kernel(
    ready, place_ref, up_ref, coef_ref, scale_ref, even_ref, odd_ref, late_a_ref, late_b_ref, out_ref
):
    for half, late_ref in enumerate((late_a_ref, late_b_ref)):

        @pl.when(place_ref[1] == half)
        def _():
            scale, steps = scale_ref[0:1], coef_ref.shape[1]
            half_gradient(half, up_ref[...], late_ref, scale, even_ref, odd_ref, steps, out_ref)


def sent_weight_kernel(
    group, cells, ready, place_ref, states_ref, norm_ref, sums_ref, coef_ref,
    d_norm_ref, reward_ref, even_ref, odd_ref, late_a_ref, late_b_ref,
    out_ref, scale_ref, up_t_ref, d_ref, adj_ref, up_ref,
):
    rows, span, lanes = states_ref.shape
    steps = coef_ref.shape[1]
    cols = span // steps
    center, inv = norm_ref[0], norm_ref[1]
    total = sums_ref[...]
    count = 1.0 / (cells * group)
    plain = spread_groups(lane_slot(total, 0) * count, lanes, group)
    cross = spread_groups(lane_slot(total, 1) * count, lanes, group)
    scale = safe_scale(total, inv, coef_ref[0], coef_ref[1], coef_ref[2], cells, group)
    scale_ref[0:8] = jnp.broadcast_to(scale, (8, LANES))
    scale_ref[8:16] = jnp.broadcast_to(1.0 / scale, (8, LANES))

    def one(row, _):
        normal = (states_ref[row].reshape(cols, steps, lanes) - center[None]) * inv[None]
        d_norm = d_norm_ref[row].reshape(cols, steps, lanes)
        d_group = (d_norm - plain[None] - normal * cross[None]) * inv[None]
        put_tiles(d_ref, d_group.reshape(span, lanes))
        reward = widen(reward_ref[place_ref[0] * rows + row], lanes)
        run = jnp.zeros_like(reward)
        for k in range(steps - 1, -1, -1):
            drift = coef_ref[2, k : k + 1]
            put_step(adj_ref, k, cols, steps, drift * run)
            d_state = drift * reward + get_step(d_ref, k, cols, steps)
            run = run + (coef_ref[1, k : k + 1] * reward + d_state)
        up_ref[pl.ds(pl.multiple_of(row * span, 16), span), :] = get_tiles(adj_ref).astype(BF16)
        return 0

    lax.fori_loop(0, rows, one, 0)
    up_t_ref[...] = jnp.transpose(up_ref[...])[: up_t_ref.shape[0]]
    for half, late_ref in enumerate((late_a_ref, late_b_ref)):

        @pl.when(place_ref[1] != half)
        def _():
            half_gradient(half, up_t_ref[...], late_ref, scale, even_ref, odd_ref, steps, out_ref)


def unpack_kernel(ready, place_ref, own_ref, other_ref, scale_ref, out_ref):
    whole = out_ref.shape[2] // LANES
    half = LANES // 2
    scale = scale_ref[8:9]
    tiles = own_ref.shape[0]
    first = place_ref[1] == 0

    def tile(index):
        low, at = index < tiles, index % tiles
        mine, other = (own_ref[at], other_ref[at]) if low else (other_ref[at], own_ref[at])
        return jnp.where(first, mine, other) * scale

    for tap in range(9):
        for piece in range(whole):
            at = piece * LANES
            out_ref[tap, :, at : at + LANES] = tile(tap * whole + piece)
        rest = tile(9 * whole + tap // 2)
        if tap % 2:
            rest = pltpu.roll(rest, half, 1)
        out_ref[tap, :, whole * LANES :] = rest[:, :half]


def call(
    kernel, outs, scratch, flops, smem=(), vmem=(), load=(), hbm=(), grant=VMEM_BYTES, aliases=None, size=None
):
    args = [*smem, *vmem, *load, *hbm]
    counts = [len(smem) + len(vmem), len(load), len(hbm) + len(outs) + len(scratch)]
    specs = [pl.BlockSpec(memory_space=pltpu.SMEM)] * len(smem)
    specs += [pl.BlockSpec(memory_space=pltpu.VMEM)] * len(vmem)
    specs += [pl.BlockSpec(memory_space=pltpu.HBM)] * (len(load) + len(hbm))
    shapes = [jax.ShapeDtypeStruct(out[0], out[1]) for out in outs]
    out_specs = [pl.BlockSpec(memory_space=out[2] if len(out) > 2 else pltpu.VMEM) for out in outs]
    if size is None:
        size = sum(a.size * a.dtype.itemsize for a in [*args, *shapes])
    buffers = [s if not isinstance(s, tuple) else pltpu.VMEM(*s) for s in scratch]
    buffers += [pltpu.VMEM(x.shape, x.dtype) for x in load]
    buffers += [pltpu.SemaphoreType.DMA((len(load),))] if load else []

    def body(*refs):
        first, wanted, rest = counts[0], counts[1], counts[2]
        sources = refs[first : first + wanted]
        middle = refs[first + wanted : first + wanted + rest]
        held = refs[first + wanted + rest : first + wanted + rest + wanted]
        copies = start_copies(list(zip(sources, held)), refs[-1]) if wanted else []
        kernel(functools.partial(wait_copies, copies), *refs[:first], *held, *middle)

    return pl.pallas_call(
        body,
        out_shape=shapes,
        in_specs=specs,
        out_specs=out_specs,
        scratch_shapes=buffers,
        input_output_aliases=aliases or {},
        compiler_params=pltpu.CompilerParams(vmem_limit_bytes=grant),
        cost_estimate=pl.CostEstimate(flops=flops, bytes_accessed=size, transcendentals=0),
    )(*args)


F16 = jnp.float16


def bit_of(axis, bit):
    return (lax.axis_index(axis) // bit) % 2


def side(which, count=1):
    unsigned = jnp.uint32
    return (which * count).astype(unsigned), ((1 - which) * count).astype(unsigned), which == 0


def part_of(value, start, count, dim):
    starts = [start if i == dim else jnp.uint32(0) for i in range(value.ndim)]
    sizes = [count if i == dim else size for i, size in enumerate(value.shape)]
    return lax.dynamic_slice(value, starts, sizes)


def half_of_dim(value, start, dim):
    return part_of(value, start, value.shape[dim] // 2, dim)


def half_sum(value, mine, send, dim):
    arrived = send(half_of_dim(value, mine[1], dim).astype(F16))
    return half_of_dim(value, mine[0], dim) + arrived.astype(value.dtype)


def both_halves(value, mine, send, dim):
    other = send(value)
    low = jnp.where(mine[2], value, other)
    high = jnp.where(mine[2], other, value)
    return jnp.concatenate([low, high], axis=dim)


def joint_sum(value, sides, dims, sends):
    def quarter(flips):
        part = value
        for mine, dim, flip in zip(sides, dims, flips):
            part = half_of_dim(part, mine[1 if flip else 0], dim)
        return part

    total = quarter((0, 0))
    arrived = [send(quarter(flips).astype(F16)) for flips, send in sends]
    for part in arrived:
        total = total + part.astype(value.dtype)
    return total


def joint_gather(value, sides, dims, sends):
    parts = {(0, 0): value}
    for flips, send in sends:
        parts[flips] = send(value)

    def order(first, second, mine, dim):
        low = jnp.where(mine[2], first, second)
        high = jnp.where(mine[2], second, first)
        return jnp.concatenate([low, high], axis=dim)

    rows = [order(parts[(0, flip)], parts[(1, flip)], sides[0], dims[0]) for flip in (0, 1)]
    return order(rows[0], rows[1], sides[1], dims[1])


FLIPS = ((1, 0), (0, 1), (1, 1))


def reduce_weights(kept, arrived, needs, sweep, travel, land, landing, sides):
    slabs, tiles, share_rows, lanes = kept.shape
    shape = (slabs, 2, tiles // 2, 2, 2, share_rows // 4, lanes)
    pieces = (kept.reshape(shape), arrived.reshape(shape))
    tall, wide = lax.axis_size("sy"), lax.axis_size("sx")

    def turned(sy, sx, turn):
        return (sy, sx ^ 2) if sx % 2 == turn else (sy ^ 1, sx)

    def send_tile(turn, flip_turn, flip_far):
        pairs = []
        for i in range(tall * wide):
            sy, sx = divmod(i, wide)
            to = turned(sy, sx, turn) if flip_turn else (sy, sx)
            to = (to[0] ^ 2, to[1]) if flip_far else to
            pairs.append((i, to[0] * wide + to[1]))
        return lambda value: lax.ppermute(value, ("sy", "sx"), pairs)

    def send_slab(bit, flip_slab, flip_far):
        pairs = []
        for i in range(slabs * tall):
            tm, sy = divmod(i, tall)
            pairs.append((i, (tm ^ (bit * flip_slab)) * tall + (sy ^ (2 * flip_far))))
        return lambda value: lax.ppermute(value, ("tm", "sy"), pairs)

    first, second, far, *slab_sides = sides

    def half(which):
        return sum(half_of_dim(x, which, 1) for x in pieces)

    outgoing, needs = lax.optimization_barrier((half(first[1]).astype(F16), needs))
    other = send_tile(0, 1, 0)(outgoing)
    other, (trajectory, leaving) = lax.optimization_barrier((other, sweep(needs)))
    value = half(first[0]) + other.astype(F32)
    trajectory = land(landing, trajectory, 0)
    landing = travel(leaving)
    value = half_sum(value, second, send_tile(1, 1, 0), 3)
    value, trajectory = lax.optimization_barrier((value, trajectory))
    bits = axis_bits(("tm",))[::-1]
    for (_, bit), mine in zip(bits[:-1], slab_sides):
        value = half_sum(value, mine, lambda x, bit=bit: swap(x, "tm", bit), 0)
    if bits:
        sends = [(flips, send_slab(bits[-1][1], *flips)) for flips in FLIPS]
        value = joint_sum(value, (slab_sides[-1], far), (0, 4), sends)
    else:
        value = half_sum(value, far, lambda x: swap(x, "sy", 2), 4)
    value = value.astype(F16)
    sends = [(flips, send_tile(1, flips[1], flips[0])) for flips in FLIPS]
    value = joint_gather(value, (far, second), (4, 3), sends)
    value, landing = lax.optimization_barrier((value, landing))
    value = both_halves(value, first, send_tile(0, 1, 0), 1)
    value, trajectory = lax.optimization_barrier((value, land(landing, trajectory, 1)))
    value = value.reshape(tiles, share_rows, lanes)
    return value.astype(F32), swap(value, "sx", 1).astype(F32), trajectory


def shards(
    latent_init, step_noise, coef_state, coef_drift, coef_noise, step_index, time_table, norm_gain,
    conv_weight, reward_grad,
):
    tile_rows, cols, channels = latent_init.shape
    group = channels // GROUPS
    lanes = -(-channels // LANES) * LANES
    extra = lanes - channels
    slabs = lax.axis_size("tm")
    steps_here = step_noise.shape[0]
    steps = steps_here * slabs
    rows = tile_rows // slabs
    span = steps * cols
    tm, sy, sx = (lax.axis_index(axis) for axis in ("tm", "sy", "sx"))
    half = half_of(tm, sy)
    conv_flops = 2 * 9 * rows * span * channels * channels
    cells = tile_rows * lax.axis_size("sy") * cols * lax.axis_size("sx")
    targets = [half_of((tm + offset) % slabs, sy) for offset in range(1, slabs)]
    tall, wide = lax.axis_size("sy"), lax.axis_size("sx")
    diagonal = [(sy + dy, sx + dx) for dy in (-1, 1) for dx in (-1, 1)]
    corners = [jnp.clip(y, 0, tall - 1) * wide + jnp.clip(x, 0, wide - 1) for y, x in diagonal]
    origins = [half_of((tm - offset + slabs) % slabs, sy) for offset in range(1, slabs)]
    place = [half, sx % 2, tm, jnp.int32(rows)] + corners + targets + origins
    place = jnp.stack(place).astype(jnp.int32)
    flags = [(sy > 0) | (half > 0), (sy < tall - 1) | (half < slabs - 1), sx > 0, sx < wide - 1]
    flags += [(y >= 0) & (y < tall) & (x >= 0) & (x < wide) for y, x in diagonal]
    flags = jnp.stack(flags).astype(F32)
    turns = [bit_of("sx", 2), bit_of("sy", 1)]
    core = bit_of("sx", 1)
    halves = [
        side(jnp.where(core == 0, turns[0], turns[1])),
        side(jnp.where(core == 0, turns[1], turns[0])),
        side(bit_of("sy", 2)),
    ]
    held = slabs
    for _, bit in axis_bits(("tm",))[::-1]:
        held //= 2
        halves.append(side(bit_of("tm", bit), held))
    cut = rows // 2
    place, flags, halves, latent_init = lax.optimization_barrier((place, flags, halves, latent_init))

    def shifted(offset):
        return [(i, (i + offset) % slabs) for i in range(slabs)]

    tiles_axes = ("sy", "sx")
    tile_devices = lax.axis_size(tiles_axes)
    sent_shape = (slabs - 1, steps_here, rows, cols, channels)
    end_shape, col_shape = ((2, cols, channels), F32), ((2, tile_rows, channels), F32)
    part_rows = CORNERS + 8 * (lanes // LANES)
    moments, table, low_rows, high_rows, first_cols, last_cols, leaving = call(
        functools.partial(start_kernel, group),
        [((tile_devices, part_rows, LANES), F32), ((4, steps_here, lanes), F32)]
        + [end_shape, end_shape, col_shape, col_shape, (sent_shape, BF16)],
        [pltpu.SemaphoreType.DMA((slabs - 1,))],
        10**6,
        smem=[step_index, place, coef_state, coef_drift, coef_noise],
        load=[latent_init, reward_grad, time_table.T, norm_gain],
        hbm=[step_noise],
        grant=WHOLE_BYTES,
    )

    def to_slabs(pieces):
        if slabs == 2:
            return lax.ppermute(pieces, "tm", shifted(1))
        return jnp.stack([lax.ppermute(pieces[i], "tm", shifted(i + 1)) for i in range(slabs - 1)])

    down, up = chain("sy")
    right_way, left_way = chain("sx")
    low = lax.ppermute(low_rows, "sy", down)
    high = lax.ppermute(high_rows, "sy", up)
    left = lax.ppermute(last_cols, "sx", right_way)
    right = lax.ppermute(first_cols, "sx", left_way)
    other_tables = to_slabs(jnp.broadcast_to(table[None], (slabs - 1,) + table.shape))
    other_tables, leaving = lax.optimization_barrier((other_tables, leaving))
    others = to_slabs(leaving)
    parts1 = share(moments, tiles_axes)
    parts1, conv_weight = lax.optimization_barrier((parts1, conv_weight))
    (coefs,) = call(
        table_kernel, [((4, steps, lanes), F32)], [], 10**5, smem=[place], vmem=[table, other_tables],
        grant=SMALL_BYTES,
    )
    packed = ((9 * (lanes - LANES) + 5 * LANES, lanes), BF16)
    weight_out, weight_back = call(
        pack_weight_kernel, [packed, packed], [], 10**7, load=[conv_weight.reshape(9, channels, channels)],
    )

    even_shape = (rows + 2, (cols + 2) * steps, lanes)
    odd_shape = (rows + 2, span, lanes)
    field_shape = (rows, span, lanes)
    y_shape = (lanes // LANES, chunk_rows(rows, span) * span, LANES)
    row_shape = (lanes // LANES, span, LANES)
    noise_shape = (steps_here, rows, cols, channels)
    even_out, odd_out, field_out = (even_shape, BF16), (odd_shape, BF16), (field_shape, F32)
    edge_row, edge_col = ((1, span, lanes), F32), ((rows, steps, lanes), F32)
    noise_scratch = [(noise_shape, BF16)]
    even1, odd1, sides, first_row, last_row = call(
        functools.partial(edge_sweep_kernel, group, cells),
        [even_out, odd_out, ((2, 2, tile_rows + 2, lanes), F32), edge_row, edge_row],
        noise_scratch + [(row_shape, F32), (row_shape, F32), pltpu.SemaphoreType.DMA((1,))],
        conv_flops // 4,
        smem=[flags, place],
        vmem=[low, high, left, right, parts1, coefs, latent_init, others, weight_out],
        hbm=[step_noise],
    )
    down_rows, up_rows = row_chain()
    top = lax.ppermute(last_row, ("tm", "sy"), down_rows)
    bottom = lax.ppermute(first_row, ("tm", "sy"), up_rows)
    states, moments, first_col, last_col = call(
        functools.partial(inner_sweep_kernel, group),
        [field_out, ((2, steps, LANES), F32), edge_col, edge_col],
        noise_scratch + [(y_shape, F32), (row_shape, F32), pltpu.SemaphoreType.DMA((1,))],
        conv_flops,
        smem=[place],
        vmem=[first_row, last_row, even1, odd1, coefs, latent_init, others, weight_out],
        hbm=[step_noise],
    )

    def side_cols(args):
        top, bottom, first, last = args
        side_out = ((rows + 2, steps, lanes), F32)
        first, last = call(
            edge_kernel, [side_out, side_out], [], 10**5, vmem=[top, bottom, first, last], grant=SMALL_BYTES
        )
        return lax.ppermute(last, "sx", right_way), lax.ppermute(first, "sx", left_way)

    def act_gradient(first, count):
        def run(reward):
            (out,) = call(
                functools.partial(act_gradient_kernel, first),
                [((count, span, lanes), F32)],
                [((count + 2,) + even_shape[1:], BF16), ((count + 2,) + odd_shape[1:], BF16)],
                conv_flops // 4,
                smem=[place],
                vmem=[reward, low, high, sides, coefs, weight_back],
            )
            return out

        return run

    order = ("sx", "sy", "tm")
    quarter = max(1, rows // 4)
    pieces = [(at, min(quarter, rows - at)) for at in range(0, rows, quarter)]

    def cols_and_first(args):
        return side_cols(args[1:]), act_gradient(*pieces[0])(args[0])

    def d_act_work(piece):
        return lambda done: (act_gradient(*piece), reward_grad)

    moments2, (((left2, right2), d_first), *d_rest) = butterfly(
        moments,
        order,
        join_moments(float(rows * cols * group)),
        [lambda done: (cols_and_first, (reward_grad, top, bottom, first_col, last_col))]
        + [d_act_work(piece) for piece in pieces[1:]],
    )
    even2, odd2, d_norm, sums, norm = call(
        functools.partial(norm_gradient_kernel, group, cells),
        [even_out, odd_out, field_out, ((steps, LANES), F32), ((2, steps, lanes), F32)],
        [],
        40 * rows * span * lanes,
        smem=[flags, place],
        vmem=[moments2, top, bottom, left2, right2, coefs, reward_grad, states, d_first, *d_rest],
    )

    share_rows = channels // slabs
    tiles = 9 * (channels // LANES) + 6

    def late_weight(half):
        def run(reward):
            (out,) = call(
                functools.partial(late_weight_kernel, half),
                [((tiles // 2, channels, LANES), F32)],
                [],
                conv_flops // 2,
                smem=[place],
                vmem=[reward, coefs, even2, odd2],
            )
            return out

        return lambda done: (run, reward_grad)

    def second_sweep(first, count):
        out_shape = (slabs, steps_here, count, cols, channels)

        def run(args):
            base = list(args[1:])
            return call(
                functools.partial(second_sweep_kernel, first),
                [(step_noise.shape, F32, pltpu.HBM), ((slabs - 1,) + out_shape[1:], F32)],
                [(noise_shape, BF16), (y_shape, F32), (row_shape, F32), (out_shape, F32)]
                + [pltpu.SemaphoreType.DMA((1,)), pltpu.SemaphoreType.DMA((1,))],
                conv_flops // 2,
                smem=[place],
                vmem=[coefs, args[0], states, others, weight_out, even2, odd2],
                hbm=[step_noise] + base,
                aliases={9: 0} if base else None,
            )

        return run

    sums, (late_a, late_b, (base, leaving)) = butterfly(
        sums,
        ("tm", "sx", "sy"),
        join_sums,
        [
            late_weight(0),
            late_weight(1),
            lambda done: (second_sweep(0, cut), (latent_init,)),
        ],
    )
    landing = to_slabs(leaving.astype(F16))

    payload = ((slabs, tiles // 2, share_rows, LANES), F32)
    up_shape = ((channels, rows * span), BF16)
    sent, scales, up_t = call(
        functools.partial(sent_weight_kernel, group, cells),
        [payload, ((16, LANES), F32), up_shape],
        [(row_shape, F32), (row_shape, F32), ((rows * span, lanes), BF16)],
        conv_flops // 2,
        smem=[place],
        vmem=[states, norm, sums, coefs, d_norm, reward_grad, even1, odd1, late_a, late_b],
        size=10**6,
    )

    def kept_weight(args):
        (kept,) = call(
            kept_weight_kernel,
            [payload],
            [],
            conv_flops // 2,
            smem=[place],
            vmem=[args[0], coefs, scales, even1, odd1, late_a, late_b],
        )
        return kept

    sent, landing = lax.optimization_barrier((sent, landing))
    arrived, kept = beside(sent, "sx", 1, kept_weight, (up_t,))

    def land(part, trajectory, which):
        (trajectory,) = call(
            functools.partial(land_kernel, (0, cut)[which]),
            [(step_noise.shape, F32, pltpu.HBM)],
            [(part.shape, F32), pltpu.SemaphoreType.DMA((slabs - 1,))],
            10**6,
            smem=[place],
            vmem=[latent_init, part.astype(F32)],
            hbm=[trajectory],
            aliases={3: 0},
        )
        return trajectory

    own, other, trajectory = reduce_weights(
        kept,
        arrived,
        (latent_init, base),
        second_sweep(cut, rows - cut),
        lambda leaving: to_slabs(leaving.astype(F16)),
        land,
        landing,
        halves,
    )
    (grad,) = call(
        unpack_kernel, [((9, share_rows, channels), F32)], [], 10**6, smem=[place], vmem=[own, other, scales],
        grant=SMALL_BYTES,
    )
    return trajectory, grad.transpose(0, 2, 1).reshape(3, 3, channels, share_rows)


def solution(mesh):
    placed = (
        P("sy", "sx", None),
        P("tm", "sy", "sx", None),
        P("tm"),
        P("tm"),
        P("tm"),
        P("tm"),
        P(),
        P(),
        P(),
        P("sy", "sx", None),
    )
    return jax.shard_map(
        shards,
        mesh=mesh,
        in_specs=placed,
        out_specs=(P("tm", "sy", "sx", None), P(None, None, None, "tm")),
        check_vma=False,
    )
```

```python
import functools

import jax
import jax.numpy as jnp
from jax import lax
from jax.experimental import pallas as pl
from jax.experimental.pallas import tpu as pltpu
from jax.sharding import PartitionSpec as P

GROUPS = 32
EPSILON = 1e-05
LANES = 128
F32 = jnp.float32
BF16 = jnp.bfloat16
VMEM_BYTES = 16 * 1024 * 1024
SMALL_BYTES = 4 * 1024 * 1024
WHOLE_BYTES = 61 * 10**6


def axis_bits(axes):
    bits = []
    for axis in axes:
        step = 1
        while step < lax.axis_size(axis):
            bits.append((axis, step))
            step *= 2
    return bits


def swap(value, axis, bit):
    pairs = [(i, i ^ bit) for i in range(lax.axis_size(axis))]
    return lax.ppermute(value, axis, pairs)


def half_of(tm_index, sy_index):
    last = lax.axis_size("tm") - 1
    return jnp.where(sy_index % 2 == 0, tm_index, last - tm_index)


def share(copies, axes):
    return lax.all_to_all(copies, axes, 0, 0)


def beside(value, axis, bit, work, needs):
    value, needs = lax.optimization_barrier((value, needs))
    other = swap(value, axis, bit)
    return lax.optimization_barrier((other, work(needs)))


def butterfly(value, axes, join, works):
    results = []
    for i, (axis, bit) in enumerate(axis_bits(axes)):
        if i < len(works):
            other, result = beside(value, axis, bit, *works[i](results))
            results.append(result)
        else:
            other = swap(value, axis, bit)
        value = join(value, other, 2**i)
    return value, results


def join_moments(count):
    def join(mine, other, size):
        gap = mine[0] - other[0]
        mean = 0.5 * (mine[0] + other[0])
        return jnp.stack([mean, mine[1] + other[1] + gap * gap * (0.5 * count * size)])

    return join


def join_sums(mine, other, size):
    return mine + other


def chain(axis):
    count = lax.axis_size(axis)
    forward = [(i, i + 1) for i in range(count - 1)]
    return forward, [(b, a) for a, b in forward]


def row_chain():
    slabs, tiles = lax.axis_size("tm"), lax.axis_size("sy")
    order = []
    for sy in range(tiles):
        for half in range(slabs):
            tm = half if sy % 2 == 0 else slabs - 1 - half
            order.append(tm * tiles + sy)
    forward = list(zip(order[:-1], order[1:]))
    return forward, [(b, a) for a, b in forward]


def group_matrix(rows, cols, group, channel_dim, slot):
    channel = lax.broadcasted_iota(jnp.int32, (rows, cols), channel_dim)
    place = lax.broadcasted_iota(jnp.int32, (rows, cols), 1 - channel_dim)
    scale = (1 << 16) // group + 1
    same = ((channel * scale) >> 16) + slot * GROUPS == place
    return (same & (channel < GROUPS * group)).astype(F32)


def exact_dot(left, right):
    return jnp.dot(left, right, precision=lax.Precision.HIGHEST, preferred_element_type=F32)


def gather_groups(values, group, slot):
    return exact_dot(values, group_matrix(values.shape[1], LANES, group, 0, slot))


def spread_groups(values, lanes, group):
    return exact_dot(values, group_matrix(LANES, lanes, group, 1, 0))


def lane_slot(values, slot):
    if slot:
        values = pltpu.roll(values, LANES - slot * GROUPS, 1)
    lane = lax.broadcasted_iota(jnp.int32, values.shape, 1)
    return jnp.where(lane < GROUPS, values, 0.0)


def merged_moments(parts, total_count, lanes, group):
    devices = parts.shape[0]
    total = jnp.sum(parts, axis=0)
    center = lane_slot(total, 0) * (1.0 / devices)
    gap = parts - center[None]
    between = lane_slot(jnp.sum(gap * gap, axis=0), 0) * (total_count / devices)
    spread = (between + lane_slot(total, 1)) * (1.0 / total_count)
    inv = lane_slot(1.0 / jnp.sqrt(spread + EPSILON), 0)
    return spread_groups(center, lanes, group), spread_groups(inv, lanes, group)


def final_moments(moments_ref, count, lanes, group):
    center = lane_slot(moments_ref[0], 0)
    inv = lane_slot(1.0 / jnp.sqrt(moments_ref[1] * (1.0 / count) + EPSILON), 0)
    return spread_groups(center, lanes, group), spread_groups(inv, lanes, group)


def start_copies(pairs, sem):
    copies = [pltpu.make_async_copy(a, b, sem.at[i]) for i, (a, b) in enumerate(pairs)]
    for copy in copies:
        copy.start()
    return copies


def wait_copies(copies):
    for copy in copies:
        copy.wait()


def widen(x, lanes):
    return jnp.concatenate([x, jnp.zeros((x.shape[0], lanes - x.shape[1]), x.dtype)], axis=1)


def framed_row(tile_ref, low_ref, high_ref, sides_ref, part, half, rows, row, lanes):
    tall = tile_ref.shape[0]
    place = half * rows + row - 1
    inner = tile_ref[jnp.clip(place, 0, tall - 1)]
    inner = jnp.where(place < 0, low_ref[part], jnp.where(place >= tall, high_ref[part], inner))
    left = sides_ref[0, part, pl.ds(place + 1, 1), :]
    right = sides_ref[1, part, pl.ds(place + 1, 1), :]
    return jnp.concatenate([left, widen(inner, lanes), right], axis=0)


def noise_of(own_ref, others_ref, place_ref, k, row, lanes):
    steps_here = own_ref.shape[0]
    slabs = others_ref.shape[0] + 1
    slab, step = divmod(k, steps_here)
    offset = lax.rem(place_ref[2] - slab + slabs, slabs)
    mine = own_ref[step, row].astype(F32)
    other = others_ref[jnp.maximum(offset - 1, 0), step, row].astype(F32)
    return widen(jnp.where(offset == 0, mine, other), lanes)


CORNERS = 8


def start_kernel(
    group, ready, index_ref, place_ref, state_ref, drift_ref, noise_coef_ref, lat_ref, reward_ref,
    time_ref, gain_ref, noise_hbm, part_ref, table_ref, low_ref, high_ref, first_ref, last_ref, sent_ref, sem,
):
    others, steps, rows = sent_ref.shape[:3]
    copies = start_copies(
        [
            (noise_hbm.at[:, pl.ds(place_ref[8 + i] * rows, rows)], sent_ref.at[i])
            for i in range(others)
        ],
        sem,
    )
    ready()
    tall, wide, channels = lat_ref.shape
    lanes = table_ref.shape[2]
    corners = []
    for part, ref in enumerate((lat_ref, reward_ref)):
        low_ref[part] = ref[tall - 1]
        high_ref[part] = ref[0]
        for row in range(tall):
            first_ref[part, row : row + 1] = ref[row, 0:1]
            last_ref[part, row : row + 1] = ref[row, wide - 1 : wide]
    for row in (0, tall - 1):
        for col in (0, wide - 1):
            for ref in (lat_ref, reward_ref):
                cell = widen(ref[row, col : col + 1], lanes)
                corners += [cell[:, at : at + LANES] for at in range(0, lanes, LANES)]
    entries = time_ref.shape[1]
    which = lax.broadcasted_iota(jnp.int32, (entries, LANES), 0)
    line = lax.broadcasted_iota(jnp.int32, (entries, LANES), 1)
    hit = jnp.zeros((entries, LANES), F32)
    for k in range(steps):
        hit = jnp.where((line == k) & (which == index_ref[k]), 1.0, hit)
    embedded = jnp.transpose(exact_dot(time_ref[...], hit))[:8]
    modulate = widen(gain_ref[...][None, :] * (1.0 + embedded), lanes)
    table_ref[0] = modulate[:steps]
    for k in range(steps):
        for i, ref in enumerate((state_ref, drift_ref, noise_coef_ref)):
            table_ref[i + 1, k : k + 1] = jnp.full((1, lanes), ref[k], F32)
    x = lat_ref[...].reshape(tall * wide, channels)
    sums = jnp.broadcast_to(jnp.sum(x, axis=0, keepdims=True), (8, channels))
    mean = gather_groups(sums, group, 0) * (1.0 / (tall * wide * group))
    gap = x - spread_groups(mean, channels, group)[0:1]
    square = jnp.broadcast_to(jnp.sum(gap * gap, axis=0, keepdims=True), (8, channels))
    part = jnp.concatenate([mean + gather_groups(square, group, 1)] + corners, axis=0)
    part_ref[...] = jnp.broadcast_to(part[None], part_ref.shape)
    wait_copies(copies)


def edge_kernel(ready, top_ref, bottom_ref, first_ref, last_ref, first_out, last_out):
    rows, steps, _ = first_ref.shape
    span = top_ref.shape[1]
    for out, ref, at in ((first_out, first_ref, 0), (last_out, last_ref, span - steps)):
        out[0] = top_ref[0, at : at + steps]
        out[1 : rows + 1] = ref[...]
        out[rows + 1] = bottom_ref[0, at : at + steps]


def table_kernel(ready, place_ref, own_ref, others_ref, out_ref):
    slabs = others_ref.shape[0] + 1
    kinds, steps, _ = own_ref.shape
    for offset in range(slabs):
        source = lax.rem(place_ref[2] - offset + slabs, slabs)
        for kind in range(kinds):
            rows = own_ref[kind] if offset == 0 else others_ref[offset - 1, kind]
            for k in range(steps):
                out_ref[kind, pl.ds(source * steps + k, 1), :] = rows[k : k + 1]


def packed_rows(taps, channels):
    whole = channels // LANES * LANES
    places = []
    for tap in range(taps):
        rest = taps * whole + tap // 2 * LANES + tap % 2 * (LANES // 2)
        places.append((tap * whole, rest))
    return whole, places


def pack_weight_kernel(ready, w_ref, out_ref, back_ref):
    taps, channels, _ = w_ref.shape
    lanes = out_ref.shape[1]
    whole, places = packed_rows(taps, channels)
    out_ref[...] = jnp.zeros(out_ref.shape, BF16)
    back_ref[...] = jnp.zeros(back_ref.shape, BF16)
    ready()
    for tap, (at, rest) in enumerate(places):
        for ref, value in ((out_ref, w_ref[tap]), (back_ref, jnp.transpose(w_ref[taps - 1 - tap]))):
            ref[at : at + whole, 0:channels] = value[:whole]
            ref[rest : rest + channels - whole, 0:channels] = value[whole:]


def half_turn(x):
    return pltpu.roll(x.astype(F32), LANES // 2, 1).astype(BF16)


def pair_rests(rests):
    pairs = []
    for i in range(0, len(rests), 2):
        pairs.append(rests[i] if i + 1 == len(rests) else rests[i] + half_turn(rests[i + 1]))
    return pairs


def convolve_rows(even_ref, odd_ref, w_ref, start, count, steps):
    span, lanes = odd_ref.shape[1:]
    parts = []
    for row_off in range(3):
        rows = pl.ds(start + row_off, count)
        parts.append(even_ref[rows, 0:span, :].reshape(count * span, lanes))
        parts.append(odd_ref[rows].reshape(count * span, lanes))
        parts.append(even_ref[rows, 2 * steps : 2 * steps + span, :].reshape(count * span, lanes))
    whole = lanes - LANES
    packed = [x[:, :whole] for x in parts] + pair_rests([x[:, whole:] for x in parts])
    return jnp.dot(jnp.concatenate(packed, axis=1), w_ref[...], preferred_element_type=F32)


def put_tiles(ref, value):
    for tile in range(ref.shape[0]):
        ref[tile] = value[:, tile * LANES : (tile + 1) * LANES]


def get_tiles(ref):
    return jnp.concatenate([ref[tile] for tile in range(ref.shape[0])], axis=1)


def get_step(ref, start, cols, steps):
    where = pl.ds(start, cols, stride=steps)
    return jnp.concatenate([ref[tile, where, :] for tile in range(ref.shape[0])], axis=1)


def put_step(ref, start, cols, steps, value):
    where = pl.ds(start, cols, stride=steps)
    for tile in range(ref.shape[0]):
        ref[tile, where, :] = value[:, tile * LANES : (tile + 1) * LANES]


def chunk_rows(rows, span):
    count = max(1, min(rows, 384 // span))
    while rows % count:
        count -= 1
    return count


def advance_row(row, at, half, rows, steps, lat_ref, noise, place_ref, coef_ref, y_ref, row_ref):
    lanes = row_ref.shape[0] * LANES
    cols = row_ref.shape[1] // steps
    own = widen(lat_ref[half * rows + row], lanes)
    run = jnp.zeros_like(own)
    for k in range(steps):
        put_step(row_ref, k, cols, steps, own + run)
        conv = get_step(y_ref, at + k, cols, steps)
        run = run + (
            coef_ref[1, k : k + 1] * own
            + coef_ref[2, k : k + 1] * (own + conv)
            + coef_ref[3, k : k + 1] * noise_of(*noise, place_ref, k, row, lanes)
        )
    return get_tiles(row_ref)


def edge_sweep_kernel(
    group, total_cells, ready, flag_ref, place_ref, low_ref, high_ref, left_ref, right_ref,
    parts_ref, coef_ref, lat_ref, others_ref, w_ref, noise_hbm,
    even_ref, odd_ref, sides_ref, first_row, last_row,
    noise_ref, y_ref, row_ref, sem,
):
    rows, span, lanes = odd_ref.shape
    rows = rows - 2
    steps = coef_ref.shape[1]
    cols = span // steps
    half = place_ref[0]
    tall = lat_ref.shape[0]
    own_noise = noise_hbm.at[:, pl.ds(half * rows, rows)]
    loads = start_copies([(own_noise, noise_ref)], sem)
    center, inv = merged_moments(parts_ref[:, :CORNERS], float(total_cells * group), lanes, group)
    center, inv = center[0:1], inv[0:1]
    pieces = lanes // LANES
    for side, ref in enumerate((left_ref, right_ref)):
        for part in range(2):
            sides_ref[side, part, 1 : tall + 1, :] = widen(ref[part], lanes)
            for end in range(2):
                at = CORNERS + ((3 - 2 * end - side) * 2 + part) * pieces
                device = place_ref[4 + 2 * end + side]
                cell = [parts_ref[device, at + i : at + i + 1, :] for i in range(pieces)]
                cell = jnp.concatenate(cell, axis=1) * flag_ref[4 + 2 * end + side]
                to = end * (tall + 1)
                sides_ref[side, part, to : to + 1, :] = cell
    ready()
    mod = coef_ref[0]

    def activate(row, _):
        field = framed_row(lat_ref, low_ref, high_ref, sides_ref, 0, half, rows, row, lanes)
        normal = (field - center) * inv
        pre = normal[:, None, :] * mod[None]
        act = pre / (1.0 + jnp.exp(-pre))
        keep = jnp.where(row == 0, flag_ref[0], jnp.where(row == rows + 1, flag_ref[1], 1.0))
        act = act * keep
        inner = act[1 : cols + 1]
        act = jnp.concatenate(
            [act[0:1] * flag_ref[2], inner, act[cols + 1 : cols + 2] * flag_ref[3]], axis=0
        )
        even_ref[row] = act.reshape((cols + 2) * steps, lanes).astype(BF16)
        odd_ref[row] = inner.reshape(span, lanes).astype(BF16)
        return 0

    lax.fori_loop(0, rows + 2, activate, 0)
    wait_copies(loads)
    for row, out in ((0, first_row), (rows - 1, last_row)):
        put_tiles(y_ref, convolve_rows(even_ref, odd_ref, w_ref, row, 1, steps))
        noise = (noise_ref, others_ref)
        out[0] = advance_row(row, 0, half, rows, steps, lat_ref, noise, place_ref, coef_ref, y_ref, row_ref)


def inner_sweep_kernel(
    group, ready, place_ref, first_row, last_row, even_ref, odd_ref, coef_ref, lat_ref, others_ref, w_ref,
    noise_hbm, states_ref, moment_ref, first_col, last_col, noise_ref, y_ref, row_ref, sem,
):
    rows, span, lanes = states_ref.shape
    steps = coef_ref.shape[1]
    cols = span // steps
    half = place_ref[0]
    own_noise = noise_hbm.at[:, pl.ds(half * rows, rows)]
    loads = start_copies([(own_noise, noise_ref)], sem)
    states_ref[0] = first_row[0]
    states_ref[rows - 1] = last_row[0]
    wait_copies(loads)
    count = chunk_rows(max(rows - 2, 1), span)

    def sweep(chunk, _):
        start = 1 + chunk * count
        put_tiles(y_ref, convolve_rows(even_ref, odd_ref, w_ref, start, count, steps))
        for inner in range(count):
            states_ref[start + inner] = advance_row(
                start + inner, inner * span, half, rows, steps, lat_ref, (noise_ref, others_ref),
                place_ref, coef_ref, y_ref, row_ref,
            )
        return 0

    lax.fori_loop(0, (rows - 2) // count, sweep, 0)
    zero = jnp.zeros((steps, lanes), F32)

    def add(row, total):
        return total + jnp.sum(states_ref[row].reshape(cols, steps, lanes), axis=0)

    mean = gather_groups(lax.fori_loop(0, rows, add, zero), group, 0) * (1.0 / (rows * cols * group))
    mean_here = spread_groups(mean, lanes, group)

    def squares(row, total):
        gap = states_ref[row].reshape(cols, steps, lanes) - mean_here[None]
        return total + jnp.sum(gap * gap, axis=0)

    moment_ref[0] = mean
    moment_ref[1] = gather_groups(lax.fori_loop(0, rows, squares, zero), group, 0)
    first_col[...] = states_ref[:, 0:steps]
    last_col[...] = states_ref[:, span - steps :]


def act_gradient_kernel(
    first, ready, place_ref, reward_ref, low_ref, high_ref, sides_ref, coef_ref, w_ref,
    out_ref, even_ref, odd_ref,
):
    rows, span, lanes = out_ref.shape
    steps = coef_ref.shape[1]
    cols = span // steps
    drift = coef_ref[2]

    def scale(row, _):
        field = framed_row(
            reward_ref, low_ref, high_ref, sides_ref, 1, place_ref[0], place_ref[3], row + first, lanes
        )
        up = field[:, None, :] * drift[None]
        even_ref[row] = up.reshape((cols + 2) * steps, lanes).astype(BF16)
        odd_ref[row] = up[1 : cols + 1].reshape(span, lanes).astype(BF16)
        return 0

    lax.fori_loop(0, rows + 2, scale, 0)
    count = chunk_rows(rows, span)

    def sweep(chunk, _):
        start = chunk * count
        out = convolve_rows(even_ref, odd_ref, w_ref, start, count, steps)
        out_ref[pl.ds(start, count)] = out.reshape(count, span, lanes)
        return 0

    lax.fori_loop(0, rows // count, sweep, 0)


def norm_gradient_kernel(
    group, total_cells, ready, flag_ref, place_ref, moments_ref, top_ref, bottom_ref, left_ref, right_ref,
    coef_ref, reward_ref, states_ref, *refs
):
    *d_act_refs, even_ref, odd_ref, d_norm_ref, sum_ref, norm_ref = refs
    rows, span, lanes = states_ref.shape
    steps = coef_ref.shape[1]
    cols = span // steps
    center, inv = final_moments(moments_ref, float(total_cells * group), lanes, group)
    norm_ref[0] = center
    norm_ref[1] = inv
    mod = coef_ref[0]

    def activate(at, inner, keep):
        field = jnp.concatenate(
            [left_ref[at][None], inner.reshape(cols, steps, lanes), right_ref[at][None]], axis=0
        )
        normal = (field - center[None]) * inv[None]
        pre = normal * mod[None]
        sig = 1.0 / (1.0 + jnp.exp(-pre))
        act = pre * sig
        if keep is not None:
            act = act * keep
        middle = act[1 : cols + 1]
        odd_ref[at] = middle.reshape(span, lanes).astype(BF16)
        act = jnp.concatenate(
            [act[0:1] * flag_ref[2], middle, act[cols + 1 : cols + 2] * flag_ref[3]], axis=0
        )
        even_ref[at] = act.reshape((cols + 2) * steps, lanes).astype(BF16)
        return [x[1 : cols + 1] for x in (normal, pre, sig)]

    activate(0, top_ref[0], flag_ref[0])
    activate(rows + 1, bottom_ref[0], flag_ref[1])

    def one(d_act_ref, first, index, sums):
        plain, cross, square = sums
        row = index + first
        normal, pre, sig = activate(row + 1, states_ref[row], None)
        slope = sig * (1.0 + pre * (1.0 - sig))
        d_norm = d_act_ref[index].reshape(cols, steps, lanes) * slope * mod[None]
        d_norm_ref[row] = d_norm.reshape(span, lanes)
        return (
            plain + jnp.sum(d_norm, axis=0),
            cross + jnp.sum(d_norm * normal, axis=0),
            square + jnp.sum(d_norm * d_norm, axis=0),
        )

    zero = jnp.zeros((steps, lanes), F32)
    sums = (zero, zero, zero)
    first = 0
    for d_act_ref in d_act_refs:
        count = d_act_ref.shape[0]
        sums = lax.fori_loop(0, count, functools.partial(one, d_act_ref, first), sums)
        first += count
    plain, cross, square = sums
    channels = reward_ref.shape[2]
    reward = reward_ref[pl.ds(place_ref[0] * rows, rows)].reshape(rows * cols, channels)
    reward = jnp.broadcast_to(jnp.sum(reward * reward, axis=0, keepdims=True), (steps, channels))
    sum_ref[...] = (
        gather_groups(plain, group, 0)
        + gather_groups(cross, group, 1)
        + gather_groups(square, group, 2)
        + gather_groups(reward, group, 3)
    )


def second_sweep_kernel(
    first, ready, place_ref, coef_ref, lat_ref, states_ref, others_ref, w_ref, even_ref, odd_ref, noise_hbm, *refs
):
    kept_hbm, sent_ref, noise_ref, y_ref, row_ref, out_ref, sem, out_sem = refs[-8:]
    all_rows, span, lanes = states_ref.shape
    slabs, steps_here, rows, cols, channels = out_ref.shape
    steps = slabs * steps_here
    half = place_ref[0]
    own_noise = noise_hbm.at[:, pl.ds(half * all_rows, all_rows)]
    wait_copies(start_copies([(own_noise, noise_ref)], sem))
    count = chunk_rows(rows, span)

    def sweep(chunk, _):
        start = chunk * count
        put_tiles(y_ref, convolve_rows(even_ref, odd_ref, w_ref, first + start, count, steps))
        for inner in range(count):
            row = first + start + inner
            own = widen(lat_ref[half * all_rows + row], lanes)
            put_tiles(row_ref, states_ref[row])
            run = jnp.zeros_like(own)
            for k in range(steps):
                conv = get_step(y_ref, inner * span + k, cols, steps)
                state = get_step(row_ref, k, cols, steps)
                run = run + (
                    coef_ref[1, k : k + 1] * state
                    + coef_ref[2, k : k + 1] * (state + conv)
                    + coef_ref[3, k : k + 1] * noise_of(noise_ref, others_ref, place_ref, k, row, lanes)
                )
                out_ref[k // steps_here, k % steps_here, start + inner] = run[:, :channels]
        return 0

    lax.fori_loop(0, rows // count, sweep, 0)
    for offset in range(1, slabs):
        sent_ref[offset - 1] = out_ref[lax.rem(place_ref[2] + offset, slabs)] * 0.125
    mine = place_ref[2]

    def complete(row, _):
        own = lat_ref[half * all_rows + first + row]
        for k in range(steps_here):
            out_ref[mine, k, row] = own + out_ref[mine, k, row]
        return 0

    lax.fori_loop(0, rows, complete, 0)
    pairs = [(out_ref.at[mine], kept_hbm.at[:, pl.ds(half * all_rows + first, rows)])]
    wait_copies(start_copies(pairs, out_sem))


def land_kernel(first, ready, place_ref, lat_ref, part_ref, base_hbm, out_hbm, hold_ref, sem):
    others, steps, count = part_ref.shape[:3]
    copies = []
    for i in range(others):
        at = place_ref[8 + others + i] * place_ref[3] + first

        def add(row, _):
            own = lat_ref[at + row]
            for k in range(steps):
                hold_ref[i, k, row] = own + 8.0 * part_ref[i, k, row]
            return 0

        lax.fori_loop(0, count, add, 0)
        copies.append(pltpu.make_async_copy(hold_ref.at[i], out_hbm.at[:, pl.ds(at, count)], sem.at[i]))
        copies[-1].start()
    wait_copies(copies)


def weight_terms(half, up_t, even_ref, odd_ref, steps, put):
    rows = odd_ref.shape[0] - 2
    span, lanes = odd_ref.shape[1:]
    whole = lanes - LANES

    def window(tap, first, last):
        row_off, col_off = divmod(tap, 3)
        if col_off == 1:
            part = odd_ref[row_off : row_off + rows, :, first:last]
        else:
            at = col_off * steps
            part = even_ref[row_off : row_off + rows, at : at + span, first:last]
        return part.reshape(rows * span, last - first)

    def emit(tile, part):
        term = jnp.dot(up_t, part, preferred_element_type=F32)
        for piece in range(part.shape[1] // LANES):
            put(tile + piece, term[:, piece * LANES : (piece + 1) * LANES])

    for i, tap in enumerate(range(6, 9) if half else range(0, 6)):
        emit(i * whole // LANES, window(tap, 0, whole))
    if half:
        rests = pair_rests([window(tap, whole, lanes) for tap in range(9)])
        emit(3 * whole // LANES, jnp.concatenate(rests, axis=1))
        put(3 * whole // LANES + 5, jnp.zeros((up_t.shape[0], LANES), F32))


def late_weight_kernel(half, ready, place_ref, reward_ref, coef_ref, even_ref, odd_ref, out_ref):
    rows, span, lanes = odd_ref.shape
    rows = rows - 2
    steps = coef_ref.shape[1]
    cols = span // steps
    channels = out_ref.shape[1]
    reward = reward_ref[pl.ds(place_ref[0] * rows, rows)].reshape(rows * cols, channels)
    up = widen(reward, lanes)[:, None, :] * coef_ref[2][None]
    up = up.reshape(rows * span, lanes).astype(BF16)

    def put(tile, value):
        out_ref[tile] = value

    weight_terms(half, jnp.transpose(up)[:channels], even_ref, odd_ref, steps, put)


def safe_scale(total, norm, mod, state_coef, drift_coef, cells, group):
    def whole(slot):
        return jnp.sqrt(jnp.sum(lane_slot(total, slot), axis=1, keepdims=True))

    gradient, reward = whole(2), whole(3)
    top_inv = jnp.max(norm, axis=1, keepdims=True)
    top_mod = jnp.max(jnp.abs(mod), axis=1, keepdims=True)
    state, drift = jnp.abs(state_coef[:, 0:1]), jnp.abs(drift_coef[:, 0:1])
    through = jnp.sum((state + drift) * reward + top_inv * gradient, axis=0, keepdims=True)
    field = top_mod * drift * (float(cells * group) ** 0.5)
    bound = jnp.sum(field * (reward + through), axis=0, keepdims=True) * 1.1
    power = jnp.clip(jnp.floor(jnp.log2(32768.0 / jnp.maximum(bound, 1e-30))), -60.0, 60.0)
    scale = jnp.ones_like(power)
    for bit in (32, 16, 8, 4, 2, 1):
        size = jnp.abs(power)
        has = jnp.floor(size / bit) - 2.0 * jnp.floor(size / (2 * bit)) > 0.5
        step = jnp.where(power > 0, 2.0**bit, 2.0**-bit)
        scale = jnp.where(has, scale * step, scale)
    return scale


def half_gradient(half, up_t, late_ref, scale, even_ref, odd_ref, steps, out_ref):
    slabs, _, share_rows, _ = out_ref.shape

    def put(tile, value):
        value = (value + late_ref[tile]) * scale
        for slab in range(slabs):
            out_ref[slab, tile] = value[slab * share_rows : (slab + 1) * share_rows]

    weight_terms(half, up_t, even_ref, odd_ref, steps, put)


def kept_weight_kernel(
    ready, place_ref, up_ref, coef_ref, scale_ref, even_ref, odd_ref, late_a_ref, late_b_ref, out_ref
):
    for half, late_ref in enumerate((late_a_ref, late_b_ref)):

        @pl.when(place_ref[1] == half)
        def _():
            scale, steps = scale_ref[0:1], coef_ref.shape[1]
            half_gradient(half, up_ref[...], late_ref, scale, even_ref, odd_ref, steps, out_ref)


def sent_weight_kernel(
    group, cells, ready, place_ref, states_ref, norm_ref, sums_ref, coef_ref,
    d_norm_ref, reward_ref, even_ref, odd_ref, late_a_ref, late_b_ref,
    out_ref, scale_ref, up_t_ref, d_ref, adj_ref, up_ref,
):
    rows, span, lanes = states_ref.shape
    steps = coef_ref.shape[1]
    cols = span // steps
    center, inv = norm_ref[0], norm_ref[1]
    total = sums_ref[...]
    count = 1.0 / (cells * group)
    plain = spread_groups(lane_slot(total, 0) * count, lanes, group)
    cross = spread_groups(lane_slot(total, 1) * count, lanes, group)
    scale = safe_scale(total, inv, coef_ref[0], coef_ref[1], coef_ref[2], cells, group)
    scale_ref[0:8] = jnp.broadcast_to(scale, (8, LANES))
    scale_ref[8:16] = jnp.broadcast_to(1.0 / scale, (8, LANES))

    def one(row, _):
        normal = (states_ref[row].reshape(cols, steps, lanes) - center[None]) * inv[None]
        d_norm = d_norm_ref[row].reshape(cols, steps, lanes)
        d_group = (d_norm - plain[None] - normal * cross[None]) * inv[None]
        put_tiles(d_ref, d_group.reshape(span, lanes))
        reward = widen(reward_ref[place_ref[0] * rows + row], lanes)
        run = jnp.zeros_like(reward)
        for k in range(steps - 1, -1, -1):
            drift = coef_ref[2, k : k + 1]
            put_step(adj_ref, k, cols, steps, drift * run)
            d_state = drift * reward + get_step(d_ref, k, cols, steps)
            run = run + (coef_ref[1, k : k + 1] * reward + d_state)
        up_ref[pl.ds(pl.multiple_of(row * span, 16), span), :] = get_tiles(adj_ref).astype(BF16)
        return 0

    lax.fori_loop(0, rows, one, 0)
    up_t_ref[...] = jnp.transpose(up_ref[...])[: up_t_ref.shape[0]]
    for half, late_ref in enumerate((late_a_ref, late_b_ref)):

        @pl.when(place_ref[1] != half)
        def _():
            half_gradient(half, up_t_ref[...], late_ref, scale, even_ref, odd_ref, steps, out_ref)


def unpack_kernel(ready, place_ref, own_ref, other_ref, scale_ref, out_ref):
    whole = out_ref.shape[2] // LANES
    half = LANES // 2
    scale = scale_ref[8:9]
    tiles = own_ref.shape[0]
    first = place_ref[1] == 0

    def tile(index):
        low, at = index < tiles, index % tiles
        mine, other = (own_ref[at], other_ref[at]) if low else (other_ref[at], own_ref[at])
        return jnp.where(first, mine, other) * scale

    for tap in range(9):
        for piece in range(whole):
            at = piece * LANES
            out_ref[tap, :, at : at + LANES] = tile(tap * whole + piece)
        rest = tile(9 * whole + tap // 2)
        if tap % 2:
            rest = pltpu.roll(rest, half, 1)
        out_ref[tap, :, whole * LANES :] = rest[:, :half]


def call(
    kernel, outs, scratch, flops, smem=(), vmem=(), load=(), hbm=(), grant=VMEM_BYTES, aliases=None, size=None
):
    args = [*smem, *vmem, *load, *hbm]
    counts = [len(smem) + len(vmem), len(load), len(hbm) + len(outs) + len(scratch)]
    specs = [pl.BlockSpec(memory_space=pltpu.SMEM)] * len(smem)
    specs += [pl.BlockSpec(memory_space=pltpu.VMEM)] * len(vmem)
    specs += [pl.BlockSpec(memory_space=pltpu.HBM)] * (len(load) + len(hbm))
    shapes = [jax.ShapeDtypeStruct(out[0], out[1]) for out in outs]
    out_specs = [pl.BlockSpec(memory_space=out[2] if len(out) > 2 else pltpu.VMEM) for out in outs]
    if size is None:
        size = sum(a.size * a.dtype.itemsize for a in [*args, *shapes])
    buffers = [s if not isinstance(s, tuple) else pltpu.VMEM(*s) for s in scratch]
    buffers += [pltpu.VMEM(x.shape, x.dtype) for x in load]
    buffers += [pltpu.SemaphoreType.DMA((len(load),))] if load else []

    def body(*refs):
        first, wanted, rest = counts[0], counts[1], counts[2]
        sources = refs[first : first + wanted]
        middle = refs[first + wanted : first + wanted + rest]
        held = refs[first + wanted + rest : first + wanted + rest + wanted]
        copies = start_copies(list(zip(sources, held)), refs[-1]) if wanted else []
        kernel(functools.partial(wait_copies, copies), *refs[:first], *held, *middle)

    return pl.pallas_call(
        body,
        out_shape=shapes,
        in_specs=specs,
        out_specs=out_specs,
        scratch_shapes=buffers,
        input_output_aliases=aliases or {},
        compiler_params=pltpu.CompilerParams(vmem_limit_bytes=grant),
        cost_estimate=pl.CostEstimate(flops=flops, bytes_accessed=size, transcendentals=0),
    )(*args)


F16 = jnp.float16


def bit_of(axis, bit):
    return (lax.axis_index(axis) // bit) % 2


def side(which, count=1):
    unsigned = jnp.uint32
    return (which * count).astype(unsigned), ((1 - which) * count).astype(unsigned), which == 0


def part_of(value, start, count, dim):
    starts = [start if i == dim else jnp.uint32(0) for i in range(value.ndim)]
    sizes = [count if i == dim else size for i, size in enumerate(value.shape)]
    return lax.dynamic_slice(value, starts, sizes)


def half_of_dim(value, start, dim):
    return part_of(value, start, value.shape[dim] // 2, dim)


def half_sum(value, mine, send, dim):
    arrived = send(half_of_dim(value, mine[1], dim).astype(F16))
    return half_of_dim(value, mine[0], dim) + arrived.astype(value.dtype)


def both_halves(value, mine, send, dim):
    other = send(value)
    low = jnp.where(mine[2], value, other)
    high = jnp.where(mine[2], other, value)
    return jnp.concatenate([low, high], axis=dim)


def joint_sum(value, sides, dims, sends):
    def quarter(flips):
        part = value
        for mine, dim, flip in zip(sides, dims, flips):
            part = half_of_dim(part, mine[1 if flip else 0], dim)
        return part

    total = quarter((0, 0))
    arrived = [send(quarter(flips).astype(F16)) for flips, send in sends]
    for part in arrived:
        total = total + part.astype(value.dtype)
    return total


def joint_gather(value, sides, dims, sends):
    parts = {(0, 0): value}
    for flips, send in sends:
        parts[flips] = send(value)

    def order(first, second, mine, dim):
        low = jnp.where(mine[2], first, second)
        high = jnp.where(mine[2], second, first)
        return jnp.concatenate([low, high], axis=dim)

    rows = [order(parts[(0, flip)], parts[(1, flip)], sides[0], dims[0]) for flip in (0, 1)]
    return order(rows[0], rows[1], sides[1], dims[1])


FLIPS = ((1, 0), (0, 1), (1, 1))


def reduce_weights(kept, arrived, needs, sweep, travel, land, landing, sides):
    slabs, tiles, share_rows, lanes = kept.shape
    shape = (slabs, 2, tiles // 2, 2, 2, share_rows // 4, lanes)
    pieces = (kept.reshape(shape), arrived.reshape(shape))
    tall, wide = lax.axis_size("sy"), lax.axis_size("sx")

    def turned(sy, sx, turn):
        return (sy, sx ^ 2) if sx % 2 == turn else (sy ^ 1, sx)

    def send_tile(turn, flip_turn, flip_far):
        pairs = []
        for i in range(tall * wide):
            sy, sx = divmod(i, wide)
            to = turned(sy, sx, turn) if flip_turn else (sy, sx)
            to = (to[0] ^ 2, to[1]) if flip_far else to
            pairs.append((i, to[0] * wide + to[1]))
        return lambda value: lax.ppermute(value, ("sy", "sx"), pairs)

    def send_slab(bit, flip_slab, flip_far):
        pairs = []
        for i in range(slabs * tall):
            tm, sy = divmod(i, tall)
            pairs.append((i, (tm ^ (bit * flip_slab)) * tall + (sy ^ (2 * flip_far))))
        return lambda value: lax.ppermute(value, ("tm", "sy"), pairs)

    first, second, far, *slab_sides = sides

    def half(which):
        return sum(half_of_dim(x, which, 1) for x in pieces)

    outgoing, needs = lax.optimization_barrier((half(first[1]).astype(F16), needs))
    other = send_tile(0, 1, 0)(outgoing)
    other, (trajectory, leaving) = lax.optimization_barrier((other, sweep(needs)))
    value = half(first[0]) + other.astype(F32)
    trajectory = land(landing, trajectory, 0)
    landing = travel(leaving)
    value = half_sum(value, second, send_tile(1, 1, 0), 3)
    value, trajectory = lax.optimization_barrier((value, trajectory))
    bits = axis_bits(("tm",))[::-1]
    for (_, bit), mine in zip(bits[:-1], slab_sides):
        value = half_sum(value, mine, lambda x, bit=bit: swap(x, "tm", bit), 0)
    if bits:
        sends = [(flips, send_slab(bits[-1][1], *flips)) for flips in FLIPS]
        value = joint_sum(value, (slab_sides[-1], far), (0, 4), sends)
    else:
        value = half_sum(value, far, lambda x: swap(x, "sy", 2), 4)
    value = value.astype(F16)
    sends = [(flips, send_tile(1, flips[1], flips[0])) for flips in FLIPS]
    value = joint_gather(value, (far, second), (4, 3), sends)
    value = both_halves(value, first, send_tile(0, 1, 0), 1)
    value, landing = lax.optimization_barrier((value, landing))
    value = value.reshape(tiles, share_rows, lanes)
    other = swap(value, "sx", 1)
    other, trajectory = lax.optimization_barrier((other, land(landing, trajectory, 1)))
    return value.astype(F32), other.astype(F32), trajectory


def shards(
    latent_init, step_noise, coef_state, coef_drift, coef_noise, step_index, time_table, norm_gain,
    conv_weight, reward_grad,
):
    tile_rows, cols, channels = latent_init.shape
    group = channels // GROUPS
    lanes = -(-channels // LANES) * LANES
    extra = lanes - channels
    slabs = lax.axis_size("tm")
    steps_here = step_noise.shape[0]
    steps = steps_here * slabs
    rows = tile_rows // slabs
    span = steps * cols
    tm, sy, sx = (lax.axis_index(axis) for axis in ("tm", "sy", "sx"))
    half = half_of(tm, sy)
    conv_flops = 2 * 9 * rows * span * channels * channels
    cells = tile_rows * lax.axis_size("sy") * cols * lax.axis_size("sx")
    targets = [half_of((tm + offset) % slabs, sy) for offset in range(1, slabs)]
    tall, wide = lax.axis_size("sy"), lax.axis_size("sx")
    diagonal = [(sy + dy, sx + dx) for dy in (-1, 1) for dx in (-1, 1)]
    corners = [jnp.clip(y, 0, tall - 1) * wide + jnp.clip(x, 0, wide - 1) for y, x in diagonal]
    origins = [half_of((tm - offset + slabs) % slabs, sy) for offset in range(1, slabs)]
    place = [half, sx % 2, tm, jnp.int32(rows)] + corners + targets + origins
    place = jnp.stack(place).astype(jnp.int32)
    flags = [(sy > 0) | (half > 0), (sy < tall - 1) | (half < slabs - 1), sx > 0, sx < wide - 1]
    flags += [(y >= 0) & (y < tall) & (x >= 0) & (x < wide) for y, x in diagonal]
    flags = jnp.stack(flags).astype(F32)
    turns = [bit_of("sx", 2), bit_of("sy", 1)]
    core = bit_of("sx", 1)
    halves = [
        side(jnp.where(core == 0, turns[0], turns[1])),
        side(jnp.where(core == 0, turns[1], turns[0])),
        side(bit_of("sy", 2)),
    ]
    held = slabs
    for _, bit in axis_bits(("tm",))[::-1]:
        held //= 2
        halves.append(side(bit_of("tm", bit), held))
    cut = rows // 2
    place, flags, halves, latent_init = lax.optimization_barrier((place, flags, halves, latent_init))

    def shifted(offset):
        return [(i, (i + offset) % slabs) for i in range(slabs)]

    tiles_axes = ("sy", "sx")
    tile_devices = lax.axis_size(tiles_axes)
    sent_shape = (slabs - 1, steps_here, rows, cols, channels)
    end_shape, col_shape = ((2, cols, channels), F32), ((2, tile_rows, channels), F32)
    part_rows = CORNERS + 8 * (lanes // LANES)
    moments, table, low_rows, high_rows, first_cols, last_cols, leaving = call(
        functools.partial(start_kernel, group),
        [((tile_devices, part_rows, LANES), F32), ((4, steps_here, lanes), F32)]
        + [end_shape, end_shape, col_shape, col_shape, (sent_shape, BF16)],
        [pltpu.SemaphoreType.DMA((slabs - 1,))],
        10**6,
        smem=[step_index, place, coef_state, coef_drift, coef_noise],
        load=[latent_init, reward_grad, time_table.T, norm_gain],
        hbm=[step_noise],
        grant=WHOLE_BYTES,
    )

    def to_slabs(pieces):
        if slabs == 2:
            return lax.ppermute(pieces, "tm", shifted(1))
        return jnp.stack([lax.ppermute(pieces[i], "tm", shifted(i + 1)) for i in range(slabs - 1)])

    down, up = chain("sy")
    right_way, left_way = chain("sx")
    low = lax.ppermute(low_rows, "sy", down)
    high = lax.ppermute(high_rows, "sy", up)
    left = lax.ppermute(last_cols, "sx", right_way)
    right = lax.ppermute(first_cols, "sx", left_way)
    other_tables = to_slabs(jnp.broadcast_to(table[None], (slabs - 1,) + table.shape))
    other_tables, leaving = lax.optimization_barrier((other_tables, leaving))
    others = to_slabs(leaving)
    parts1 = share(moments, tiles_axes)
    parts1, conv_weight = lax.optimization_barrier((parts1, conv_weight))
    (coefs,) = call(
        table_kernel, [((4, steps, lanes), F32)], [], 10**5, smem=[place], vmem=[table, other_tables],
        grant=SMALL_BYTES,
    )
    packed = ((9 * (lanes - LANES) + 5 * LANES, lanes), BF16)
    weight_out, weight_back = call(
        pack_weight_kernel, [packed, packed], [], 10**7, vmem=[conv_weight.reshape(9, channels, channels)],
    )

    even_shape = (rows + 2, (cols + 2) * steps, lanes)
    odd_shape = (rows + 2, span, lanes)
    field_shape = (rows, span, lanes)
    y_shape = (lanes // LANES, chunk_rows(rows, span) * span, LANES)
    row_shape = (lanes // LANES, span, LANES)
    noise_shape = (steps_here, rows, cols, channels)
    even_out, odd_out, field_out = (even_shape, BF16), (odd_shape, BF16), (field_shape, F32)
    edge_row, edge_col = ((1, span, lanes), F32), ((rows, steps, lanes), F32)
    noise_scratch = [(noise_shape, BF16)]
    even1, odd1, sides, first_row, last_row = call(
        functools.partial(edge_sweep_kernel, group, cells),
        [even_out, odd_out, ((2, 2, tile_rows + 2, lanes), F32), edge_row, edge_row],
        noise_scratch + [(row_shape, F32), (row_shape, F32), pltpu.SemaphoreType.DMA((1,))],
        conv_flops // 4,
        smem=[flags, place],
        vmem=[low, high, left, right, parts1, coefs, latent_init, others, weight_out],
        hbm=[step_noise],
    )
    down_rows, up_rows = row_chain()
    top = lax.ppermute(last_row, ("tm", "sy"), down_rows)
    bottom = lax.ppermute(first_row, ("tm", "sy"), up_rows)
    states, moments, first_col, last_col = call(
        functools.partial(inner_sweep_kernel, group),
        [field_out, ((2, steps, LANES), F32), edge_col, edge_col],
        noise_scratch + [(y_shape, F32), (row_shape, F32), pltpu.SemaphoreType.DMA((1,))],
        conv_flops,
        smem=[place],
        vmem=[first_row, last_row, even1, odd1, coefs, latent_init, others, weight_out],
        hbm=[step_noise],
    )

    def side_cols(args):
        top, bottom, first, last = args
        side_out = ((rows + 2, steps, lanes), F32)
        first, last = call(
            edge_kernel, [side_out, side_out], [], 10**5, vmem=[top, bottom, first, last], grant=SMALL_BYTES
        )
        return lax.ppermute(last, "sx", right_way), lax.ppermute(first, "sx", left_way)

    def act_gradient(first, count):
        def run(reward):
            (out,) = call(
                functools.partial(act_gradient_kernel, first),
                [((count, span, lanes), F32)],
                [((count + 2,) + even_shape[1:], BF16), ((count + 2,) + odd_shape[1:], BF16)],
                conv_flops // 4,
                smem=[place],
                vmem=[reward, low, high, sides, coefs, weight_back],
            )
            return out

        return run

    order = ("sx", "sy", "tm")
    quarter = max(1, rows // 4)
    pieces = [(at, min(quarter, rows - at)) for at in range(0, rows, quarter)]

    def cols_and_first(args):
        return side_cols(args[1:]), act_gradient(*pieces[0])(args[0])

    def d_act_work(piece):
        return lambda done: (act_gradient(*piece), reward_grad)

    moments2, (((left2, right2), d_first), *d_rest) = butterfly(
        moments,
        order,
        join_moments(float(rows * cols * group)),
        [lambda done: (cols_and_first, (reward_grad, top, bottom, first_col, last_col))]
        + [d_act_work(piece) for piece in pieces[1:]],
    )
    even2, odd2, d_norm, sums, norm = call(
        functools.partial(norm_gradient_kernel, group, cells),
        [even_out, odd_out, field_out, ((steps, LANES), F32), ((2, steps, lanes), F32)],
        [],
        40 * rows * span * lanes,
        smem=[flags, place],
        vmem=[moments2, top, bottom, left2, right2, coefs, reward_grad, states, d_first, *d_rest],
    )

    share_rows = channels // slabs
    tiles = 9 * (channels // LANES) + 6

    def late_weight(half):
        def run(reward):
            (out,) = call(
                functools.partial(late_weight_kernel, half),
                [((tiles // 2, channels, LANES), F32)],
                [],
                conv_flops // 2,
                smem=[place],
                vmem=[reward, coefs, even2, odd2],
            )
            return out

        return lambda done: (run, reward_grad)

    def second_sweep(first, count):
        out_shape = (slabs, steps_here, count, cols, channels)

        def run(args):
            base = list(args[1:])
            return call(
                functools.partial(second_sweep_kernel, first),
                [(step_noise.shape, F32, pltpu.HBM), ((slabs - 1,) + out_shape[1:], F32)],
                [(noise_shape, BF16), (y_shape, F32), (row_shape, F32), (out_shape, F32)]
                + [pltpu.SemaphoreType.DMA((1,)), pltpu.SemaphoreType.DMA((1,))],
                conv_flops // 2,
                smem=[place],
                vmem=[coefs, args[0], states, others, weight_out, even2, odd2],
                hbm=[step_noise] + base,
                aliases={9: 0} if base else None,
            )

        return run

    sums, (late_a, late_b, (base, leaving)) = butterfly(
        sums,
        ("tm", "sx", "sy"),
        join_sums,
        [
            late_weight(0),
            late_weight(1),
            lambda done: (second_sweep(0, cut), (latent_init,)),
        ],
    )
    landing = to_slabs(leaving.astype(F16))

    payload = ((slabs, tiles // 2, share_rows, LANES), F32)
    up_shape = ((channels, rows * span), BF16)
    sent, scales, up_t = call(
        functools.partial(sent_weight_kernel, group, cells),
        [payload, ((16, LANES), F32), up_shape],
        [(row_shape, F32), (row_shape, F32), ((rows * span, lanes), BF16)],
        conv_flops // 2,
        smem=[place],
        vmem=[states, norm, sums, coefs, d_norm, reward_grad, even1, odd1, late_a, late_b],
        size=10**6,
    )

    def kept_weight(args):
        (kept,) = call(
            kept_weight_kernel,
            [payload],
            [],
            conv_flops // 2,
            smem=[place],
            vmem=[args[0], coefs, scales, even1, odd1, late_a, late_b],
        )
        return kept

    sent, landing = lax.optimization_barrier((sent, landing))
    arrived, kept = beside(sent, "sx", 1, kept_weight, (up_t,))

    def land(part, trajectory, which):
        (trajectory,) = call(
            functools.partial(land_kernel, (0, cut)[which]),
            [(step_noise.shape, F32, pltpu.HBM)],
            [(part.shape, F32), pltpu.SemaphoreType.DMA((slabs - 1,))],
            10**6,
            smem=[place],
            vmem=[latent_init, part.astype(F32)],
            hbm=[trajectory],
            aliases={3: 0},
        )
        return trajectory

    own, other, trajectory = reduce_weights(
        kept,
        arrived,
        (latent_init, base),
        second_sweep(cut, rows - cut),
        lambda leaving: to_slabs(leaving.astype(F16)),
        land,
        landing,
        halves,
    )
    (grad,) = call(
        unpack_kernel, [((9, share_rows, channels), F32)], [], 10**6, smem=[place], vmem=[own, other, scales],
        grant=SMALL_BYTES,
    )
    return trajectory, grad.transpose(0, 2, 1).reshape(3, 3, channels, share_rows)


def solution(mesh):
    placed = (
        P("sy", "sx", None),
        P("tm", "sy", "sx", None),
        P("tm"),
        P("tm"),
        P("tm"),
        P("tm"),
        P(),
        P(),
        P(),
        P("sy", "sx", None),
    )
    return jax.shard_map(
        shards,
        mesh=mesh,
        in_specs=placed,
        out_specs=(P("tm", "sy", "sx", None), P(None, None, None, "tm")),
        check_vma=False,
    )
```

```python
import functools

import jax
import jax.numpy as jnp
from jax import lax
from jax.experimental import pallas as pl
from jax.experimental.pallas import tpu as pltpu
from jax.sharding import PartitionSpec as P

GROUPS = 32
EPSILON = 1e-05
LANES = 128
F32 = jnp.float32
BF16 = jnp.bfloat16
VMEM_BYTES = 16 * 1024 * 1024
SMALL_BYTES = 4 * 1024 * 1024
WHOLE_BYTES = 61 * 10**6


def axis_bits(axes):
    bits = []
    for axis in axes:
        step = 1
        while step < lax.axis_size(axis):
            bits.append((axis, step))
            step *= 2
    return bits


def swap(value, axis, bit):
    pairs = [(i, i ^ bit) for i in range(lax.axis_size(axis))]
    return lax.ppermute(value, axis, pairs)


def half_of(tm_index, sy_index):
    last = lax.axis_size("tm") - 1
    return jnp.where(sy_index % 2 == 0, tm_index, last - tm_index)


def share(copies, axes):
    return lax.all_to_all(copies, axes, 0, 0)


def beside(value, axis, bit, work, needs):
    value, needs = lax.optimization_barrier((value, needs))
    other = swap(value, axis, bit)
    return lax.optimization_barrier((other, work(needs)))


def butterfly(value, axes, join, works):
    results = []
    for i, (axis, bit) in enumerate(axis_bits(axes)):
        if i < len(works):
            other, result = beside(value, axis, bit, *works[i](results))
            results.append(result)
        else:
            other = swap(value, axis, bit)
        value = join(value, other, 2**i)
    return value, results


def join_moments(count):
    def join(mine, other, size):
        gap = mine[0] - other[0]
        mean = 0.5 * (mine[0] + other[0])
        return jnp.stack([mean, mine[1] + other[1] + gap * gap * (0.5 * count * size)])

    return join


def join_sums(mine, other, size):
    return mine + other


def chain(axis):
    count = lax.axis_size(axis)
    forward = [(i, i + 1) for i in range(count - 1)]
    return forward, [(b, a) for a, b in forward]


def row_chain():
    slabs, tiles = lax.axis_size("tm"), lax.axis_size("sy")
    order = []
    for sy in range(tiles):
        for half in range(slabs):
            tm = half if sy % 2 == 0 else slabs - 1 - half
            order.append(tm * tiles + sy)
    forward = list(zip(order[:-1], order[1:]))
    return forward, [(b, a) for a, b in forward]


def group_matrix(rows, cols, group, channel_dim, slot):
    channel = lax.broadcasted_iota(jnp.int32, (rows, cols), channel_dim)
    place = lax.broadcasted_iota(jnp.int32, (rows, cols), 1 - channel_dim)
    scale = (1 << 16) // group + 1
    same = ((channel * scale) >> 16) + slot * GROUPS == place
    return (same & (channel < GROUPS * group)).astype(F32)


def exact_dot(left, right):
    return jnp.dot(left, right, precision=lax.Precision.HIGHEST, preferred_element_type=F32)


def gather_groups(values, group, slot):
    return exact_dot(values, group_matrix(values.shape[1], LANES, group, 0, slot))


def spread_groups(values, lanes, group):
    return exact_dot(values, group_matrix(LANES, lanes, group, 1, 0))


def lane_slot(values, slot):
    if slot:
        values = pltpu.roll(values, LANES - slot * GROUPS, 1)
    lane = lax.broadcasted_iota(jnp.int32, values.shape, 1)
    return jnp.where(lane < GROUPS, values, 0.0)


def merged_moments(parts, total_count, lanes, group):
    devices = parts.shape[0]
    total = jnp.sum(parts, axis=0)
    center = lane_slot(total, 0) * (1.0 / devices)
    gap = parts - center[None]
    between = lane_slot(jnp.sum(gap * gap, axis=0), 0) * (total_count / devices)
    spread = (between + lane_slot(total, 1)) * (1.0 / total_count)
    inv = lane_slot(1.0 / jnp.sqrt(spread + EPSILON), 0)
    return spread_groups(center, lanes, group), spread_groups(inv, lanes, group)


def final_moments(moments_ref, count, lanes, group):
    center = lane_slot(moments_ref[0], 0)
    inv = lane_slot(1.0 / jnp.sqrt(moments_ref[1] * (1.0 / count) + EPSILON), 0)
    return spread_groups(center, lanes, group), spread_groups(inv, lanes, group)


def start_copies(pairs, sem):
    copies = [pltpu.make_async_copy(a, b, sem.at[i]) for i, (a, b) in enumerate(pairs)]
    for copy in copies:
        copy.start()
    return copies


def wait_copies(copies):
    for copy in copies:
        copy.wait()


def widen(x, lanes):
    return jnp.concatenate([x, jnp.zeros((x.shape[0], lanes - x.shape[1]), x.dtype)], axis=1)


def framed_row(tile_ref, low_ref, high_ref, sides_ref, part, half, rows, row, lanes):
    tall = tile_ref.shape[0]
    place = half * rows + row - 1
    inner = tile_ref[jnp.clip(place, 0, tall - 1)]
    inner = jnp.where(place < 0, low_ref[part], jnp.where(place >= tall, high_ref[part], inner))
    left = sides_ref[0, part, pl.ds(place + 1, 1), :]
    right = sides_ref[1, part, pl.ds(place + 1, 1), :]
    return jnp.concatenate([left, widen(inner, lanes), right], axis=0)


def noise_of(own_ref, others_ref, place_ref, k, row, lanes):
    steps_here = own_ref.shape[0]
    slabs = others_ref.shape[0] + 1
    slab, step = divmod(k, steps_here)
    offset = lax.rem(place_ref[2] - slab + slabs, slabs)
    mine = own_ref[step, row].astype(F32)
    other = others_ref[jnp.maximum(offset - 1, 0), step, row].astype(F32)
    return widen(jnp.where(offset == 0, mine, other), lanes)


CORNERS = 8


def start_kernel(
    group, ready, index_ref, place_ref, state_ref, drift_ref, noise_coef_ref, lat_ref, reward_ref,
    time_ref, gain_ref, noise_hbm, part_ref, table_ref, low_ref, high_ref, first_ref, last_ref, sent_ref, sem,
):
    others, steps, rows = sent_ref.shape[:3]
    copies = start_copies(
        [
            (noise_hbm.at[:, pl.ds(place_ref[8 + i] * rows, rows)], sent_ref.at[i])
            for i in range(others)
        ],
        sem,
    )
    loads = ready.args[0]
    wait_copies(loads[:2])
    tall, wide, channels = lat_ref.shape
    lanes = table_ref.shape[2]
    corners = []
    for part, ref in enumerate((lat_ref, reward_ref)):
        low_ref[part] = ref[tall - 1]
        high_ref[part] = ref[0]
        for row in range(tall):
            first_ref[part, row : row + 1] = ref[row, 0:1]
            last_ref[part, row : row + 1] = ref[row, wide - 1 : wide]
    for row in (0, tall - 1):
        for col in (0, wide - 1):
            for ref in (lat_ref, reward_ref):
                cell = widen(ref[row, col : col + 1], lanes)
                corners += [cell[:, at : at + LANES] for at in range(0, lanes, LANES)]
    x = lat_ref[...].reshape(tall * wide, channels)
    sums = jnp.broadcast_to(jnp.sum(x, axis=0, keepdims=True), (8, channels))
    mean = gather_groups(sums, group, 0) * (1.0 / (tall * wide * group))
    gap = x - spread_groups(mean, channels, group)[0:1]
    square = jnp.broadcast_to(jnp.sum(gap * gap, axis=0, keepdims=True), (8, channels))
    part = jnp.concatenate([mean + gather_groups(square, group, 1)] + corners, axis=0)
    part_ref[...] = jnp.broadcast_to(part[None], part_ref.shape)
    wait_copies(loads[2:])
    entries = time_ref.shape[1]
    which = lax.broadcasted_iota(jnp.int32, (entries, LANES), 0)
    line = lax.broadcasted_iota(jnp.int32, (entries, LANES), 1)
    hit = jnp.zeros((entries, LANES), F32)
    for k in range(steps):
        hit = jnp.where((line == k) & (which == index_ref[k]), 1.0, hit)
    embedded = jnp.transpose(exact_dot(time_ref[...], hit))[:8]
    modulate = widen(gain_ref[...][None, :] * (1.0 + embedded), lanes)
    table_ref[0] = modulate[:steps]
    for k in range(steps):
        for i, ref in enumerate((state_ref, drift_ref, noise_coef_ref)):
            table_ref[i + 1, k : k + 1] = jnp.full((1, lanes), ref[k], F32)
    wait_copies(copies)


def edge_kernel(ready, top_ref, bottom_ref, first_ref, last_ref, first_out, last_out):
    rows, steps, _ = first_ref.shape
    span = top_ref.shape[1]
    for out, ref, at in ((first_out, first_ref, 0), (last_out, last_ref, span - steps)):
        out[0] = top_ref[0, at : at + steps]
        out[1 : rows + 1] = ref[...]
        out[rows + 1] = bottom_ref[0, at : at + steps]


def table_kernel(ready, place_ref, own_ref, others_ref, out_ref):
    slabs = others_ref.shape[0] + 1
    kinds, steps, _ = own_ref.shape
    for offset in range(slabs):
        source = lax.rem(place_ref[2] - offset + slabs, slabs)
        for kind in range(kinds):
            rows = own_ref[kind] if offset == 0 else others_ref[offset - 1, kind]
            for k in range(steps):
                out_ref[kind, pl.ds(source * steps + k, 1), :] = rows[k : k + 1]


def packed_rows(taps, channels):
    whole = channels // LANES * LANES
    places = []
    for tap in range(taps):
        rest = taps * whole + tap // 2 * LANES + tap % 2 * (LANES // 2)
        places.append((tap * whole, rest))
    return whole, places


def pack_weight_kernel(ready, w_ref, out_ref, back_ref):
    taps, channels, _ = w_ref.shape
    lanes = out_ref.shape[1]
    whole, places = packed_rows(taps, channels)
    out_ref[...] = jnp.zeros(out_ref.shape, BF16)
    back_ref[...] = jnp.zeros(back_ref.shape, BF16)
    ready()
    for tap, (at, rest) in enumerate(places):
        for ref, value in ((out_ref, w_ref[tap]), (back_ref, jnp.transpose(w_ref[taps - 1 - tap]))):
            ref[at : at + whole, 0:channels] = value[:whole]
            ref[rest : rest + channels - whole, 0:channels] = value[whole:]


def half_turn(x):
    return pltpu.roll(x.astype(F32), LANES // 2, 1).astype(BF16)


def pair_rests(rests):
    pairs = []
    for i in range(0, len(rests), 2):
        pairs.append(rests[i] if i + 1 == len(rests) else rests[i] + half_turn(rests[i + 1]))
    return pairs


def convolve_rows(even_ref, odd_ref, w_ref, start, count, steps):
    span, lanes = odd_ref.shape[1:]
    parts = []
    for row_off in range(3):
        rows = pl.ds(start + row_off, count)
        parts.append(even_ref[rows, 0:span, :].reshape(count * span, lanes))
        parts.append(odd_ref[rows].reshape(count * span, lanes))
        parts.append(even_ref[rows, 2 * steps : 2 * steps + span, :].reshape(count * span, lanes))
    whole = lanes - LANES
    packed = [x[:, :whole] for x in parts] + pair_rests([x[:, whole:] for x in parts])
    return jnp.dot(jnp.concatenate(packed, axis=1), w_ref[...], preferred_element_type=F32)


def put_tiles(ref, value):
    for tile in range(ref.shape[0]):
        ref[tile] = value[:, tile * LANES : (tile + 1) * LANES]


def get_tiles(ref):
    return jnp.concatenate([ref[tile] for tile in range(ref.shape[0])], axis=1)


def get_step(ref, start, cols, steps):
    where = pl.ds(start, cols, stride=steps)
    return jnp.concatenate([ref[tile, where, :] for tile in range(ref.shape[0])], axis=1)


def put_step(ref, start, cols, steps, value):
    where = pl.ds(start, cols, stride=steps)
    for tile in range(ref.shape[0]):
        ref[tile, where, :] = value[:, tile * LANES : (tile + 1) * LANES]


def chunk_rows(rows, span):
    count = max(1, min(rows, 384 // span))
    while rows % count:
        count -= 1
    return count


def advance_row(row, at, half, rows, steps, lat_ref, noise, place_ref, coef_ref, y_ref, row_ref):
    lanes = row_ref.shape[0] * LANES
    cols = row_ref.shape[1] // steps
    own = widen(lat_ref[half * rows + row], lanes)
    run = jnp.zeros_like(own)
    for k in range(steps):
        put_step(row_ref, k, cols, steps, own + run)
        conv = get_step(y_ref, at + k, cols, steps)
        run = run + (
            coef_ref[1, k : k + 1] * own
            + coef_ref[2, k : k + 1] * (own + conv)
            + coef_ref[3, k : k + 1] * noise_of(*noise, place_ref, k, row, lanes)
        )
    return get_tiles(row_ref)


def edge_sweep_kernel(
    group, total_cells, ready, flag_ref, place_ref, low_ref, high_ref, left_ref, right_ref,
    parts_ref, coef_ref, lat_ref, others_ref, w_ref, noise_hbm,
    even_ref, odd_ref, sides_ref, first_row, last_row,
    noise_ref, y_ref, row_ref, sem,
):
    rows, span, lanes = odd_ref.shape
    rows = rows - 2
    steps = coef_ref.shape[1]
    cols = span // steps
    half = place_ref[0]
    tall = lat_ref.shape[0]
    own_noise = noise_hbm.at[:, pl.ds(half * rows, rows)]
    loads = start_copies([(own_noise, noise_ref)], sem)
    center, inv = merged_moments(parts_ref[:, :CORNERS], float(total_cells * group), lanes, group)
    center, inv = center[0:1], inv[0:1]
    pieces = lanes // LANES
    for side, ref in enumerate((left_ref, right_ref)):
        for part in range(2):
            sides_ref[side, part, 1 : tall + 1, :] = widen(ref[part], lanes)
            for end in range(2):
                at = CORNERS + ((3 - 2 * end - side) * 2 + part) * pieces
                device = place_ref[4 + 2 * end + side]
                cell = [parts_ref[device, at + i : at + i + 1, :] for i in range(pieces)]
                cell = jnp.concatenate(cell, axis=1) * flag_ref[4 + 2 * end + side]
                to = end * (tall + 1)
                sides_ref[side, part, to : to + 1, :] = cell
    ready()
    mod = coef_ref[0]

    def activate(row, _):
        field = framed_row(lat_ref, low_ref, high_ref, sides_ref, 0, half, rows, row, lanes)
        normal = (field - center) * inv
        pre = normal[:, None, :] * mod[None]
        act = pre / (1.0 + jnp.exp(-pre))
        keep = jnp.where(row == 0, flag_ref[0], jnp.where(row == rows + 1, flag_ref[1], 1.0))
        act = act * keep
        inner = act[1 : cols + 1]
        act = jnp.concatenate(
            [act[0:1] * flag_ref[2], inner, act[cols + 1 : cols + 2] * flag_ref[3]], axis=0
        )
        even_ref[row] = act.reshape((cols + 2) * steps, lanes).astype(BF16)
        odd_ref[row] = inner.reshape(span, lanes).astype(BF16)
        return 0

    lax.fori_loop(0, rows + 2, activate, 0)
    wait_copies(loads)
    for row, out in ((0, first_row), (rows - 1, last_row)):
        put_tiles(y_ref, convolve_rows(even_ref, odd_ref, w_ref, row, 1, steps))
        noise = (noise_ref, others_ref)
        out[0] = advance_row(row, 0, half, rows, steps, lat_ref, noise, place_ref, coef_ref, y_ref, row_ref)


def inner_sweep_kernel(
    group, ready, place_ref, first_row, last_row, even_ref, odd_ref, coef_ref, lat_ref, others_ref, w_ref,
    noise_hbm, states_ref, moment_ref, first_col, last_col, noise_ref, y_ref, row_ref, sem,
):
    rows, span, lanes = states_ref.shape
    steps = coef_ref.shape[1]
    cols = span // steps
    half = place_ref[0]
    own_noise = noise_hbm.at[:, pl.ds(half * rows, rows)]
    loads = start_copies([(own_noise, noise_ref)], sem)
    states_ref[0] = first_row[0]
    states_ref[rows - 1] = last_row[0]
    wait_copies(loads)
    count = chunk_rows(max(rows - 2, 1), span)

    def sweep(chunk, _):
        start = 1 + chunk * count
        put_tiles(y_ref, convolve_rows(even_ref, odd_ref, w_ref, start, count, steps))
        for inner in range(count):
            states_ref[start + inner] = advance_row(
                start + inner, inner * span, half, rows, steps, lat_ref, (noise_ref, others_ref),
                place_ref, coef_ref, y_ref, row_ref,
            )
        return 0

    lax.fori_loop(0, (rows - 2) // count, sweep, 0)
    zero = jnp.zeros((steps, lanes), F32)

    def add(row, total):
        return total + jnp.sum(states_ref[row].reshape(cols, steps, lanes), axis=0)

    mean = gather_groups(lax.fori_loop(0, rows, add, zero), group, 0) * (1.0 / (rows * cols * group))
    mean_here = spread_groups(mean, lanes, group)

    def squares(row, total):
        gap = states_ref[row].reshape(cols, steps, lanes) - mean_here[None]
        return total + jnp.sum(gap * gap, axis=0)

    moment_ref[0] = mean
    moment_ref[1] = gather_groups(lax.fori_loop(0, rows, squares, zero), group, 0)
    first_col[...] = states_ref[:, 0:steps]
    last_col[...] = states_ref[:, span - steps :]


def act_gradient_kernel(
    first, ready, place_ref, reward_ref, low_ref, high_ref, sides_ref, coef_ref, w_ref,
    out_ref, even_ref, odd_ref,
):
    rows, span, lanes = out_ref.shape
    steps = coef_ref.shape[1]
    cols = span // steps
    drift = coef_ref[2]

    def scale(row, _):
        field = framed_row(
            reward_ref, low_ref, high_ref, sides_ref, 1, place_ref[0], place_ref[3], row + first, lanes
        )
        up = field[:, None, :] * drift[None]
        even_ref[row] = up.reshape((cols + 2) * steps, lanes).astype(BF16)
        odd_ref[row] = up[1 : cols + 1].reshape(span, lanes).astype(BF16)
        return 0

    lax.fori_loop(0, rows + 2, scale, 0)
    count = chunk_rows(rows, span)

    def sweep(chunk, _):
        start = chunk * count
        out = convolve_rows(even_ref, odd_ref, w_ref, start, count, steps)
        out_ref[pl.ds(start, count)] = out.reshape(count, span, lanes)
        return 0

    lax.fori_loop(0, rows // count, sweep, 0)


def norm_gradient_kernel(
    group, total_cells, ready, flag_ref, place_ref, moments_ref, top_ref, bottom_ref, left_ref, right_ref,
    coef_ref, reward_ref, states_ref, *refs
):
    *d_act_refs, even_ref, odd_ref, d_norm_ref, sum_ref, norm_ref = refs
    rows, span, lanes = states_ref.shape
    steps = coef_ref.shape[1]
    cols = span // steps
    center, inv = final_moments(moments_ref, float(total_cells * group), lanes, group)
    norm_ref[0] = center
    norm_ref[1] = inv
    mod = coef_ref[0]

    def activate(at, inner, keep):
        field = jnp.concatenate(
            [left_ref[at][None], inner.reshape(cols, steps, lanes), right_ref[at][None]], axis=0
        )
        normal = (field - center[None]) * inv[None]
        pre = normal * mod[None]
        sig = 1.0 / (1.0 + jnp.exp(-pre))
        act = pre * sig
        if keep is not None:
            act = act * keep
        middle = act[1 : cols + 1]
        odd_ref[at] = middle.reshape(span, lanes).astype(BF16)
        act = jnp.concatenate(
            [act[0:1] * flag_ref[2], middle, act[cols + 1 : cols + 2] * flag_ref[3]], axis=0
        )
        even_ref[at] = act.reshape((cols + 2) * steps, lanes).astype(BF16)
        return [x[1 : cols + 1] for x in (normal, pre, sig)]

    activate(0, top_ref[0], flag_ref[0])
    activate(rows + 1, bottom_ref[0], flag_ref[1])

    def one(d_act_ref, first, index, sums):
        plain, cross, square = sums
        row = index + first
        normal, pre, sig = activate(row + 1, states_ref[row], None)
        slope = sig * (1.0 + pre * (1.0 - sig))
        d_norm = d_act_ref[index].reshape(cols, steps, lanes) * slope * mod[None]
        d_norm_ref[row] = d_norm.reshape(span, lanes)
        return (
            plain + jnp.sum(d_norm, axis=0),
            cross + jnp.sum(d_norm * normal, axis=0),
            square + jnp.sum(d_norm * d_norm, axis=0),
        )

    zero = jnp.zeros((steps, lanes), F32)
    sums = (zero, zero, zero)
    first = 0
    for d_act_ref in d_act_refs:
        count = d_act_ref.shape[0]
        sums = lax.fori_loop(0, count, functools.partial(one, d_act_ref, first), sums)
        first += count
    plain, cross, square = sums
    channels = reward_ref.shape[2]
    reward = reward_ref[pl.ds(place_ref[0] * rows, rows)].reshape(rows * cols, channels)
    reward = jnp.broadcast_to(jnp.sum(reward * reward, axis=0, keepdims=True), (steps, channels))
    sum_ref[...] = (
        gather_groups(plain, group, 0)
        + gather_groups(cross, group, 1)
        + gather_groups(square, group, 2)
        + gather_groups(reward, group, 3)
    )


def second_sweep_kernel(
    first, ready, place_ref, coef_ref, lat_ref, states_ref, others_ref, w_ref, even_ref, odd_ref, noise_hbm, *refs
):
    kept_hbm, sent_ref, noise_ref, y_ref, row_ref, out_ref, sem, out_sem = refs[-8:]
    all_rows, span, lanes = states_ref.shape
    slabs, steps_here, rows, cols, channels = out_ref.shape
    steps = slabs * steps_here
    half = place_ref[0]
    own_noise = noise_hbm.at[:, pl.ds(half * all_rows, all_rows)]
    wait_copies(start_copies([(own_noise, noise_ref)], sem))
    count = chunk_rows(rows, span)

    def sweep(chunk, _):
        start = chunk * count
        put_tiles(y_ref, convolve_rows(even_ref, odd_ref, w_ref, first + start, count, steps))
        for inner in range(count):
            row = first + start + inner
            own = widen(lat_ref[half * all_rows + row], lanes)
            put_tiles(row_ref, states_ref[row])
            run = jnp.zeros_like(own)
            for k in range(steps):
                conv = get_step(y_ref, inner * span + k, cols, steps)
                state = get_step(row_ref, k, cols, steps)
                run = run + (
                    coef_ref[1, k : k + 1] * state
                    + coef_ref[2, k : k + 1] * (state + conv)
                    + coef_ref[3, k : k + 1] * noise_of(noise_ref, others_ref, place_ref, k, row, lanes)
                )
                out_ref[k // steps_here, k % steps_here, start + inner] = run[:, :channels]
        return 0

    lax.fori_loop(0, rows // count, sweep, 0)
    for offset in range(1, slabs):
        sent_ref[offset - 1] = out_ref[lax.rem(place_ref[2] + offset, slabs)] * 0.125
    mine = place_ref[2]

    def complete(row, _):
        own = lat_ref[half * all_rows + first + row]
        for k in range(steps_here):
            out_ref[mine, k, row] = own + out_ref[mine, k, row]
        return 0

    lax.fori_loop(0, rows, complete, 0)
    pairs = [(out_ref.at[mine], kept_hbm.at[:, pl.ds(half * all_rows + first, rows)])]
    wait_copies(start_copies(pairs, out_sem))


def land_kernel(first, ready, place_ref, lat_ref, part_ref, base_hbm, out_hbm, hold_ref, sem):
    others, steps, count = part_ref.shape[:3]
    copies = []
    for i in range(others):
        at = place_ref[8 + others + i] * place_ref[3] + first

        def add(row, _):
            own = lat_ref[at + row]
            for k in range(steps):
                hold_ref[i, k, row] = own + 8.0 * part_ref[i, k, row]
            return 0

        lax.fori_loop(0, count, add, 0)
        copies.append(pltpu.make_async_copy(hold_ref.at[i], out_hbm.at[:, pl.ds(at, count)], sem.at[i]))
        copies[-1].start()
    wait_copies(copies)


def weight_terms(half, up_t, even_ref, odd_ref, steps, put):
    rows = odd_ref.shape[0] - 2
    span, lanes = odd_ref.shape[1:]
    whole = lanes - LANES

    def window(tap, first, last):
        row_off, col_off = divmod(tap, 3)
        if col_off == 1:
            part = odd_ref[row_off : row_off + rows, :, first:last]
        else:
            at = col_off * steps
            part = even_ref[row_off : row_off + rows, at : at + span, first:last]
        return part.reshape(rows * span, last - first)

    def emit(tile, part):
        term = jnp.dot(up_t, part, preferred_element_type=F32)
        for piece in range(part.shape[1] // LANES):
            put(tile + piece, term[:, piece * LANES : (piece + 1) * LANES])

    for i, tap in enumerate(range(6, 9) if half else range(0, 6)):
        emit(i * whole // LANES, window(tap, 0, whole))
    if half:
        rests = pair_rests([window(tap, whole, lanes) for tap in range(9)])
        emit(3 * whole // LANES, jnp.concatenate(rests, axis=1))
        put(3 * whole // LANES + 5, jnp.zeros((up_t.shape[0], LANES), F32))


def late_weight_kernel(half, ready, place_ref, reward_ref, coef_ref, even_ref, odd_ref, out_ref):
    rows, span, lanes = odd_ref.shape
    rows = rows - 2
    steps = coef_ref.shape[1]
    cols = span // steps
    channels = out_ref.shape[1]
    reward = reward_ref[pl.ds(place_ref[0] * rows, rows)].reshape(rows * cols, channels)
    up = widen(reward, lanes)[:, None, :] * coef_ref[2][None]
    up = up.reshape(rows * span, lanes).astype(BF16)

    def put(tile, value):
        out_ref[tile] = value

    weight_terms(half, jnp.transpose(up)[:channels], even_ref, odd_ref, steps, put)


def safe_scale(total, norm, mod, state_coef, drift_coef, cells, group):
    def whole(slot):
        return jnp.sqrt(jnp.sum(lane_slot(total, slot), axis=1, keepdims=True))

    gradient, reward = whole(2), whole(3)
    top_inv = jnp.max(norm, axis=1, keepdims=True)
    top_mod = jnp.max(jnp.abs(mod), axis=1, keepdims=True)
    state, drift = jnp.abs(state_coef[:, 0:1]), jnp.abs(drift_coef[:, 0:1])
    through = jnp.sum((state + drift) * reward + top_inv * gradient, axis=0, keepdims=True)
    field = top_mod * drift * (float(cells * group) ** 0.5)
    bound = jnp.sum(field * (reward + through), axis=0, keepdims=True) * 1.1
    power = jnp.clip(jnp.floor(jnp.log2(32768.0 / jnp.maximum(bound, 1e-30))), -60.0, 60.0)
    scale = jnp.ones_like(power)
    for bit in (32, 16, 8, 4, 2, 1):
        size = jnp.abs(power)
        has = jnp.floor(size / bit) - 2.0 * jnp.floor(size / (2 * bit)) > 0.5
        step = jnp.where(power > 0, 2.0**bit, 2.0**-bit)
        scale = jnp.where(has, scale * step, scale)
    return scale


def half_gradient(half, up_t, late_ref, scale, even_ref, odd_ref, steps, out_ref):
    slabs, _, share_rows, _ = out_ref.shape

    def put(tile, value):
        value = (value + late_ref[tile]) * scale
        for slab in range(slabs):
            out_ref[slab, tile] = value[slab * share_rows : (slab + 1) * share_rows]

    weight_terms(half, up_t, even_ref, odd_ref, steps, put)


def kept_weight_kernel(
    ready, place_ref, up_ref, coef_ref, scale_ref, even_ref, odd_ref, late_a_ref, late_b_ref, out_ref
):
    for half, late_ref in enumerate((late_a_ref, late_b_ref)):

        @pl.when(place_ref[1] == half)
        def _():
            scale, steps = scale_ref[0:1], coef_ref.shape[1]
            half_gradient(half, up_ref[...], late_ref, scale, even_ref, odd_ref, steps, out_ref)


def sent_weight_kernel(
    group, cells, ready, place_ref, states_ref, norm_ref, sums_ref, coef_ref,
    d_norm_ref, reward_ref, even_ref, odd_ref, late_a_ref, late_b_ref,
    out_ref, scale_ref, up_t_ref, d_ref, adj_ref, up_ref,
):
    rows, span, lanes = states_ref.shape
    steps = coef_ref.shape[1]
    cols = span // steps
    center, inv = norm_ref[0], norm_ref[1]
    total = sums_ref[...]
    count = 1.0 / (cells * group)
    plain = spread_groups(lane_slot(total, 0) * count, lanes, group)
    cross = spread_groups(lane_slot(total, 1) * count, lanes, group)
    scale = safe_scale(total, inv, coef_ref[0], coef_ref[1], coef_ref[2], cells, group)
    scale_ref[0:8] = jnp.broadcast_to(scale, (8, LANES))
    scale_ref[8:16] = jnp.broadcast_to(1.0 / scale, (8, LANES))

    def one(row, _):
        normal = (states_ref[row].reshape(cols, steps, lanes) - center[None]) * inv[None]
        d_norm = d_norm_ref[row].reshape(cols, steps, lanes)
        d_group = (d_norm - plain[None] - normal * cross[None]) * inv[None]
        put_tiles(d_ref, d_group.reshape(span, lanes))
        reward = widen(reward_ref[place_ref[0] * rows + row], lanes)
        run = jnp.zeros_like(reward)
        for k in range(steps - 1, -1, -1):
            drift = coef_ref[2, k : k + 1]
            put_step(adj_ref, k, cols, steps, drift * run)
            d_state = drift * reward + get_step(d_ref, k, cols, steps)
            run = run + (coef_ref[1, k : k + 1] * reward + d_state)
        up_ref[pl.ds(pl.multiple_of(row * span, 16), span), :] = get_tiles(adj_ref).astype(BF16)
        return 0

    lax.fori_loop(0, rows, one, 0)
    up_t_ref[...] = jnp.transpose(up_ref[...])[: up_t_ref.shape[0]]
    for half, late_ref in enumerate((late_a_ref, late_b_ref)):

        @pl.when(place_ref[1] != half)
        def _():
            half_gradient(half, up_t_ref[...], late_ref, scale, even_ref, odd_ref, steps, out_ref)


def unpack_kernel(ready, place_ref, own_ref, other_ref, scale_ref, out_ref):
    whole = out_ref.shape[2] // LANES
    half = LANES // 2
    scale = scale_ref[8:9]
    tiles = own_ref.shape[0]
    first = place_ref[1] == 0

    def tile(index):
        low, at = index < tiles, index % tiles
        mine, other = (own_ref[at], other_ref[at]) if low else (other_ref[at], own_ref[at])
        return jnp.where(first, mine, other) * scale

    for tap in range(9):
        for piece in range(whole):
            at = piece * LANES
            out_ref[tap, :, at : at + LANES] = tile(tap * whole + piece)
        rest = tile(9 * whole + tap // 2)
        if tap % 2:
            rest = pltpu.roll(rest, half, 1)
        out_ref[tap, :, whole * LANES :] = rest[:, :half]


def call(
    kernel, outs, scratch, flops, smem=(), vmem=(), load=(), hbm=(), grant=VMEM_BYTES, aliases=None, size=None
):
    args = [*smem, *vmem, *load, *hbm]
    counts = [len(smem) + len(vmem), len(load), len(hbm) + len(outs) + len(scratch)]
    specs = [pl.BlockSpec(memory_space=pltpu.SMEM)] * len(smem)
    specs += [pl.BlockSpec(memory_space=pltpu.VMEM)] * len(vmem)
    specs += [pl.BlockSpec(memory_space=pltpu.HBM)] * (len(load) + len(hbm))
    shapes = [jax.ShapeDtypeStruct(out[0], out[1]) for out in outs]
    out_specs = [pl.BlockSpec(memory_space=out[2] if len(out) > 2 else pltpu.VMEM) for out in outs]
    if size is None:
        size = sum(a.size * a.dtype.itemsize for a in [*args, *shapes])
    buffers = [s if not isinstance(s, tuple) else pltpu.VMEM(*s) for s in scratch]
    buffers += [pltpu.VMEM(x.shape, x.dtype) for x in load]
    buffers += [pltpu.SemaphoreType.DMA((len(load),))] if load else []

    def body(*refs):
        first, wanted, rest = counts[0], counts[1], counts[2]
        sources = refs[first : first + wanted]
        middle = refs[first + wanted : first + wanted + rest]
        held = refs[first + wanted + rest : first + wanted + rest + wanted]
        copies = start_copies(list(zip(sources, held)), refs[-1]) if wanted else []
        kernel(functools.partial(wait_copies, copies), *refs[:first], *held, *middle)

    return pl.pallas_call(
        body,
        out_shape=shapes,
        in_specs=specs,
        out_specs=out_specs,
        scratch_shapes=buffers,
        input_output_aliases=aliases or {},
        compiler_params=pltpu.CompilerParams(vmem_limit_bytes=grant),
        cost_estimate=pl.CostEstimate(flops=flops, bytes_accessed=size, transcendentals=0),
    )(*args)


F16 = jnp.float16


def bit_of(axis, bit):
    return (lax.axis_index(axis) // bit) % 2


def side(which, count=1):
    unsigned = jnp.uint32
    return (which * count).astype(unsigned), ((1 - which) * count).astype(unsigned), which == 0


def part_of(value, start, count, dim):
    starts = [start if i == dim else jnp.uint32(0) for i in range(value.ndim)]
    sizes = [count if i == dim else size for i, size in enumerate(value.shape)]
    return lax.dynamic_slice(value, starts, sizes)


def half_of_dim(value, start, dim):
    return part_of(value, start, value.shape[dim] // 2, dim)


def half_sum(value, mine, send, dim):
    arrived = send(half_of_dim(value, mine[1], dim).astype(F16))
    return half_of_dim(value, mine[0], dim) + arrived.astype(value.dtype)


def both_halves(value, mine, send, dim):
    other = send(value)
    low = jnp.where(mine[2], value, other)
    high = jnp.where(mine[2], other, value)
    return jnp.concatenate([low, high], axis=dim)


def joint_sum(value, sides, dims, sends):
    def quarter(flips):
        part = value
        for mine, dim, flip in zip(sides, dims, flips):
            part = half_of_dim(part, mine[1 if flip else 0], dim)
        return part

    total = quarter((0, 0))
    arrived = [send(quarter(flips).astype(F16)) for flips, send in sends]
    for part in arrived:
        total = total + part.astype(value.dtype)
    return total


def joint_gather(value, sides, dims, sends):
    parts = {(0, 0): value}
    for flips, send in sends:
        parts[flips] = send(value)

    def order(first, second, mine, dim):
        low = jnp.where(mine[2], first, second)
        high = jnp.where(mine[2], second, first)
        return jnp.concatenate([low, high], axis=dim)

    rows = [order(parts[(0, flip)], parts[(1, flip)], sides[0], dims[0]) for flip in (0, 1)]
    return order(rows[0], rows[1], sides[1], dims[1])


FLIPS = ((1, 0), (0, 1), (1, 1))


def reduce_weights(kept, arrived, needs, sweep, travel, land, landing, sides):
    slabs, tiles, share_rows, lanes = kept.shape
    shape = (slabs, 2, tiles // 2, 2, 2, share_rows // 4, lanes)
    pieces = (kept.reshape(shape), arrived.reshape(shape))
    tall, wide = lax.axis_size("sy"), lax.axis_size("sx")

    def turned(sy, sx, turn):
        return (sy, sx ^ 2) if sx % 2 == turn else (sy ^ 1, sx)

    def send_tile(turn, flip_turn, flip_far):
        pairs = []
        for i in range(tall * wide):
            sy, sx = divmod(i, wide)
            to = turned(sy, sx, turn) if flip_turn else (sy, sx)
            to = (to[0] ^ 2, to[1]) if flip_far else to
            pairs.append((i, to[0] * wide + to[1]))
        return lambda value: lax.ppermute(value, ("sy", "sx"), pairs)

    def send_slab(bit, flip_slab, flip_far):
        pairs = []
        for i in range(slabs * tall):
            tm, sy = divmod(i, tall)
            pairs.append((i, (tm ^ (bit * flip_slab)) * tall + (sy ^ (2 * flip_far))))
        return lambda value: lax.ppermute(value, ("tm", "sy"), pairs)

    first, second, far, *slab_sides = sides

    def half(which):
        return sum(half_of_dim(x, which, 1) for x in pieces)

    outgoing, needs = lax.optimization_barrier((half(first[1]).astype(F16), needs))
    other = send_tile(0, 1, 0)(outgoing)
    other, (trajectory, leaving) = lax.optimization_barrier((other, sweep(needs)))
    value = half(first[0]) + other.astype(F32)
    trajectory = land(landing, trajectory, 0)
    landing = travel(leaving)
    value = half_sum(value, second, send_tile(1, 1, 0), 3)
    value, trajectory = lax.optimization_barrier((value, trajectory))
    bits = axis_bits(("tm",))[::-1]
    for (_, bit), mine in zip(bits[:-1], slab_sides):
        value = half_sum(value, mine, lambda x, bit=bit: swap(x, "tm", bit), 0)
    if bits:
        sends = [(flips, send_slab(bits[-1][1], *flips)) for flips in FLIPS]
        value = joint_sum(value, (slab_sides[-1], far), (0, 4), sends)
    else:
        value = half_sum(value, far, lambda x: swap(x, "sy", 2), 4)
    value = value.astype(F16)
    sends = [(flips, send_tile(1, flips[1], flips[0])) for flips in FLIPS]
    value = joint_gather(value, (far, second), (4, 3), sends)
    value = both_halves(value, first, send_tile(0, 1, 0), 1)
    value, landing = lax.optimization_barrier((value, landing))
    value = value.reshape(tiles, share_rows, lanes)
    other = swap(value, "sx", 1)
    other, trajectory = lax.optimization_barrier((other, land(landing, trajectory, 1)))
    return value.astype(F32), other.astype(F32), trajectory


def shards(
    latent_init, step_noise, coef_state, coef_drift, coef_noise, step_index, time_table, norm_gain,
    conv_weight, reward_grad,
):
    tile_rows, cols, channels = latent_init.shape
    group = channels // GROUPS
    lanes = -(-channels // LANES) * LANES
    extra = lanes - channels
    slabs = lax.axis_size("tm")
    steps_here = step_noise.shape[0]
    steps = steps_here * slabs
    rows = tile_rows // slabs
    span = steps * cols
    tm, sy, sx = (lax.axis_index(axis) for axis in ("tm", "sy", "sx"))
    half = half_of(tm, sy)
    conv_flops = 2 * 9 * rows * span * channels * channels
    cells = tile_rows * lax.axis_size("sy") * cols * lax.axis_size("sx")
    targets = [half_of((tm + offset) % slabs, sy) for offset in range(1, slabs)]
    tall, wide = lax.axis_size("sy"), lax.axis_size("sx")
    diagonal = [(sy + dy, sx + dx) for dy in (-1, 1) for dx in (-1, 1)]
    corners = [jnp.clip(y, 0, tall - 1) * wide + jnp.clip(x, 0, wide - 1) for y, x in diagonal]
    origins = [half_of((tm - offset + slabs) % slabs, sy) for offset in range(1, slabs)]
    place = [half, sx % 2, tm, jnp.int32(rows)] + corners + targets + origins
    place = jnp.stack(place).astype(jnp.int32)
    flags = [(sy > 0) | (half > 0), (sy < tall - 1) | (half < slabs - 1), sx > 0, sx < wide - 1]
    flags += [(y >= 0) & (y < tall) & (x >= 0) & (x < wide) for y, x in diagonal]
    flags = jnp.stack(flags).astype(F32)
    turns = [bit_of("sx", 2), bit_of("sy", 1)]
    core = bit_of("sx", 1)
    halves = [
        side(jnp.where(core == 0, turns[0], turns[1])),
        side(jnp.where(core == 0, turns[1], turns[0])),
        side(bit_of("sy", 2)),
    ]
    held = slabs
    for _, bit in axis_bits(("tm",))[::-1]:
        held //= 2
        halves.append(side(bit_of("tm", bit), held))
    cut = rows // 2
    place, flags, halves, latent_init = lax.optimization_barrier((place, flags, halves, latent_init))

    def shifted(offset):
        return [(i, (i + offset) % slabs) for i in range(slabs)]

    tiles_axes = ("sy", "sx")
    tile_devices = lax.axis_size(tiles_axes)
    sent_shape = (slabs - 1, steps_here, rows, cols, channels)
    end_shape, col_shape = ((2, cols, channels), F32), ((2, tile_rows, channels), F32)
    part_rows = CORNERS + 8 * (lanes // LANES)
    moments, table, low_rows, high_rows, first_cols, last_cols, leaving = call(
        functools.partial(start_kernel, group),
        [((tile_devices, part_rows, LANES), F32), ((4, steps_here, lanes), F32)]
        + [end_shape, end_shape, col_shape, col_shape, (sent_shape, BF16)],
        [pltpu.SemaphoreType.DMA((slabs - 1,))],
        10**6,
        smem=[step_index, place, coef_state, coef_drift, coef_noise],
        load=[latent_init, reward_grad, time_table.T, norm_gain],
        hbm=[step_noise],
        grant=WHOLE_BYTES,
    )

    def to_slabs(pieces):
        if slabs == 2:
            return lax.ppermute(pieces, "tm", shifted(1))
        return jnp.stack([lax.ppermute(pieces[i], "tm", shifted(i + 1)) for i in range(slabs - 1)])

    down, up = chain("sy")
    right_way, left_way = chain("sx")
    low = lax.ppermute(low_rows, "sy", down)
    high = lax.ppermute(high_rows, "sy", up)
    left = lax.ppermute(last_cols, "sx", right_way)
    right = lax.ppermute(first_cols, "sx", left_way)
    other_tables = to_slabs(jnp.broadcast_to(table[None], (slabs - 1,) + table.shape))
    other_tables, leaving = lax.optimization_barrier((other_tables, leaving))
    others = to_slabs(leaving)
    parts1 = share(moments, tiles_axes)
    parts1, conv_weight = lax.optimization_barrier((parts1, conv_weight))
    (coefs,) = call(
        table_kernel, [((4, steps, lanes), F32)], [], 10**5, smem=[place], vmem=[table, other_tables],
        grant=SMALL_BYTES,
    )
    packed = ((9 * (lanes - LANES) + 5 * LANES, lanes), BF16)
    weight_out, weight_back = call(
        pack_weight_kernel, [packed, packed], [], 10**7, vmem=[conv_weight.reshape(9, channels, channels)],
    )

    even_shape = (rows + 2, (cols + 2) * steps, lanes)
    odd_shape = (rows + 2, span, lanes)
    field_shape = (rows, span, lanes)
    y_shape = (lanes // LANES, chunk_rows(rows, span) * span, LANES)
    row_shape = (lanes // LANES, span, LANES)
    noise_shape = (steps_here, rows, cols, channels)
    even_out, odd_out, field_out = (even_shape, BF16), (odd_shape, BF16), (field_shape, F32)
    edge_row, edge_col = ((1, span, lanes), F32), ((rows, steps, lanes), F32)
    noise_scratch = [(noise_shape, BF16)]
    even1, odd1, sides, first_row, last_row = call(
        functools.partial(edge_sweep_kernel, group, cells),
        [even_out, odd_out, ((2, 2, tile_rows + 2, lanes), F32), edge_row, edge_row],
        noise_scratch + [(row_shape, F32), (row_shape, F32), pltpu.SemaphoreType.DMA((1,))],
        conv_flops // 4,
        smem=[flags, place],
        vmem=[low, high, left, right, parts1, coefs, latent_init, others, weight_out],
        hbm=[step_noise],
    )
    down_rows, up_rows = row_chain()
    top = lax.ppermute(last_row, ("tm", "sy"), down_rows)
    bottom = lax.ppermute(first_row, ("tm", "sy"), up_rows)
    states, moments, first_col, last_col = call(
        functools.partial(inner_sweep_kernel, group),
        [field_out, ((2, steps, LANES), F32), edge_col, edge_col],
        noise_scratch + [(y_shape, F32), (row_shape, F32), pltpu.SemaphoreType.DMA((1,))],
        conv_flops,
        smem=[place],
        vmem=[first_row, last_row, even1, odd1, coefs, latent_init, others, weight_out],
        hbm=[step_noise],
    )

    def side_cols(args):
        top, bottom, first, last = args
        side_out = ((rows + 2, steps, lanes), F32)
        first, last = call(
            edge_kernel, [side_out, side_out], [], 10**5, vmem=[top, bottom, first, last], grant=SMALL_BYTES
        )
        return lax.ppermute(last, "sx", right_way), lax.ppermute(first, "sx", left_way)

    def act_gradient(first, count):
        def run(reward):
            (out,) = call(
                functools.partial(act_gradient_kernel, first),
                [((count, span, lanes), F32)],
                [((count + 2,) + even_shape[1:], BF16), ((count + 2,) + odd_shape[1:], BF16)],
                conv_flops // 4,
                smem=[place],
                vmem=[reward, low, high, sides, coefs, weight_back],
            )
            return out

        return run

    order = ("sx", "sy", "tm")
    quarter = max(1, rows // 4)
    pieces = [(at, min(quarter, rows - at)) for at in range(0, rows, quarter)]

    def cols_and_first(args):
        return side_cols(args[1:]), act_gradient(*pieces[0])(args[0])

    def d_act_work(piece):
        return lambda done: (act_gradient(*piece), reward_grad)

    moments2, (((left2, right2), d_first), *d_rest) = butterfly(
        moments,
        order,
        join_moments(float(rows * cols * group)),
        [lambda done: (cols_and_first, (reward_grad, top, bottom, first_col, last_col))]
        + [d_act_work(piece) for piece in pieces[1:]],
    )
    even2, odd2, d_norm, sums, norm = call(
        functools.partial(norm_gradient_kernel, group, cells),
        [even_out, odd_out, field_out, ((steps, LANES), F32), ((2, steps, lanes), F32)],
        [],
        40 * rows * span * lanes,
        smem=[flags, place],
        vmem=[moments2, top, bottom, left2, right2, coefs, reward_grad, states, d_first, *d_rest],
    )

    share_rows = channels // slabs
    tiles = 9 * (channels // LANES) + 6

    def late_weight(half):
        def run(reward):
            (out,) = call(
                functools.partial(late_weight_kernel, half),
                [((tiles // 2, channels, LANES), F32)],
                [],
                conv_flops // 2,
                smem=[place],
                vmem=[reward, coefs, even2, odd2],
            )
            return out

        return lambda done: (run, reward_grad)

    def second_sweep(first, count):
        out_shape = (slabs, steps_here, count, cols, channels)

        def run(args):
            base = list(args[1:])
            return call(
                functools.partial(second_sweep_kernel, first),
                [(step_noise.shape, F32, pltpu.HBM), ((slabs - 1,) + out_shape[1:], F32)],
                [(noise_shape, BF16), (y_shape, F32), (row_shape, F32), (out_shape, F32)]
                + [pltpu.SemaphoreType.DMA((1,)), pltpu.SemaphoreType.DMA((1,))],
                conv_flops // 2,
                smem=[place],
                vmem=[coefs, args[0], states, others, weight_out, even2, odd2],
                hbm=[step_noise] + base,
                aliases={9: 0} if base else None,
            )

        return run

    sums, (late_a, late_b, (base, leaving)) = butterfly(
        sums,
        ("tm", "sx", "sy"),
        join_sums,
        [
            late_weight(0),
            late_weight(1),
            lambda done: (second_sweep(0, cut), (latent_init,)),
        ],
    )
    landing = to_slabs(leaving.astype(F16))

    payload = ((slabs, tiles // 2, share_rows, LANES), F32)
    up_shape = ((channels, rows * span), BF16)
    sent, scales, up_t = call(
        functools.partial(sent_weight_kernel, group, cells),
        [payload, ((16, LANES), F32), up_shape],
        [(row_shape, F32), (row_shape, F32), ((rows * span, lanes), BF16)],
        conv_flops // 2,
        smem=[place],
        vmem=[states, norm, sums, coefs, d_norm, reward_grad, even1, odd1, late_a, late_b],
        size=10**6,
    )

    def kept_weight(args):
        (kept,) = call(
            kept_weight_kernel,
            [payload],
            [],
            conv_flops // 2,
            smem=[place],
            vmem=[args[0], coefs, scales, even1, odd1, late_a, late_b],
        )
        return kept

    sent, landing = lax.optimization_barrier((sent, landing))
    arrived, kept = beside(sent, "sx", 1, kept_weight, (up_t,))

    def land(part, trajectory, which):
        (trajectory,) = call(
            functools.partial(land_kernel, (0, cut)[which]),
            [(step_noise.shape, F32, pltpu.HBM)],
            [(part.shape, F32), pltpu.SemaphoreType.DMA((slabs - 1,))],
            10**6,
            smem=[place],
            vmem=[latent_init, part.astype(F32)],
            hbm=[trajectory],
            aliases={3: 0},
        )
        return trajectory

    own, other, trajectory = reduce_weights(
        kept,
        arrived,
        (latent_init, base),
        second_sweep(cut, rows - cut),
        lambda leaving: to_slabs(leaving.astype(F16)),
        land,
        landing,
        halves,
    )
    (grad,) = call(
        unpack_kernel, [((9, share_rows, channels), F32)], [], 10**6, smem=[place], vmem=[own, other, scales],
        grant=SMALL_BYTES,
    )
    return trajectory, grad.transpose(0, 2, 1).reshape(3, 3, channels, share_rows)


def solution(mesh):
    placed = (
        P("sy", "sx", None),
        P("tm", "sy", "sx", None),
        P("tm"),
        P("tm"),
        P("tm"),
        P("tm"),
        P(),
        P(),
        P(),
        P("sy", "sx", None),
    )
    return jax.shard_map(
        shards,
        mesh=mesh,
        in_specs=placed,
        out_specs=(P("tm", "sy", "sx", None), P(None, None, None, "tm")),
        check_vma=False,
    )
```

```python
import functools

import jax
import jax.numpy as jnp
from jax import lax
from jax.experimental import pallas as pl
from jax.experimental.pallas import tpu as pltpu
from jax.sharding import PartitionSpec as P

GROUPS = 32
EPSILON = 1e-05
LANES = 128
F32 = jnp.float32
BF16 = jnp.bfloat16
VMEM_BYTES = 16 * 1024 * 1024
SMALL_BYTES = 4 * 1024 * 1024
WHOLE_BYTES = 61 * 10**6


def axis_bits(axes):
    bits = []
    for axis in axes:
        step = 1
        while step < lax.axis_size(axis):
            bits.append((axis, step))
            step *= 2
    return bits


def swap(value, axis, bit):
    pairs = [(i, i ^ bit) for i in range(lax.axis_size(axis))]
    return lax.ppermute(value, axis, pairs)


def half_of(tm_index, sy_index):
    last = lax.axis_size("tm") - 1
    return jnp.where(sy_index % 2 == 0, tm_index, last - tm_index)


def share(copies, axes):
    return lax.all_to_all(copies, axes, 0, 0)


def beside(value, axis, bit, work, needs):
    value, needs = lax.optimization_barrier((value, needs))
    other = swap(value, axis, bit)
    return lax.optimization_barrier((other, work(needs)))


def butterfly(value, axes, join, works):
    results = []
    for i, (axis, bit) in enumerate(axis_bits(axes)):
        if i < len(works):
            other, result = beside(value, axis, bit, *works[i](results))
            results.append(result)
        else:
            other = swap(value, axis, bit)
        value = join(value, other, 2**i)
    return value, results


def join_moments(count):
    def join(mine, other, size):
        gap = mine[0] - other[0]
        mean = 0.5 * (mine[0] + other[0])
        return jnp.stack([mean, mine[1] + other[1] + gap * gap * (0.5 * count * size)])

    return join


def join_sums(mine, other, size):
    return mine + other


def chain(axis):
    count = lax.axis_size(axis)
    forward = [(i, i + 1) for i in range(count - 1)]
    return forward, [(b, a) for a, b in forward]


def row_chain():
    slabs, tiles = lax.axis_size("tm"), lax.axis_size("sy")
    order = []
    for sy in range(tiles):
        for half in range(slabs):
            tm = half if sy % 2 == 0 else slabs - 1 - half
            order.append(tm * tiles + sy)
    forward = list(zip(order[:-1], order[1:]))
    return forward, [(b, a) for a, b in forward]


def group_matrix(rows, cols, group, channel_dim, slot):
    channel = lax.broadcasted_iota(jnp.int32, (rows, cols), channel_dim)
    place = lax.broadcasted_iota(jnp.int32, (rows, cols), 1 - channel_dim)
    scale = (1 << 16) // group + 1
    same = ((channel * scale) >> 16) + slot * GROUPS == place
    return (same & (channel < GROUPS * group)).astype(F32)


def exact_dot(left, right):
    return jnp.dot(left, right, precision=lax.Precision.HIGHEST, preferred_element_type=F32)


def gather_groups(values, group, slot):
    return exact_dot(values, group_matrix(values.shape[1], LANES, group, 0, slot))


def spread_groups(values, lanes, group):
    return exact_dot(values, group_matrix(LANES, lanes, group, 1, 0))


def lane_slot(values, slot):
    if slot:
        values = pltpu.roll(values, LANES - slot * GROUPS, 1)
    lane = lax.broadcasted_iota(jnp.int32, values.shape, 1)
    return jnp.where(lane < GROUPS, values, 0.0)


def merged_moments(parts, total_count, lanes, group):
    devices = parts.shape[0]
    total = jnp.sum(parts, axis=0)
    center = lane_slot(total, 0) * (1.0 / devices)
    gap = parts - center[None]
    between = lane_slot(jnp.sum(gap * gap, axis=0), 0) * (total_count / devices)
    spread = (between + lane_slot(total, 1)) * (1.0 / total_count)
    inv = lane_slot(1.0 / jnp.sqrt(spread + EPSILON), 0)
    return spread_groups(center, lanes, group), spread_groups(inv, lanes, group)


def final_moments(moments_ref, count, lanes, group):
    center = lane_slot(moments_ref[0], 0)
    inv = lane_slot(1.0 / jnp.sqrt(moments_ref[1] * (1.0 / count) + EPSILON), 0)
    return spread_groups(center, lanes, group), spread_groups(inv, lanes, group)


def start_copies(pairs, sem):
    copies = [pltpu.make_async_copy(a, b, sem.at[i]) for i, (a, b) in enumerate(pairs)]
    for copy in copies:
        copy.start()
    return copies


def wait_copies(copies):
    for copy in copies:
        copy.wait()


def widen(x, lanes):
    return jnp.concatenate([x, jnp.zeros((x.shape[0], lanes - x.shape[1]), x.dtype)], axis=1)


def framed_row(tile_ref, low_ref, high_ref, sides_ref, part, half, rows, row, lanes):
    tall = tile_ref.shape[0]
    place = half * rows + row - 1
    inner = tile_ref[jnp.clip(place, 0, tall - 1)]
    inner = jnp.where(place < 0, low_ref[part], jnp.where(place >= tall, high_ref[part], inner))
    left = sides_ref[0, part, pl.ds(place + 1, 1), :]
    right = sides_ref[1, part, pl.ds(place + 1, 1), :]
    return jnp.concatenate([left, widen(inner, lanes), right], axis=0)


def noise_of(own_ref, others_ref, place_ref, k, row, lanes):
    steps_here = own_ref.shape[0]
    slabs = others_ref.shape[0] + 1
    slab, step = divmod(k, steps_here)
    offset = lax.rem(place_ref[2] - slab + slabs, slabs)
    mine = own_ref[step, row].astype(F32)
    other = others_ref[jnp.maximum(offset - 1, 0), step, row].astype(F32)
    return widen(jnp.where(offset == 0, mine, other), lanes)


CORNERS = 8


def start_kernel(
    group, ready, index_ref, place_ref, state_ref, drift_ref, noise_coef_ref, lat_ref, reward_ref,
    time_ref, gain_ref, noise_hbm, part_ref, table_ref, low_ref, high_ref, first_ref, last_ref, sent_ref, sem,
):
    others, steps, rows = sent_ref.shape[:3]
    copies = start_copies(
        [
            (noise_hbm.at[:, pl.ds(place_ref[8 + i] * rows, rows)], sent_ref.at[i])
            for i in range(others)
        ],
        sem,
    )
    ready()
    tall, wide, channels = lat_ref.shape
    lanes = table_ref.shape[2]
    corners = []
    for part, ref in enumerate((lat_ref, reward_ref)):
        low_ref[part] = ref[tall - 1]
        high_ref[part] = ref[0]
        for row in range(tall):
            first_ref[part, row : row + 1] = ref[row, 0:1]
            last_ref[part, row : row + 1] = ref[row, wide - 1 : wide]
    for row in (0, tall - 1):
        for col in (0, wide - 1):
            for ref in (lat_ref, reward_ref):
                cell = widen(ref[row, col : col + 1], lanes)
                corners += [cell[:, at : at + LANES] for at in range(0, lanes, LANES)]
    entries = time_ref.shape[1]
    which = lax.broadcasted_iota(jnp.int32, (entries, LANES), 0)
    line = lax.broadcasted_iota(jnp.int32, (entries, LANES), 1)
    hit = jnp.zeros((entries, LANES), F32)
    for k in range(steps):
        hit = jnp.where((line == k) & (which == index_ref[k]), 1.0, hit)
    embedded = jnp.transpose(exact_dot(time_ref[...], hit))[:8]
    modulate = widen(gain_ref[...][None, :] * (1.0 + embedded), lanes)
    table_ref[0] = modulate[:steps]
    for k in range(steps):
        for i, ref in enumerate((state_ref, drift_ref, noise_coef_ref)):
            table_ref[i + 1, k : k + 1] = jnp.full((1, lanes), ref[k], F32)
    x = lat_ref[...].reshape(tall * wide, channels)
    sums = jnp.broadcast_to(jnp.sum(x, axis=0, keepdims=True), (8, channels))
    mean = gather_groups(sums, group, 0) * (1.0 / (tall * wide * group))
    gap = x - spread_groups(mean, channels, group)[0:1]
    square = jnp.broadcast_to(jnp.sum(gap * gap, axis=0, keepdims=True), (8, channels))
    part = jnp.concatenate([mean + gather_groups(square, group, 1)] + corners, axis=0)
    part_ref[...] = jnp.broadcast_to(part[None], part_ref.shape)
    wait_copies(copies)


def edge_kernel(ready, top_ref, bottom_ref, first_ref, last_ref, first_out, last_out):
    rows, steps, _ = first_ref.shape
    span = top_ref.shape[1]
    for out, ref, at in ((first_out, first_ref, 0), (last_out, last_ref, span - steps)):
        out[0] = top_ref[0, at : at + steps]
        out[1 : rows + 1] = ref[...]
        out[rows + 1] = bottom_ref[0, at : at + steps]


def table_kernel(ready, place_ref, own_ref, others_ref, out_ref):
    slabs = others_ref.shape[0] + 1
    kinds, steps, _ = own_ref.shape
    for offset in range(slabs):
        source = lax.rem(place_ref[2] - offset + slabs, slabs)
        for kind in range(kinds):
            rows = own_ref[kind] if offset == 0 else others_ref[offset - 1, kind]
            for k in range(steps):
                out_ref[kind, pl.ds(source * steps + k, 1), :] = rows[k : k + 1]


def packed_rows(taps, channels):
    whole = channels // LANES * LANES
    places = []
    for tap in range(taps):
        rest = taps * whole + tap // 2 * LANES + tap % 2 * (LANES // 2)
        places.append((tap * whole, rest))
    return whole, places


def pack_weight_kernel(ready, w_ref, out_ref, back_ref):
    taps, channels, _ = w_ref.shape
    lanes = out_ref.shape[1]
    whole, places = packed_rows(taps, channels)
    out_ref[...] = jnp.zeros(out_ref.shape, BF16)
    back_ref[...] = jnp.zeros(back_ref.shape, BF16)
    ready()
    for tap, (at, rest) in enumerate(places):
        for ref, value in ((out_ref, w_ref[tap]), (back_ref, jnp.transpose(w_ref[taps - 1 - tap]))):
            ref[at : at + whole, 0:channels] = value[:whole]
            ref[rest : rest + channels - whole, 0:channels] = value[whole:]


def half_turn(x):
    return pltpu.roll(x.astype(F32), LANES // 2, 1).astype(BF16)


def pair_rests(rests):
    pairs = []
    for i in range(0, len(rests), 2):
        pairs.append(rests[i] if i + 1 == len(rests) else rests[i] + half_turn(rests[i + 1]))
    return pairs


def convolve_rows(even_ref, odd_ref, w_ref, start, count, steps):
    span, lanes = odd_ref.shape[1:]
    parts = []
    for row_off in range(3):
        rows = pl.ds(start + row_off, count)
        parts.append(even_ref[rows, 0:span, :].reshape(count * span, lanes))
        parts.append(odd_ref[rows].reshape(count * span, lanes))
        parts.append(even_ref[rows, 2 * steps : 2 * steps + span, :].reshape(count * span, lanes))
    whole = lanes - LANES
    packed = [x[:, :whole] for x in parts] + pair_rests([x[:, whole:] for x in parts])
    return jnp.dot(jnp.concatenate(packed, axis=1), w_ref[...], preferred_element_type=F32)


def put_tiles(ref, value):
    for tile in range(ref.shape[0]):
        ref[tile] = value[:, tile * LANES : (tile + 1) * LANES]


def get_tiles(ref):
    return jnp.concatenate([ref[tile] for tile in range(ref.shape[0])], axis=1)


def get_step(ref, start, cols, steps):
    where = pl.ds(start, cols, stride=steps)
    return jnp.concatenate([ref[tile, where, :] for tile in range(ref.shape[0])], axis=1)


def put_step(ref, start, cols, steps, value):
    where = pl.ds(start, cols, stride=steps)
    for tile in range(ref.shape[0]):
        ref[tile, where, :] = value[:, tile * LANES : (tile + 1) * LANES]


def chunk_rows(rows, span):
    count = max(1, min(rows, 384 // span))
    while rows % count:
        count -= 1
    return count


def advance_row(row, at, half, rows, steps, lat_ref, noise, place_ref, coef_ref, y_ref, row_ref):
    lanes = row_ref.shape[0] * LANES
    cols = row_ref.shape[1] // steps
    own = widen(lat_ref[half * rows + row], lanes)
    run = jnp.zeros_like(own)
    for k in range(steps):
        put_step(row_ref, k, cols, steps, own + run)
        conv = get_step(y_ref, at + k, cols, steps)
        run = run + (
            coef_ref[1, k : k + 1] * own
            + coef_ref[2, k : k + 1] * (own + conv)
            + coef_ref[3, k : k + 1] * noise_of(*noise, place_ref, k, row, lanes)
        )
    return get_tiles(row_ref)


def edge_sweep_kernel(
    group, total_cells, ready, flag_ref, place_ref, low_ref, high_ref, left_ref, right_ref,
    parts_ref, coef_ref, lat_ref, others_ref, w_ref, noise_hbm,
    even_ref, odd_ref, sides_ref, first_row, last_row,
    noise_ref, y_ref, row_ref, sem,
):
    rows, span, lanes = odd_ref.shape
    rows = rows - 2
    steps = coef_ref.shape[1]
    cols = span // steps
    half = place_ref[0]
    tall = lat_ref.shape[0]
    own_noise = noise_hbm.at[:, pl.ds(half * rows, rows)]
    loads = start_copies([(own_noise, noise_ref)], sem)
    center, inv = merged_moments(parts_ref[:, :CORNERS], float(total_cells * group), lanes, group)
    center, inv = center[0:1], inv[0:1]
    pieces = lanes // LANES
    for side, ref in enumerate((left_ref, right_ref)):
        for part in range(2):
            sides_ref[side, part, 1 : tall + 1, :] = widen(ref[part], lanes)
            for end in range(2):
                at = CORNERS + ((3 - 2 * end - side) * 2 + part) * pieces
                device = place_ref[4 + 2 * end + side]
                cell = [parts_ref[device, at + i : at + i + 1, :] for i in range(pieces)]
                cell = jnp.concatenate(cell, axis=1) * flag_ref[4 + 2 * end + side]
                to = end * (tall + 1)
                sides_ref[side, part, to : to + 1, :] = cell
    ready()
    mod = coef_ref[0]

    def activate(row, _):
        field = framed_row(lat_ref, low_ref, high_ref, sides_ref, 0, half, rows, row, lanes)
        normal = (field - center) * inv
        pre = normal[:, None, :] * mod[None]
        act = pre / (1.0 + jnp.exp(-pre))
        keep = jnp.where(row == 0, flag_ref[0], jnp.where(row == rows + 1, flag_ref[1], 1.0))
        act = act * keep
        inner = act[1 : cols + 1]
        act = jnp.concatenate(
            [act[0:1] * flag_ref[2], inner, act[cols + 1 : cols + 2] * flag_ref[3]], axis=0
        )
        even_ref[row] = act.reshape((cols + 2) * steps, lanes).astype(BF16)
        odd_ref[row] = inner.reshape(span, lanes).astype(BF16)
        return 0

    lax.fori_loop(0, rows + 2, activate, 0)
    wait_copies(loads)
    for row, out in ((0, first_row), (rows - 1, last_row)):
        put_tiles(y_ref, convolve_rows(even_ref, odd_ref, w_ref, row, 1, steps))
        noise = (noise_ref, others_ref)
        out[0] = advance_row(row, 0, half, rows, steps, lat_ref, noise, place_ref, coef_ref, y_ref, row_ref)


def inner_sweep_kernel(
    group, ready, place_ref, first_row, last_row, even_ref, odd_ref, coef_ref, lat_ref, others_ref, w_ref,
    noise_hbm, states_ref, moment_ref, first_col, last_col, noise_ref, y_ref, row_ref, sem,
):
    rows, span, lanes = states_ref.shape
    steps = coef_ref.shape[1]
    cols = span // steps
    half = place_ref[0]
    own_noise = noise_hbm.at[:, pl.ds(half * rows, rows)]
    loads = start_copies([(own_noise, noise_ref)], sem)
    states_ref[0] = first_row[0]
    states_ref[rows - 1] = last_row[0]
    wait_copies(loads)
    count = chunk_rows(max(rows - 2, 1), span)

    def sweep(chunk, _):
        start = 1 + chunk * count
        put_tiles(y_ref, convolve_rows(even_ref, odd_ref, w_ref, start, count, steps))
        for inner in range(count):
            states_ref[start + inner] = advance_row(
                start + inner, inner * span, half, rows, steps, lat_ref, (noise_ref, others_ref),
                place_ref, coef_ref, y_ref, row_ref,
            )
        return 0

    lax.fori_loop(0, (rows - 2) // count, sweep, 0)
    zero = jnp.zeros((steps, lanes), F32)

    def add(row, total):
        return total + jnp.sum(states_ref[row].reshape(cols, steps, lanes), axis=0)

    mean = gather_groups(lax.fori_loop(0, rows, add, zero), group, 0) * (1.0 / (rows * cols * group))
    mean_here = spread_groups(mean, lanes, group)

    def squares(row, total):
        gap = states_ref[row].reshape(cols, steps, lanes) - mean_here[None]
        return total + jnp.sum(gap * gap, axis=0)

    moment_ref[0] = mean
    moment_ref[1] = gather_groups(lax.fori_loop(0, rows, squares, zero), group, 0)
    first_col[...] = states_ref[:, 0:steps]
    last_col[...] = states_ref[:, span - steps :]


def act_gradient_kernel(
    first, ready, place_ref, reward_ref, low_ref, high_ref, sides_ref, coef_ref, w_ref,
    out_ref, even_ref, odd_ref,
):
    rows, span, lanes = out_ref.shape
    steps = coef_ref.shape[1]
    cols = span // steps
    drift = coef_ref[2]

    def scale(row, _):
        field = framed_row(
            reward_ref, low_ref, high_ref, sides_ref, 1, place_ref[0], place_ref[3], row + first, lanes
        )
        up = field[:, None, :] * drift[None]
        even_ref[row] = up.reshape((cols + 2) * steps, lanes).astype(BF16)
        odd_ref[row] = up[1 : cols + 1].reshape(span, lanes).astype(BF16)
        return 0

    lax.fori_loop(0, rows + 2, scale, 0)
    count = chunk_rows(rows, span)

    def sweep(chunk, _):
        start = chunk * count
        out = convolve_rows(even_ref, odd_ref, w_ref, start, count, steps)
        out_ref[pl.ds(start, count)] = out.reshape(count, span, lanes)
        return 0

    lax.fori_loop(0, rows // count, sweep, 0)


def norm_gradient_kernel(
    group, total_cells, ready, flag_ref, place_ref, moments_ref, top_ref, bottom_ref, left_ref, right_ref,
    coef_ref, reward_ref, states_ref, *refs
):
    *d_act_refs, even_ref, odd_ref, d_norm_ref, sum_ref, norm_ref = refs
    rows, span, lanes = states_ref.shape
    steps = coef_ref.shape[1]
    cols = span // steps
    center, inv = final_moments(moments_ref, float(total_cells * group), lanes, group)
    norm_ref[0] = center
    norm_ref[1] = inv
    mod = coef_ref[0]

    def activate(at, inner, keep):
        field = jnp.concatenate(
            [left_ref[at][None], inner.reshape(cols, steps, lanes), right_ref[at][None]], axis=0
        )
        normal = (field - center[None]) * inv[None]
        pre = normal * mod[None]
        sig = 1.0 / (1.0 + jnp.exp(-pre))
        act = pre * sig
        if keep is not None:
            act = act * keep
        middle = act[1 : cols + 1]
        odd_ref[at] = middle.reshape(span, lanes).astype(BF16)
        act = jnp.concatenate(
            [act[0:1] * flag_ref[2], middle, act[cols + 1 : cols + 2] * flag_ref[3]], axis=0
        )
        even_ref[at] = act.reshape((cols + 2) * steps, lanes).astype(BF16)
        return [x[1 : cols + 1] for x in (normal, pre, sig)]

    activate(0, top_ref[0], flag_ref[0])
    activate(rows + 1, bottom_ref[0], flag_ref[1])

    def one(d_act_ref, first, index, sums):
        plain, cross, square = sums
        row = index + first
        normal, pre, sig = activate(row + 1, states_ref[row], None)
        slope = sig * (1.0 + pre * (1.0 - sig))
        d_norm = d_act_ref[index].reshape(cols, steps, lanes) * slope * mod[None]
        d_norm_ref[row] = d_norm.reshape(span, lanes)
        return (
            plain + jnp.sum(d_norm, axis=0),
            cross + jnp.sum(d_norm * normal, axis=0),
            square + jnp.sum(d_norm * d_norm, axis=0),
        )

    zero = jnp.zeros((steps, lanes), F32)
    sums = (zero, zero, zero)
    first = 0
    for d_act_ref in d_act_refs:
        count = d_act_ref.shape[0]
        sums = lax.fori_loop(0, count, functools.partial(one, d_act_ref, first), sums)
        first += count
    plain, cross, square = sums
    channels = reward_ref.shape[2]
    reward = reward_ref[pl.ds(place_ref[0] * rows, rows)].reshape(rows * cols, channels)
    reward = jnp.broadcast_to(jnp.sum(reward * reward, axis=0, keepdims=True), (steps, channels))
    sum_ref[...] = (
        gather_groups(plain, group, 0)
        + gather_groups(cross, group, 1)
        + gather_groups(square, group, 2)
        + gather_groups(reward, group, 3)
    )


def second_sweep_kernel(
    first, ready, place_ref, coef_ref, lat_ref, states_ref, others_ref, w_ref, even_ref, odd_ref, noise_hbm, *refs
):
    kept_hbm, sent_ref, noise_ref, y_ref, row_ref, out_ref, sem, out_sem = refs[-8:]
    all_rows, span, lanes = states_ref.shape
    slabs, steps_here, rows, cols, channels = out_ref.shape
    steps = slabs * steps_here
    half = place_ref[0]
    own_noise = noise_hbm.at[:, pl.ds(half * all_rows, all_rows)]
    wait_copies(start_copies([(own_noise, noise_ref)], sem))
    count = chunk_rows(rows, span)

    def sweep(chunk, _):
        start = chunk * count
        put_tiles(y_ref, convolve_rows(even_ref, odd_ref, w_ref, first + start, count, steps))
        for inner in range(count):
            row = first + start + inner
            own = widen(lat_ref[half * all_rows + row], lanes)
            put_tiles(row_ref, states_ref[row])
            run = jnp.zeros_like(own)
            for k in range(steps):
                conv = get_step(y_ref, inner * span + k, cols, steps)
                state = get_step(row_ref, k, cols, steps)
                run = run + (
                    coef_ref[1, k : k + 1] * state
                    + coef_ref[2, k : k + 1] * (state + conv)
                    + coef_ref[3, k : k + 1] * noise_of(noise_ref, others_ref, place_ref, k, row, lanes)
                )
                out_ref[k // steps_here, k % steps_here, start + inner] = run[:, :channels]
        return 0

    lax.fori_loop(0, rows // count, sweep, 0)
    for offset in range(1, slabs):
        sent_ref[offset - 1] = out_ref[lax.rem(place_ref[2] + offset, slabs)] * 0.125
    mine = place_ref[2]

    def complete(row, _):
        own = lat_ref[half * all_rows + first + row]
        for k in range(steps_here):
            out_ref[mine, k, row] = own + out_ref[mine, k, row]
        return 0

    lax.fori_loop(0, rows, complete, 0)
    pairs = [(out_ref.at[mine], kept_hbm.at[:, pl.ds(half * all_rows + first, rows)])]
    wait_copies(start_copies(pairs, out_sem))


def land_kernel(first, ready, place_ref, lat_ref, part_ref, base_hbm, out_hbm, hold_ref, sem):
    others, steps, count = part_ref.shape[:3]
    copies = []
    for i in range(others):
        at = place_ref[8 + others + i] * place_ref[3] + first

        def add(row, _):
            own = lat_ref[at + row]
            for k in range(steps):
                hold_ref[i, k, row] = own + 8.0 * part_ref[i, k, row]
            return 0

        lax.fori_loop(0, count, add, 0)
        copies.append(pltpu.make_async_copy(hold_ref.at[i], out_hbm.at[:, pl.ds(at, count)], sem.at[i]))
        copies[-1].start()
    wait_copies(copies)


def weight_terms(half, up_t, even_ref, odd_ref, steps, put):
    rows = odd_ref.shape[0] - 2
    span, lanes = odd_ref.shape[1:]
    whole = lanes - LANES

    def window(tap, first, last):
        row_off, col_off = divmod(tap, 3)
        if col_off == 1:
            part = odd_ref[row_off : row_off + rows, :, first:last]
        else:
            at = col_off * steps
            part = even_ref[row_off : row_off + rows, at : at + span, first:last]
        return part.reshape(rows * span, last - first)

    def emit(tile, part):
        term = jnp.dot(up_t, part, preferred_element_type=F32)
        for piece in range(part.shape[1] // LANES):
            put(tile + piece, term[:, piece * LANES : (piece + 1) * LANES])

    for i, tap in enumerate(range(6, 9) if half else range(0, 6)):
        emit(i * whole // LANES, window(tap, 0, whole))
    if half:
        rests = pair_rests([window(tap, whole, lanes) for tap in range(9)])
        emit(3 * whole // LANES, jnp.concatenate(rests, axis=1))
        put(3 * whole // LANES + 5, jnp.zeros((up_t.shape[0], LANES), F32))


def late_weight_kernel(half, ready, place_ref, reward_ref, coef_ref, even_ref, odd_ref, out_ref):
    rows, span, lanes = odd_ref.shape
    rows = rows - 2
    steps = coef_ref.shape[1]
    cols = span // steps
    channels = out_ref.shape[1]
    reward = reward_ref[pl.ds(place_ref[0] * rows, rows)].reshape(rows * cols, channels)
    up = widen(reward, lanes)[:, None, :] * coef_ref[2][None]
    up = up.reshape(rows * span, lanes).astype(BF16)

    def put(tile, value):
        out_ref[tile] = value

    weight_terms(half, jnp.transpose(up)[:channels], even_ref, odd_ref, steps, put)


def safe_scale(total, norm, mod, state_coef, drift_coef, cells, group):
    def whole(slot):
        return jnp.sqrt(jnp.sum(lane_slot(total, slot), axis=1, keepdims=True))

    gradient, reward = whole(2), whole(3)
    top_inv = jnp.max(norm, axis=1, keepdims=True)
    top_mod = jnp.max(jnp.abs(mod), axis=1, keepdims=True)
    state, drift = jnp.abs(state_coef[:, 0:1]), jnp.abs(drift_coef[:, 0:1])
    through = jnp.sum((state + drift) * reward + top_inv * gradient, axis=0, keepdims=True)
    field = top_mod * drift * (float(cells * group) ** 0.5)
    bound = jnp.sum(field * (reward + through), axis=0, keepdims=True) * 1.1
    power = jnp.clip(jnp.floor(jnp.log2(32768.0 / jnp.maximum(bound, 1e-30))), -60.0, 60.0)
    scale = jnp.ones_like(power)
    for bit in (32, 16, 8, 4, 2, 1):
        size = jnp.abs(power)
        has = jnp.floor(size / bit) - 2.0 * jnp.floor(size / (2 * bit)) > 0.5
        step = jnp.where(power > 0, 2.0**bit, 2.0**-bit)
        scale = jnp.where(has, scale * step, scale)
    return scale


def half_gradient(half, up_t, late_ref, scale, even_ref, odd_ref, steps, out_ref):
    slabs, _, share_rows, _ = out_ref.shape

    def put(tile, value):
        value = (value + late_ref[tile]) * scale
        for slab in range(slabs):
            out_ref[slab, tile] = value[slab * share_rows : (slab + 1) * share_rows]

    weight_terms(half, up_t, even_ref, odd_ref, steps, put)


def kept_weight_kernel(
    ready, place_ref, up_ref, coef_ref, scale_ref, even_ref, odd_ref, late_a_ref, late_b_ref, out_ref
):
    for half, late_ref in enumerate((late_a_ref, late_b_ref)):

        @pl.when(place_ref[1] == half)
        def _():
            scale, steps = scale_ref[0:1], coef_ref.shape[1]
            half_gradient(half, up_ref[...], late_ref, scale, even_ref, odd_ref, steps, out_ref)


def sent_weight_kernel(
    group, cells, ready, place_ref, states_ref, norm_ref, sums_ref, coef_ref,
    d_norm_ref, reward_ref, even_ref, odd_ref, late_a_ref, late_b_ref,
    out_ref, scale_ref, up_t_ref, d_ref, adj_ref, up_ref,
):
    rows, span, lanes = states_ref.shape
    steps = coef_ref.shape[1]
    cols = span // steps
    center, inv = norm_ref[0], norm_ref[1]
    total = sums_ref[...]
    count = 1.0 / (cells * group)
    plain = spread_groups(lane_slot(total, 0) * count, lanes, group)
    cross = spread_groups(lane_slot(total, 1) * count, lanes, group)
    scale = safe_scale(total, inv, coef_ref[0], coef_ref[1], coef_ref[2], cells, group)
    scale_ref[0:8] = jnp.broadcast_to(scale, (8, LANES))
    scale_ref[8:16] = jnp.broadcast_to(1.0 / scale, (8, LANES))

    def one(row, _):
        normal = (states_ref[row].reshape(cols, steps, lanes) - center[None]) * inv[None]
        d_norm = d_norm_ref[row].reshape(cols, steps, lanes)
        d_group = (d_norm - plain[None] - normal * cross[None]) * inv[None]
        put_tiles(d_ref, d_group.reshape(span, lanes))
        reward = widen(reward_ref[place_ref[0] * rows + row], lanes)
        run = jnp.zeros_like(reward)
        for k in range(steps - 1, -1, -1):
            drift = coef_ref[2, k : k + 1]
            put_step(adj_ref, k, cols, steps, drift * run)
            d_state = drift * reward + get_step(d_ref, k, cols, steps)
            run = run + (coef_ref[1, k : k + 1] * reward + d_state)
        up_ref[pl.ds(pl.multiple_of(row * span, 16), span), :] = get_tiles(adj_ref).astype(BF16)
        return 0

    lax.fori_loop(0, rows, one, 0)
    up_t_ref[...] = jnp.transpose(up_ref[...])[: up_t_ref.shape[0]]
    for half, late_ref in enumerate((late_a_ref, late_b_ref)):

        @pl.when(place_ref[1] != half)
        def _():
            half_gradient(half, up_t_ref[...], late_ref, scale, even_ref, odd_ref, steps, out_ref)


def unpack_kernel(ready, place_ref, own_ref, other_ref, scale_ref, out_ref):
    whole = out_ref.shape[2] // LANES
    half = LANES // 2
    scale = scale_ref[8:9]
    tiles = own_ref.shape[0]
    first = place_ref[1] == 0

    def tile(index):
        low, at = index < tiles, index % tiles
        mine, other = (own_ref[at], other_ref[at]) if low else (other_ref[at], own_ref[at])
        return jnp.where(first, mine, other) * scale

    for tap in range(9):
        for piece in range(whole):
            at = piece * LANES
            out_ref[tap, :, at : at + LANES] = tile(tap * whole + piece)
        rest = tile(9 * whole + tap // 2)
        if tap % 2:
            rest = pltpu.roll(rest, half, 1)
        out_ref[tap, :, whole * LANES :] = rest[:, :half]


def call(
    kernel, outs, scratch, flops, smem=(), vmem=(), load=(), hbm=(), grant=VMEM_BYTES, aliases=None, size=None
):
    args = [*smem, *vmem, *load, *hbm]
    counts = [len(smem) + len(vmem), len(load), len(hbm) + len(outs) + len(scratch)]
    specs = [pl.BlockSpec(memory_space=pltpu.SMEM)] * len(smem)
    specs += [pl.BlockSpec(memory_space=pltpu.VMEM)] * len(vmem)
    specs += [pl.BlockSpec(memory_space=pltpu.HBM)] * (len(load) + len(hbm))
    shapes = [jax.ShapeDtypeStruct(out[0], out[1]) for out in outs]
    out_specs = [pl.BlockSpec(memory_space=out[2] if len(out) > 2 else pltpu.VMEM) for out in outs]
    if size is None:
        size = sum(a.size * a.dtype.itemsize for a in [*args, *shapes])
    buffers = [s if not isinstance(s, tuple) else pltpu.VMEM(*s) for s in scratch]
    buffers += [pltpu.VMEM(x.shape, x.dtype) for x in load]
    buffers += [pltpu.SemaphoreType.DMA((len(load),))] if load else []

    def body(*refs):
        first, wanted, rest = counts[0], counts[1], counts[2]
        sources = refs[first : first + wanted]
        middle = refs[first + wanted : first + wanted + rest]
        held = refs[first + wanted + rest : first + wanted + rest + wanted]
        copies = start_copies(list(zip(sources, held)), refs[-1]) if wanted else []
        kernel(functools.partial(wait_copies, copies), *refs[:first], *held, *middle)

    return pl.pallas_call(
        body,
        out_shape=shapes,
        in_specs=specs,
        out_specs=out_specs,
        scratch_shapes=buffers,
        input_output_aliases=aliases or {},
        compiler_params=pltpu.CompilerParams(vmem_limit_bytes=grant),
        cost_estimate=pl.CostEstimate(flops=flops, bytes_accessed=size, transcendentals=0),
    )(*args)


F16 = jnp.float16


def bit_of(axis, bit):
    return (lax.axis_index(axis) // bit) % 2


def side(which, count=1):
    unsigned = jnp.uint32
    return (which * count).astype(unsigned), ((1 - which) * count).astype(unsigned), which == 0


def part_of(value, start, count, dim):
    starts = [start if i == dim else jnp.uint32(0) for i in range(value.ndim)]
    sizes = [count if i == dim else size for i, size in enumerate(value.shape)]
    return lax.dynamic_slice(value, starts, sizes)


def half_of_dim(value, start, dim):
    return part_of(value, start, value.shape[dim] // 2, dim)


def half_sum(value, mine, send, dim):
    arrived = send(half_of_dim(value, mine[1], dim).astype(F16))
    return half_of_dim(value, mine[0], dim) + arrived.astype(value.dtype)


def both_halves(value, mine, send, dim):
    other = send(value)
    low = jnp.where(mine[2], value, other)
    high = jnp.where(mine[2], other, value)
    return jnp.concatenate([low, high], axis=dim)


def joint_sum(value, sides, dims, sends):
    def quarter(flips):
        part = value
        for mine, dim, flip in zip(sides, dims, flips):
            part = half_of_dim(part, mine[1 if flip else 0], dim)
        return part

    total = quarter((0, 0))
    arrived = [send(quarter(flips).astype(F16)) for flips, send in sends]
    for part in arrived:
        total = total + part.astype(value.dtype)
    return total


def joint_gather(value, sides, dims, sends):
    parts = {(0, 0): value}
    for flips, send in sends:
        parts[flips] = send(value)

    def order(first, second, mine, dim):
        low = jnp.where(mine[2], first, second)
        high = jnp.where(mine[2], second, first)
        return jnp.concatenate([low, high], axis=dim)

    rows = [order(parts[(0, flip)], parts[(1, flip)], sides[0], dims[0]) for flip in (0, 1)]
    return order(rows[0], rows[1], sides[1], dims[1])


FLIPS = ((1, 0), (0, 1), (1, 1))


def reduce_weights(kept, arrived, needs, sweep, travel, land, landing, sides):
    slabs, tiles, share_rows, lanes = kept.shape
    shape = (slabs, 2, tiles // 2, 2, 2, share_rows // 4, lanes)
    pieces = (kept.reshape(shape), arrived.reshape(shape))
    tall, wide = lax.axis_size("sy"), lax.axis_size("sx")

    def turned(sy, sx, turn):
        return (sy, sx ^ 2) if sx % 2 == turn else (sy ^ 1, sx)

    def send_tile(turn, flip_turn, flip_far):
        pairs = []
        for i in range(tall * wide):
            sy, sx = divmod(i, wide)
            to = turned(sy, sx, turn) if flip_turn else (sy, sx)
            to = (to[0] ^ 2, to[1]) if flip_far else to
            pairs.append((i, to[0] * wide + to[1]))
        return lambda value: lax.ppermute(value, ("sy", "sx"), pairs)

    def send_slab(bit, flip_slab, flip_far):
        pairs = []
        for i in range(slabs * tall):
            tm, sy = divmod(i, tall)
            pairs.append((i, (tm ^ (bit * flip_slab)) * tall + (sy ^ (2 * flip_far))))
        return lambda value: lax.ppermute(value, ("tm", "sy"), pairs)

    first, second, far, *slab_sides = sides

    def half(which):
        return sum(half_of_dim(x, which, 1) for x in pieces)

    outgoing, needs = lax.optimization_barrier((half(first[1]).astype(F16), needs))
    other = send_tile(0, 1, 0)(outgoing)
    other, (trajectory, leaving) = lax.optimization_barrier((other, sweep(needs)))
    value = half(first[0]) + other.astype(F32)
    trajectory = land(landing, trajectory, 0)
    landing = travel(leaving)
    value = half_sum(value, second, send_tile(1, 1, 0), 3)
    value, trajectory = lax.optimization_barrier((value, trajectory))
    bits = axis_bits(("tm",))[::-1]
    for (_, bit), mine in zip(bits[:-1], slab_sides):
        value = half_sum(value, mine, lambda x, bit=bit: swap(x, "tm", bit), 0)
    if bits:
        sends = [(flips, send_slab(bits[-1][1], *flips)) for flips in FLIPS]
        value = joint_sum(value, (slab_sides[-1], far), (0, 4), sends)
    else:
        value = half_sum(value, far, lambda x: swap(x, "sy", 2), 4)
    value = value.astype(F16)
    sends = [(flips, send_tile(1, flips[1], flips[0])) for flips in FLIPS]
    value = joint_gather(value, (far, second), (4, 3), sends)
    value = both_halves(value, first, send_tile(0, 1, 0), 1)
    value, landing = lax.optimization_barrier((value, landing))
    value = value.reshape(tiles, share_rows, lanes)
    other = swap(value, "sx", 1)
    other, trajectory = lax.optimization_barrier((other, land(landing, trajectory, 1)))
    return value.astype(F32), other.astype(F32), trajectory


def shards(
    latent_init, step_noise, coef_state, coef_drift, coef_noise, step_index, time_table, norm_gain,
    conv_weight, reward_grad,
):
    tile_rows, cols, channels = latent_init.shape
    group = channels // GROUPS
    lanes = -(-channels // LANES) * LANES
    extra = lanes - channels
    slabs = lax.axis_size("tm")
    steps_here = step_noise.shape[0]
    steps = steps_here * slabs
    rows = tile_rows // slabs
    span = steps * cols
    tm, sy, sx = (lax.axis_index(axis) for axis in ("tm", "sy", "sx"))
    half = half_of(tm, sy)
    conv_flops = 2 * 9 * rows * span * channels * channels
    cells = tile_rows * lax.axis_size("sy") * cols * lax.axis_size("sx")
    targets = [half_of((tm + offset) % slabs, sy) for offset in range(1, slabs)]
    tall, wide = lax.axis_size("sy"), lax.axis_size("sx")
    diagonal = [(sy + dy, sx + dx) for dy in (-1, 1) for dx in (-1, 1)]
    corners = [jnp.clip(y, 0, tall - 1) * wide + jnp.clip(x, 0, wide - 1) for y, x in diagonal]
    origins = [half_of((tm - offset + slabs) % slabs, sy) for offset in range(1, slabs)]
    place = [half, sx % 2, tm, jnp.int32(rows)] + corners + targets + origins
    place = jnp.stack(place).astype(jnp.int32)
    flags = [(sy > 0) | (half > 0), (sy < tall - 1) | (half < slabs - 1), sx > 0, sx < wide - 1]
    flags += [(y >= 0) & (y < tall) & (x >= 0) & (x < wide) for y, x in diagonal]
    flags = jnp.stack(flags).astype(F32)
    turns = [bit_of("sx", 2), bit_of("sy", 1)]
    core = bit_of("sx", 1)
    halves = [
        side(jnp.where(core == 0, turns[0], turns[1])),
        side(jnp.where(core == 0, turns[1], turns[0])),
        side(bit_of("sy", 2)),
    ]
    held = slabs
    for _, bit in axis_bits(("tm",))[::-1]:
        held //= 2
        halves.append(side(bit_of("tm", bit), held))
    cut = max(1, rows // 4)
    place, flags, halves, latent_init = lax.optimization_barrier((place, flags, halves, latent_init))

    def shifted(offset):
        return [(i, (i + offset) % slabs) for i in range(slabs)]

    tiles_axes = ("sy", "sx")
    tile_devices = lax.axis_size(tiles_axes)
    sent_shape = (slabs - 1, steps_here, rows, cols, channels)
    end_shape, col_shape = ((2, cols, channels), F32), ((2, tile_rows, channels), F32)
    part_rows = CORNERS + 8 * (lanes // LANES)
    moments, table, low_rows, high_rows, first_cols, last_cols, leaving = call(
        functools.partial(start_kernel, group),
        [((tile_devices, part_rows, LANES), F32), ((4, steps_here, lanes), F32)]
        + [end_shape, end_shape, col_shape, col_shape, (sent_shape, BF16)],
        [pltpu.SemaphoreType.DMA((slabs - 1,))],
        10**6,
        smem=[step_index, place, coef_state, coef_drift, coef_noise],
        load=[latent_init, reward_grad, time_table.T, norm_gain],
        hbm=[step_noise],
        grant=WHOLE_BYTES,
    )

    def to_slabs(pieces):
        if slabs == 2:
            return lax.ppermute(pieces, "tm", shifted(1))
        return jnp.stack([lax.ppermute(pieces[i], "tm", shifted(i + 1)) for i in range(slabs - 1)])

    down, up = chain("sy")
    right_way, left_way = chain("sx")
    low = lax.ppermute(low_rows, "sy", down)
    high = lax.ppermute(high_rows, "sy", up)
    left = lax.ppermute(last_cols, "sx", right_way)
    right = lax.ppermute(first_cols, "sx", left_way)
    other_tables = to_slabs(jnp.broadcast_to(table[None], (slabs - 1,) + table.shape))
    other_tables, leaving = lax.optimization_barrier((other_tables, leaving))
    others = to_slabs(leaving)
    parts1 = share(moments, tiles_axes)
    parts1, conv_weight = lax.optimization_barrier((parts1, conv_weight))
    (coefs,) = call(
        table_kernel, [((4, steps, lanes), F32)], [], 10**5, smem=[place], vmem=[table, other_tables],
        grant=SMALL_BYTES,
    )
    packed = ((9 * (lanes - LANES) + 5 * LANES, lanes), BF16)
    weight_out, weight_back = call(
        pack_weight_kernel, [packed, packed], [], 10**7, vmem=[conv_weight.reshape(9, channels, channels)],
    )

    even_shape = (rows + 2, (cols + 2) * steps, lanes)
    odd_shape = (rows + 2, span, lanes)
    field_shape = (rows, span, lanes)
    y_shape = (lanes // LANES, chunk_rows(rows, span) * span, LANES)
    row_shape = (lanes // LANES, span, LANES)
    noise_shape = (steps_here, rows, cols, channels)
    even_out, odd_out, field_out = (even_shape, BF16), (odd_shape, BF16), (field_shape, F32)
    edge_row, edge_col = ((1, span, lanes), F32), ((rows, steps, lanes), F32)
    noise_scratch = [(noise_shape, BF16)]
    even1, odd1, sides, first_row, last_row = call(
        functools.partial(edge_sweep_kernel, group, cells),
        [even_out, odd_out, ((2, 2, tile_rows + 2, lanes), F32), edge_row, edge_row],
        noise_scratch + [(row_shape, F32), (row_shape, F32), pltpu.SemaphoreType.DMA((1,))],
        conv_flops // 4,
        smem=[flags, place],
        vmem=[low, high, left, right, parts1, coefs, latent_init, others, weight_out],
        hbm=[step_noise],
    )
    down_rows, up_rows = row_chain()
    top = lax.ppermute(last_row, ("tm", "sy"), down_rows)
    bottom = lax.ppermute(first_row, ("tm", "sy"), up_rows)
    states, moments, first_col, last_col = call(
        functools.partial(inner_sweep_kernel, group),
        [field_out, ((2, steps, LANES), F32), edge_col, edge_col],
        noise_scratch + [(y_shape, F32), (row_shape, F32), pltpu.SemaphoreType.DMA((1,))],
        conv_flops,
        smem=[place],
        vmem=[first_row, last_row, even1, odd1, coefs, latent_init, others, weight_out],
        hbm=[step_noise],
    )

    def side_cols(args):
        top, bottom, first, last = args
        side_out = ((rows + 2, steps, lanes), F32)
        first, last = call(
            edge_kernel, [side_out, side_out], [], 10**5, vmem=[top, bottom, first, last], grant=SMALL_BYTES
        )
        return lax.ppermute(last, "sx", right_way), lax.ppermute(first, "sx", left_way)

    def act_gradient(first, count):
        def run(reward):
            (out,) = call(
                functools.partial(act_gradient_kernel, first),
                [((count, span, lanes), F32)],
                [((count + 2,) + even_shape[1:], BF16), ((count + 2,) + odd_shape[1:], BF16)],
                conv_flops // 4,
                smem=[place],
                vmem=[reward, low, high, sides, coefs, weight_back],
            )
            return out

        return run

    order = ("sx", "sy", "tm")
    quarter = max(1, rows // 4)
    pieces = [(at, min(quarter, rows - at)) for at in range(0, rows, quarter)]

    def cols_and_first(args):
        return side_cols(args[1:]), act_gradient(*pieces[0])(args[0])

    def d_act_work(piece):
        return lambda done: (act_gradient(*piece), reward_grad)

    moments2, (((left2, right2), d_first), *d_rest) = butterfly(
        moments,
        order,
        join_moments(float(rows * cols * group)),
        [lambda done: (cols_and_first, (reward_grad, top, bottom, first_col, last_col))]
        + [d_act_work(piece) for piece in pieces[1:]],
    )
    even2, odd2, d_norm, sums, norm = call(
        functools.partial(norm_gradient_kernel, group, cells),
        [even_out, odd_out, field_out, ((steps, LANES), F32), ((2, steps, lanes), F32)],
        [],
        40 * rows * span * lanes,
        smem=[flags, place],
        vmem=[moments2, top, bottom, left2, right2, coefs, reward_grad, states, d_first, *d_rest],
    )

    share_rows = channels // slabs
    tiles = 9 * (channels // LANES) + 6

    def late_weight(half):
        def run(reward):
            (out,) = call(
                functools.partial(late_weight_kernel, half),
                [((tiles // 2, channels, LANES), F32)],
                [],
                conv_flops // 2,
                smem=[place],
                vmem=[reward, coefs, even2, odd2],
            )
            return out

        return lambda done: (run, reward_grad)

    def second_sweep(first, count):
        out_shape = (slabs, steps_here, count, cols, channels)

        def run(args):
            base = list(args[1:])
            return call(
                functools.partial(second_sweep_kernel, first),
                [(step_noise.shape, F32, pltpu.HBM), ((slabs - 1,) + out_shape[1:], F32)],
                [(noise_shape, BF16), (y_shape, F32), (row_shape, F32), (out_shape, F32)]
                + [pltpu.SemaphoreType.DMA((1,)), pltpu.SemaphoreType.DMA((1,))],
                conv_flops // 2,
                smem=[place],
                vmem=[coefs, args[0], states, others, weight_out, even2, odd2],
                hbm=[step_noise] + base,
                aliases={9: 0} if base else None,
            )

        return run

    sums, (late_a, late_b, (base, leaving)) = butterfly(
        sums,
        ("tm", "sx", "sy"),
        join_sums,
        [
            late_weight(0),
            late_weight(1),
            lambda done: (second_sweep(0, cut), (latent_init,)),
        ],
    )
    landing = to_slabs(leaving.astype(F16))

    payload = ((slabs, tiles // 2, share_rows, LANES), F32)
    up_shape = ((channels, rows * span), BF16)
    sent, scales, up_t = call(
        functools.partial(sent_weight_kernel, group, cells),
        [payload, ((16, LANES), F32), up_shape],
        [(row_shape, F32), (row_shape, F32), ((rows * span, lanes), BF16)],
        conv_flops // 2,
        smem=[place],
        vmem=[states, norm, sums, coefs, d_norm, reward_grad, even1, odd1, late_a, late_b],
        size=10**6,
    )

    def kept_weight(args):
        (kept,) = call(
            kept_weight_kernel,
            [payload],
            [],
            conv_flops // 2,
            smem=[place],
            vmem=[args[0], coefs, scales, even1, odd1, late_a, late_b],
        )
        return kept

    sent, landing = lax.optimization_barrier((sent, landing))
    arrived, kept = beside(sent, "sx", 1, kept_weight, (up_t,))

    def land(part, trajectory, which):
        (trajectory,) = call(
            functools.partial(land_kernel, (0, cut)[which]),
            [(step_noise.shape, F32, pltpu.HBM)],
            [(part.shape, F32), pltpu.SemaphoreType.DMA((slabs - 1,))],
            10**6,
            smem=[place],
            vmem=[latent_init, part.astype(F32)],
            hbm=[trajectory],
            aliases={3: 0},
        )
        return trajectory

    own, other, trajectory = reduce_weights(
        kept,
        arrived,
        (latent_init, base),
        second_sweep(cut, rows - cut),
        lambda leaving: to_slabs(leaving.astype(F16)),
        land,
        landing,
        halves,
    )
    (grad,) = call(
        unpack_kernel, [((9, share_rows, channels), F32)], [], 10**6, smem=[place], vmem=[own, other, scales],
        grant=SMALL_BYTES,
    )
    return trajectory, grad.transpose(0, 2, 1).reshape(3, 3, channels, share_rows)


def solution(mesh):
    placed = (
        P("sy", "sx", None),
        P("tm", "sy", "sx", None),
        P("tm"),
        P("tm"),
        P("tm"),
        P("tm"),
        P(),
        P(),
        P(),
        P("sy", "sx", None),
    )
    return jax.shard_map(
        shards,
        mesh=mesh,
        in_specs=placed,
        out_specs=(P("tm", "sy", "sx", None), P(None, None, None, "tm")),
        check_vma=False,
    )
```
